32 devices in a mesh: dom: 8 (over z, core), sub: 4 (over y, x).
Axes of the slice: x: 2, y: 2, z: 4, core: 2. Of those that a mesh axis runs over, the one named last changes fastest.
Arguments:
- a_tiles: bfloat16 [128, 10, 128, 128], P(('dom', 'sub')), may hold values from -0.5 to 0.5
- a_cols: int32 [128, 10], P(('dom', 'sub')), may hold values from 0 to 127, as said below
- a_count: int32 [128], P(('dom', 'sub')), may hold values from 3 to 10, as said below
- p_tiles: bfloat16 [128, 128, 256], P(('dom', 'sub')), may hold values from -0.5 to 0.5
- p_cols: int32 [128, 2], P(('dom', 'sub')), may hold values from 0 to 15, as said below
Outputs:
- coarse_band: bfloat16 [2048, 768], P(('dom', 'sub'))
The draws below stay inside these ranges and needn't reach their ends.
Inputs may be any that keep to these rules, and one draw needn't show every extreme that they name: `a_cols`: slot 0 of fine tile f holds f itself. Every column tile of fine tile f lies in its group g(f), or among the last 4 tiles of group g(f) - 1, or among the first 4 tiles of group g(f) + 1. Values in slots at or beyond a_count are such tiles too. `a_count`: each device has at least one fine row tile with all 10 slots live. `p_cols`: both coarse tiles of fine tile f lie in group g(f), between g(f) * 2 and (g(f) + 1) * 2 - 1. With j = f mod 16, the first, h, is within 1 of g(f) * 2 + (j * 2) // 16; the second is g(f) * 2 + (h - g(f) * 2 + 2 // 2) mod 2.
All inputs are finite; a program needn't handle non-finite values.
Results may differ from the reference program's by a relative error of at most 0.0049.
Values may be sent and summed in bfloat16 or wider, within the bound.
No kernel may reach another device: no remote copies, remote signals or barrier semaphores. Data moves between devices by JAX's collectives and lax.ppermute only.
A program may use at most 128 MiB of HBM per device.

```python
import jax
import jax.numpy as jnp
from jax import lax

TILE = 128
ROW_TILES = 4
SLOTS = 10
GROUP_TILES = 16
COARSE_GROUP = 2
GROUPS = 8
FINE_TILES = 128
COARSE_TILES = 16


def draw_a_cols(key, part):
    key = jax.random.fold_in(key, 7)
    key_region, key_own, key_edge = jax.random.split(key, 3)
    tile_ids = jnp.arange(FINE_TILES, dtype=jnp.int32)[:, None]
    group_ids = tile_ids // GROUP_TILES
    region = jax.random.randint(key_region, (FINE_TILES, SLOTS), 0, 10)
    own_tiles = group_ids * GROUP_TILES + jax.random.randint(key_own, (FINE_TILES, SLOTS), 0, GROUP_TILES)
    edge_offset = jax.random.randint(key_edge, (FINE_TILES, SLOTS), 0, ROW_TILES)
    left_tiles = group_ids * GROUP_TILES - ROW_TILES + edge_offset
    right_tiles = (group_ids + 1) * GROUP_TILES + edge_offset
    chosen = jnp.where((region == 0) & (group_ids > 0), left_tiles, jnp.where((region == 1) & (group_ids < GROUPS - 1), right_tiles, own_tiles))
    chosen = chosen.at[:, 0].set(tile_ids[:, 0])
    return chosen.astype(jnp.int32)


def draw_a_count(key, part):
    key = jax.random.fold_in(key, 11)
    key_count, key_full = jax.random.split(key)
    counts = jax.random.randint(key_count, (FINE_TILES,), 3, SLOTS + 1)
    full_rows = jax.random.randint(key_full, (FINE_TILES // ROW_TILES,), 0, ROW_TILES)
    tile_ids = jnp.arange(FINE_TILES, dtype=jnp.int32)
    counts = jnp.where(tile_ids % ROW_TILES == full_rows[tile_ids // ROW_TILES], SLOTS, counts)
    return counts.astype(jnp.int32)


def draw_p_cols(key, part):
    key = jax.random.fold_in(key, 5)
    key_jitter = jax.random.fold_in(key, 0)
    tile_ids = jnp.arange(FINE_TILES, dtype=jnp.int32)
    group_ids = tile_ids // GROUP_TILES
    local_ids = tile_ids % GROUP_TILES
    base_tile = local_ids * COARSE_GROUP // GROUP_TILES
    jitter = jax.random.randint(key_jitter, (FINE_TILES,), -1, 2)
    jitter = jnp.where((local_ids == 0) | (local_ids == GROUP_TILES - 1), 0, jitter)
    home_tile = jnp.clip(base_tile + jitter, 0, COARSE_GROUP - 1)
    other_tile = (home_tile + COARSE_GROUP // 2) % COARSE_GROUP
    both = jnp.stack([group_ids * COARSE_GROUP + home_tile, group_ids * COARSE_GROUP + other_tile], axis=1)
    return both.astype(jnp.int32)


def block_scale(stream_key, extent, cuts, least, largest):
    factor_of = 1.0
    for axis_at, blocks in cuts:
        heights = jax.random.uniform(jax.random.fold_in(jax.random.fold_in(stream_key, 6), axis_at), (blocks,), jnp.float32, least / len(cuts), largest / len(cuts))
        factor_of = factor_of * jnp.repeat(jnp.exp(heights), extent[axis_at] // blocks).reshape((-1,) + (1,) * (len(extent) - 1 - axis_at))
    return factor_of


def gaussian(rng, extent, scale, reach, shards=(), kind=jnp.bfloat16):
    loudness = block_scale(rng, extent, shards, -0.22, 0.18) if shards else 1.0
    entries = jax.random.normal(rng, extent, jnp.float32) * scale * loudness
    return jnp.minimum(jnp.maximum(entries, -reach), reach).astype(kind)


def setup_inputs(seed: int = 0) -> dict:
    key_of = jax.random.split(jax.random.key(seed), 6)
    a_tiles = gaussian(key_of[0], (FINE_TILES, SLOTS, TILE, TILE), TILE ** -0.5, 0.5, ((0, 32),))
    a_cols = draw_a_cols(jax.random.fold_in(key_of[5], 71), 0)
    a_count = draw_a_count(jax.random.fold_in(key_of[5], 71), 0)
    p_tiles = gaussian(key_of[3], (FINE_TILES, TILE, 2 * TILE), TILE ** -0.5, 0.5, ((0, 32),))
    p_cols = draw_p_cols(jax.random.fold_in(key_of[5], 71), 0)
    return dict(a_tiles=a_tiles, a_cols=a_cols, a_count=a_count, p_tiles=p_tiles, p_cols=p_cols)


def reference(a_tiles, a_cols, a_count, p_tiles, p_cols):
    slot_count = a_tiles.shape[1]
    tile_size = a_tiles.shape[2]
    block_ids = jnp.arange(slot_count, dtype=jnp.int32)
    band_blocks = 3 * COARSE_GROUP

    def tile_terms(a_row, column_ids, live_count, p_row, p_home, group_id):
        fetched = p_tiles[column_ids].astype(jnp.float32)
        products = jnp.einsum("kab,kbc->kac", a_row.astype(jnp.float32), fetched, precision=lax.Precision.HIGHEST)
        live_slots = (block_ids < live_count).astype(jnp.float32)
        products = products * live_slots[:, None, None]
        block_index = p_cols[column_ids] - (group_id - 1) * COARSE_GROUP
        pieces = products.reshape(slot_count, tile_size, 2, tile_size).transpose(0, 2, 1, 3)
        q_block = jnp.zeros((band_blocks, tile_size, tile_size), jnp.float32).at[block_index].add(pieces)
        q_block = q_block.transpose(1, 0, 2).reshape(tile_size, band_blocks * tile_size).astype(jnp.bfloat16)
        contribution = jnp.einsum("ab,ac->bc", p_row.astype(jnp.float32), q_block.astype(jnp.float32), precision=lax.Precision.HIGHEST)
        return contribution.reshape(2, tile_size, band_blocks * tile_size)

    def accumulate(coarse, block_start):
        tile_ids = block_start * ROW_TILES + jnp.arange(ROW_TILES, dtype=jnp.int32)
        group_ids = tile_ids // GROUP_TILES
        terms = jax.vmap(tile_terms)(a_tiles[tile_ids], a_cols[tile_ids], a_count[tile_ids], p_tiles[tile_ids], p_cols[tile_ids], group_ids)
        coarse = coarse.at[p_cols[tile_ids]].add(terms)
        return coarse, None

    start_coarse = jnp.zeros((COARSE_TILES, tile_size, band_blocks * tile_size), jnp.float32)
    coarse, _ = lax.scan(accumulate, start_coarse, jnp.arange(FINE_TILES // ROW_TILES, dtype=jnp.int32))
    return coarse.reshape(COARSE_TILES * tile_size, band_blocks * tile_size).astype(jnp.bfloat16)
```

```python
import functools

import jax
import jax.numpy as jnp
from jax import lax
from jax.experimental import pallas as pl
from jax.experimental.pallas import tpu as pltpu
from jax.sharding import PartitionSpec as P

COARSE_ROWS = 64
BF16 = jnp.bfloat16
F32 = jnp.float32


def side_by_side(a_ref, f):
    return jnp.concatenate([a_ref[f, k] for k in range(a_ref.shape[1])], axis=1)


def placed_product(a_row, pool, index):
    stacked = jnp.concatenate([pool[i] for i in index], axis=0)
    return jnp.dot(a_row, stacked, preferred_element_type=F32).astype(BF16)


def own_tiles(rows, zero, half, me, pair_ref, pool):
    tiles = []
    for m in range(half):
        at = [me * rows + f for f in range(rows)]
        if half > 1:
            at = [jnp.where(pair_ref[rows + i] == m, i, zero) for i in at]
        tiles.append([pool[i] for i in at])
    return tiles


def restrict(tiles, q, half):
    outs = []
    for m in range(half):
        lhs = jnp.concatenate(tiles[m], axis=0)
        outs.append(
            lax.dot_general(lhs, q, (((0,), (0,)), ((), ())), preferred_element_type=F32)
        )
    return outs


def assemble_kernel(subs, *refs):
    col_refs, p_refs, (pool, left_ref, right_ref) = refs[:subs], refs[subs : 2 * subs], refs[2 * subs :]
    rows, tile = p_refs[0].shape[:2]
    me = lax.axis_index("sub")
    for k in range(subs):
        base = lax.bitwise_xor(me, k) * rows
        for f in range(rows):
            first = pl.multiple_of(
                jnp.where(col_refs[k][0, f] > col_refs[k][1, f], tile, 0), tile
            )
            for t, start in ((0, first), (1, pl.multiple_of(tile - first, tile))):
                pool[base + f, :, t * tile : (t + 1) * tile] = p_refs[k][f, :, pl.ds(start, tile)]
    pool[subs * rows] = jnp.zeros(pool.shape[1:], pool.dtype)
    left_ref[...] = pool[(subs - 1) * rows : subs * rows]
    right_ref[...] = pool[:rows]


def group_kernel(subs, half, cols_ref, count_ref, pair_ref, a_ref, pool, mid_ref, q):
    rows, slots, tile = a_ref.shape[0], a_ref.shape[1], a_ref.shape[2]
    zero = subs * rows
    me = lax.axis_index("sub")
    first = lax.axis_index("dom") * (subs * rows)
    for f in range(rows):
        a_row = side_by_side(a_ref, f)
        index = [[None] * slots for _ in range(half)]
        for k in range(slots):
            rel = cols_ref[f, k] - first
            inside = (rel >= 0) & (rel < zero) & (k < count_ref[f])
            safe = jnp.where(inside, rel, 0)
            for m in range(half):
                here = inside if half == 1 else inside & (pair_ref[rows + safe] == m)
                index[m][k] = jnp.where(here, safe, zero)
        for m in range(half):
            block = placed_product(a_row, pool, index[m])
            lo, hi = m * tile, (m + half) * tile
            q[f * tile : (f + 1) * tile, lo : lo + tile] = block[:, :tile]
            q[f * tile : (f + 1) * tile, hi : hi + tile] = block[:, tile:]
    for m, out in enumerate(restrict(own_tiles(rows, zero, half, me, pair_ref, pool), q[...], half)):
        mid_ref[m * tile : (m + 1) * tile] = out[:tile]
        mid_ref[(m + half) * tile : (m + half + 1) * tile] = out[tile:]


def halo_kernel(
    subs, half, cols_ref, count_ref, pair_ref, a_ref, mid_ref, pool, left_ref, right_ref, *rest
):
    outs, (edge, q, total) = rest[:subs], rest[subs:]
    rows, slots, tile = a_ref.shape[0], a_ref.shape[1], a_ref.shape[2]
    width = 2 * half * tile
    zero = 2 * rows
    me = lax.axis_index("sub")
    edge[:rows] = left_ref[...]
    edge[rows:zero] = right_ref[...]
    edge[zero] = jnp.zeros(edge.shape[1:], edge.dtype)
    first = lax.axis_index("dom") * (subs * rows)
    index = [[[[None] * slots for _ in range(half)] for _ in range(2)] for _ in range(rows)]
    for f in range(rows):
        for k in range(slots):
            rel = cols_ref[f, k] - first
            live = k < count_ref[f]
            left, right = live & (rel < 0), live & (rel >= subs * rows)
            for side, (inside, at, pair) in enumerate(
                ((left, rel + rows, 0), (right, rel - subs * rows + rows, subs * rows))
            ):
                safe = jnp.where(inside, at, 0)
                for m in range(half):
                    here = inside if half == 1 else inside & (pair_ref[pair + safe] == m)
                    index[f][side][m][k] = jnp.where(here, safe, zero)
    for f in range(rows):
        a_row = side_by_side(a_ref, f)
        for side in range(2):
            for m in range(half):
                block = placed_product(a_row, edge, index[f][side][m])
                lo, hi = side * width + m * tile, side * width + (m + half) * tile
                q[f * tile : (f + 1) * tile, lo : lo + tile] = block[:, :tile]
                q[f * tile : (f + 1) * tile, hi : hi + tile] = block[:, tile:]

    tiles = own_tiles(rows, subs * rows, half, me, pair_ref, pool)
    for m, out in enumerate(restrict(tiles, q[...], half)):
        for row, part in ((m * tile, out[:tile]), ((m + half) * tile, out[tile:])):
            total[row : row + tile, :width] = part[:, :width]
            total[row : row + tile, 2 * width :] = part[:, width:]
    total[:, width : 2 * width] = mid_ref[...]
    for k in range(subs):
        at = pl.multiple_of(lax.bitwise_xor(me, k) * COARSE_ROWS, COARSE_ROWS)
        outs[k][...] = total[pl.ds(at, COARSE_ROWS)].astype(outs[k].dtype)


def local(a_tiles, a_cols, a_count, p_tiles, p_cols):
    rows, slots, tile = a_tiles.shape[:3]
    subs, doms = lax.axis_size("sub"), lax.axis_size("dom")
    coarse_group = subs * COARSE_ROWS // tile
    half = coarse_group // 2
    width = coarse_group * tile
    group_tiles = rows * subs

    smem = pl.BlockSpec(memory_space=pltpu.SMEM)
    vmem = pl.BlockSpec(memory_space=pltpu.VMEM)
    p_bytes = rows * tile * 2 * tile * 2
    a_bytes = a_tiles.size * 2
    spare = 3 << 20

    def exchange(value, k):
        return lax.ppermute(value, "sub", [(s, s ^ k) for s in range(subs)])

    tiles = [p_tiles] + [exchange(p_tiles, k) for k in range(1, subs)]
    cols = [p_cols.T] + [exchange(p_cols.T, k) for k in range(1, subs)]

    pool, to_next, to_previous = pl.pallas_call(
        functools.partial(assemble_kernel, subs),
        out_shape=[
            jax.ShapeDtypeStruct((n, tile, 2 * tile), BF16) for n in (group_tiles + 1, rows, rows)
        ],
        in_specs=[smem] * subs + [vmem] * subs,
        out_specs=[vmem] * 3,
        compiler_params=pltpu.CompilerParams(vmem_limit_bytes=spare),
        cost_estimate=pl.CostEstimate(
            flops=1 << 30, bytes_accessed=2 * subs * p_bytes, transcendentals=0
        ),
        name="assemble",
    )(*cols, *tiles)
    left = lax.ppermute(to_next, "dom", [(d, d + 1) for d in range(doms - 1)])
    right = lax.ppermute(to_previous, "dom", [(d + 1, d) for d in range(doms - 1)])
    if half == 1:
        pair = jnp.zeros((1,), jnp.int32)
    else:
        m_own = jnp.min(p_cols, axis=1) - lax.axis_index("dom") * coarse_group
        m_group = lax.all_gather(m_own, "sub", axis=0, tiled=True)
        m_left = lax.ppermute(
            m_group[group_tiles - rows :], "dom", [(d, d + 1) for d in range(doms - 1)]
        )
        m_right = lax.ppermute(m_group[:rows], "dom", [(d + 1, d) for d in range(doms - 1)])
        pair = jnp.concatenate([m_left, m_group, m_right])

    flops = 2 * rows * slots * tile * tile * 2 * tile * half
    mid = pl.pallas_call(
        functools.partial(group_kernel, subs, half),
        out_shape=jax.ShapeDtypeStruct((width, width), F32),
        in_specs=[smem, smem, smem, vmem, vmem],
        out_specs=vmem,
        scratch_shapes=[pltpu.VMEM((rows * tile, width), BF16)],
        compiler_params=pltpu.CompilerParams(
            vmem_limit_bytes=2 * rows * tile * width + 4 * width * width + spare
        ),
        cost_estimate=pl.CostEstimate(
            flops=flops, bytes_accessed=a_bytes + subs * p_bytes, transcendentals=0
        ),
        name="group_part",
    )(a_cols, a_count, pair, a_tiles, pool)
    parts = pl.pallas_call(
        functools.partial(halo_kernel, subs, half),
        out_shape=[
            jax.ShapeDtypeStruct((COARSE_ROWS, 3 * width), F32 if k == 0 else BF16)
            for k in range(subs)
        ],
        in_specs=[smem, smem, smem, vmem, vmem, vmem, vmem, vmem],
        out_specs=[vmem] * subs,
        scratch_shapes=[
            pltpu.VMEM((2 * rows + 1, tile, 2 * tile), BF16),
            pltpu.VMEM((rows * tile, 2 * width), BF16),
            pltpu.VMEM((width, 3 * width), F32),
        ],
        compiler_params=pltpu.CompilerParams(
            vmem_limit_bytes=3 * p_bytes + 4 * rows * tile * width + 24 * width * width + spare
        ),
        cost_estimate=pl.CostEstimate(
            flops=2 * flops, bytes_accessed=a_bytes + 2 * p_bytes, transcendentals=0
        ),
        name="halo_part",
    )(a_cols, a_count, pair, a_tiles, mid, pool, left, right)
    owned = parts[0]
    for k in range(1, subs):
        owned = owned + exchange(parts[k], k).astype(F32)
    return owned.astype(BF16)


def solution(mesh):
    placed = (
        P(("dom", "sub"), None, None, None),
        P(("dom", "sub"), None),
        P(("dom", "sub")),
        P(("dom", "sub"), None, None),
        P(("dom", "sub"), None),
    )
    return jax.shard_map(
        local, mesh=mesh, in_specs=placed, out_specs=P(("dom", "sub"), None), check_vma=False
    )
```

```python
import functools

import jax
import jax.numpy as jnp
from jax import lax
from jax.experimental import pallas as pl
from jax.experimental.pallas import tpu as pltpu
from jax.sharding import PartitionSpec as P

COARSE_ROWS = 64
BF16 = jnp.bfloat16
F32 = jnp.float32


def side_by_side(a_ref, f):
    return jnp.concatenate([a_ref[f, k] for k in range(a_ref.shape[1])], axis=1)


def placed_product(a_row, pool, index):
    stacked = jnp.concatenate([pool[i] for i in index], axis=0)
    return jnp.dot(a_row, stacked, preferred_element_type=F32).astype(BF16)


def own_tiles(rows, zero, half, me, pair_ref, pool):
    tiles = []
    for m in range(half):
        at = [me * rows + f for f in range(rows)]
        if half > 1:
            at = [jnp.where(pair_ref[rows + i] == m, i, zero) for i in at]
        tiles.append([pool[i] for i in at])
    return tiles


def restrict(tiles, q, half):
    outs = []
    for m in range(half):
        lhs = jnp.concatenate(tiles[m], axis=0)
        outs.append(
            lax.dot_general(lhs, q, (((0,), (0,)), ((), ())), preferred_element_type=F32)
        )
    return outs


def order_kernel(cols_ref, p_ref, own_ref):
    rows, tile = p_ref.shape[:2]
    for f in range(rows):
        first = pl.multiple_of(jnp.where(cols_ref[0, f] > cols_ref[1, f], tile, 0), tile)
        for t, start in ((0, first), (1, pl.multiple_of(tile - first, tile))):
            own_ref[f, :, t * tile : (t + 1) * tile] = p_ref[f, :, pl.ds(start, tile)]


def hand_out_kernel(subs, pool, near_ref, far_ref):
    rows = near_ref.shape[0]
    odd = lax.rem(lax.axis_index("dom"), 2)
    last = (subs - 1) * rows
    near_ref[...] = pool[pl.ds((1 - odd) * last, rows)]
    far_ref[...] = pool[pl.ds(odd * last, rows)]


def edge_kernel(subs, half, cols_ref, count_ref, pair_ref, a_ref, own_ref, out_ref, turned):
    rows, slots, tile = a_ref.shape[:3]
    first = lax.axis_index("dom") * (subs * rows)
    me = lax.axis_index("sub")
    out_ref[...] = jnp.zeros(out_ref.shape, F32)
    for f in range(rows):
        turned[f] = own_ref[f].T
    for f in range(rows):
        for k in range(slots):
            rel = cols_ref[f, k] - first
            live = (k < count_ref[f]) & ((rel < 0) | (rel >= subs * rows))

            @pl.when(live)
            def _():
                at = jnp.where(rel < 0, rel + rows, rel - subs * rows + rows)
                term = jnp.dot(turned[f], a_ref[f, k], preferred_element_type=F32)
                if half == 1:
                    out_ref[at] += term
                else:
                    m = pair_ref[rows + me * rows + f]
                    for start, part in ((m, term[:tile]), (m + half, term[tile:])):
                        out_ref[at, pl.ds(pl.multiple_of(start * tile, tile), tile)] += part


def group_kernel(subs, half, cols_ref, count_ref, pair_ref, a_ref, edge_ref, *rest):
    p_refs, rest = rest[:subs], rest[subs:]
    outs, (pool, q, mid_ref) = rest[:subs], rest[subs:]
    rows, slots, tile = a_ref.shape[0], a_ref.shape[1], a_ref.shape[2]
    zero = subs * rows
    width = 2 * half * tile
    me = lax.axis_index("sub")
    first = lax.axis_index("dom") * (subs * rows)
    for k in range(subs):
        pool[pl.ds(lax.bitwise_xor(me, k) * rows, rows)] = p_refs[k][...]
    pool[zero] = jnp.zeros(pool.shape[1:], pool.dtype)
    for f in range(rows):
        a_row = side_by_side(a_ref, f)
        index = [[None] * slots for _ in range(half)]
        for k in range(slots):
            rel = cols_ref[f, k] - first
            inside = (rel >= 0) & (rel < zero) & (k < count_ref[f])
            safe = jnp.where(inside, rel, 0)
            for m in range(half):
                here = inside if half == 1 else inside & (pair_ref[rows + safe] == m)
                index[m][k] = jnp.where(here, safe, zero)
        for m in range(half):
            block = placed_product(a_row, pool, index[m])
            lo, hi = m * tile, (m + half) * tile
            q[f * tile : (f + 1) * tile, lo : lo + tile] = block[:, :tile]
            q[f * tile : (f + 1) * tile, hi : hi + tile] = block[:, tile:]
    for m, out in enumerate(restrict(own_tiles(rows, zero, half, me, pair_ref, pool), q[...], half)):
        mid_ref[m * tile : (m + 1) * tile] = out[:tile]
        mid_ref[(m + half) * tile : (m + half + 1) * tile] = out[tile:]
    for k in range(subs):
        at = pl.ds(pl.multiple_of(lax.bitwise_xor(me, k) * COARSE_ROWS, COARSE_ROWS), COARSE_ROWS)
        kind = outs[k].dtype
        outs[k][:, :width] = mid_ref[at].astype(kind)
        for c in range(2 * rows):
            outs[k][:, width + c * tile : width + (c + 1) * tile] = edge_ref[c, at].astype(kind)


def sum_kernel(subs, width, *refs):
    part_refs, (mid_ref, edge_ref) = refs[:subs], refs[subs:]
    total = part_refs[0][...]
    for k in range(1, subs):
        total = total + part_refs[k][...].astype(F32)
    mid_ref[...] = total[:, :width].astype(BF16)
    sums = total[:, width:]
    high = sums.astype(BF16)
    edge_ref[:COARSE_ROWS] = high
    edge_ref[COARSE_ROWS:] = (sums - high.astype(F32)).astype(BF16)


def finish_kernel(subs, half, pair_ref, near_ref, far_ref, mid_ref, both_ref, out_ref, edge):
    rows, tile = near_ref.shape[:2]
    width = 2 * half * tile
    odd = lax.rem(lax.axis_index("dom"), 2)
    edge[pl.ds((1 - odd) * rows, rows)] = near_ref[...]
    edge[pl.ds(odd * rows, rows)] = far_ref[...]
    out_ref[:, width : 2 * width] = mid_ref[...]
    both = both_ref[...]
    for side in range(2):
        blocks = [jnp.zeros((COARSE_ROWS, tile), F32) for _ in range(2 * half)]
        tiles = range(side * rows, (side + 1) * rows)
        if half == 1:
            stacked = jnp.concatenate([edge[c] for c in tiles], axis=0)
            lhs = both[:, side * rows * tile : (side + 1) * rows * tile]
            term = jnp.dot(lhs, stacked, preferred_element_type=F32)
            term = term[:COARSE_ROWS] + term[COARSE_ROWS:]
            blocks = [term[:, :tile], term[:, tile:]]
        else:
            for c in tiles:
                lhs = both[:, c * tile : (c + 1) * tile]
                term = jnp.dot(lhs, edge[c], preferred_element_type=F32)
                term = term[:COARSE_ROWS] + term[COARSE_ROWS:]
                m_here = pair_ref[c if side == 0 else subs * rows + c]
                for m in range(half):
                    here = m_here == m
                    blocks[m] = blocks[m] + jnp.where(here, term[:, :tile], 0.0)
                    blocks[m + half] = blocks[m + half] + jnp.where(here, term[:, tile:], 0.0)
        for b in range(2 * half):
            at = 2 * side * width + b * tile
            out_ref[:, at : at + tile] = blocks[b].astype(BF16)


def local(a_tiles, a_cols, a_count, p_tiles, p_cols):
    rows, slots, tile = a_tiles.shape[:3]
    subs, doms = lax.axis_size("sub"), lax.axis_size("dom")
    coarse_group = subs * COARSE_ROWS // tile
    half = coarse_group // 2
    width = coarse_group * tile
    group_tiles = rows * subs

    smem = pl.BlockSpec(memory_space=pltpu.SMEM)
    vmem = pl.BlockSpec(memory_space=pltpu.VMEM)
    p_bytes = rows * tile * 2 * tile * 2
    a_bytes = a_tiles.size * 2
    spare = 3 << 20

    def exchange(value, k):
        return lax.ppermute(value, "sub", [(s, s ^ k) for s in range(subs)])

    own = pl.pallas_call(
        order_kernel,
        out_shape=jax.ShapeDtypeStruct(p_tiles.shape, BF16),
        in_specs=[smem, vmem],
        out_specs=vmem,
        compiler_params=pltpu.CompilerParams(vmem_limit_bytes=spare),
        cost_estimate=pl.CostEstimate(
            flops=1 << 30, bytes_accessed=2 * p_bytes, transcendentals=0
        ),
        name="order_columns",
    )(p_cols.T, p_tiles)

    if half == 1:
        pair = jnp.zeros((1,), jnp.int32)
    else:
        m_own = jnp.min(p_cols, axis=1) - lax.axis_index("dom") * coarse_group
        m_group = lax.all_gather(m_own, "sub", axis=0, tiled=True)
        m_left = lax.ppermute(
            m_group[group_tiles - rows :], "dom", [(d, d + 1) for d in range(doms - 1)]
        )
        m_right = lax.ppermute(m_group[:rows], "dom", [(d + 1, d) for d in range(doms - 1)])
        pair = jnp.concatenate([m_left, m_group, m_right])

    flops = 2 * rows * slots * tile * tile * 2 * tile * half
    edges = pl.pallas_call(
        functools.partial(edge_kernel, subs, half),
        out_shape=jax.ShapeDtypeStruct((2 * rows, width, tile), F32),
        in_specs=[smem, smem, smem, vmem, vmem],
        out_specs=vmem,
        scratch_shapes=[pltpu.VMEM((rows, 2 * tile, tile), BF16)],
        compiler_params=pltpu.CompilerParams(vmem_limit_bytes=8 * rows * tile * width + spare),
        cost_estimate=pl.CostEstimate(
            flops=flops, bytes_accessed=a_bytes + p_bytes, transcendentals=0
        ),
        name="edge_part",
    )(a_cols, a_count, pair, a_tiles, own)

    tiles = [own] + [exchange(own, k) for k in range(1, subs)]
    span = width + 2 * rows * tile
    *parts, pool = pl.pallas_call(
        functools.partial(group_kernel, subs, half),
        out_shape=[
            jax.ShapeDtypeStruct((COARSE_ROWS, span), F32 if k == 0 else BF16)
            for k in range(subs)
        ]
        + [jax.ShapeDtypeStruct((group_tiles + 1, tile, 2 * tile), BF16)],
        in_specs=[smem, smem, smem] + [vmem] * (subs + 2),
        out_specs=[vmem] * (subs + 1),
        scratch_shapes=[
            pltpu.VMEM((rows * tile, width), BF16),
            pltpu.VMEM((width, width), F32),
        ],
        compiler_params=pltpu.CompilerParams(
            vmem_limit_bytes=2 * rows * tile * width + 4 * width * width + spare
        ),
        cost_estimate=pl.CostEstimate(
            flops=flops, bytes_accessed=a_bytes + subs * p_bytes, transcendentals=0
        ),
        name="group_part",
    )(a_cols, a_count, pair, a_tiles, edges, *tiles)
    received = [exchange(parts[k], k) for k in range(1, subs)]
    to_near, to_far = pl.pallas_call(
        functools.partial(hand_out_kernel, subs),
        out_shape=[jax.ShapeDtypeStruct(p_tiles.shape, BF16)] * 2,
        in_specs=[vmem],
        out_specs=[vmem] * 2,
        compiler_params=pltpu.CompilerParams(vmem_limit_bytes=spare),
        name="hand_out",
    )(pool)
    far = lax.ppermute(
        to_far, "dom", [(d, d - 1 + 2 * (d % 2)) for d in range(1, doms - 1)]
    )
    near = lax.ppermute(to_near, "dom", [(d, d ^ 1) for d in range(doms)])
    mid, both = pl.pallas_call(
        functools.partial(sum_kernel, subs, width),
        out_shape=[
            jax.ShapeDtypeStruct((COARSE_ROWS, width), BF16),
            jax.ShapeDtypeStruct((2 * COARSE_ROWS, span - width), BF16),
        ],
        in_specs=[vmem] * subs,
        out_specs=[vmem] * 2,
        compiler_params=pltpu.CompilerParams(vmem_limit_bytes=spare),
        cost_estimate=pl.CostEstimate(
            flops=1 << 31, bytes_accessed=8 * COARSE_ROWS * span, transcendentals=0
        ),
        name="sum_parts",
    )(parts[0], *received)
    return pl.pallas_call(
        functools.partial(finish_kernel, subs, half),
        out_shape=jax.ShapeDtypeStruct((COARSE_ROWS, 3 * width), BF16),
        in_specs=[smem] + [vmem] * 4,
        out_specs=vmem,
        scratch_shapes=[pltpu.VMEM((2 * rows, tile, 2 * tile), BF16)],
        compiler_params=pltpu.CompilerParams(vmem_limit_bytes=2 * p_bytes + spare),
        cost_estimate=pl.CostEstimate(
            flops=1 << 28, bytes_accessed=4 * p_bytes, transcendentals=0
        ),
        name="finish",
    )(pair, near, far, mid, both)


def solution(mesh):
    placed = (
        P(("dom", "sub"), None, None, None),
        P(("dom", "sub"), None),
        P(("dom", "sub")),
        P(("dom", "sub"), None, None),
        P(("dom", "sub"), None),
    )
    return jax.shard_map(
        local, mesh=mesh, in_specs=placed, out_specs=P(("dom", "sub"), None), check_vma=False
    )
```

```python
import functools

import jax
import jax.numpy as jnp
from jax import lax
from jax.experimental import pallas as pl
from jax.experimental.pallas import tpu as pltpu
from jax.sharding import PartitionSpec as P

COARSE_ROWS = 64
BF16 = jnp.bfloat16
F32 = jnp.float32


def side_by_side(a_ref, f):
    return jnp.concatenate([a_ref[f, k] for k in range(a_ref.shape[1])], axis=1)


def placed_product(a_row, pool, index):
    stacked = jnp.concatenate([pool[i] for i in index], axis=0)
    return jnp.dot(a_row, stacked, preferred_element_type=F32).astype(BF16)


def own_tiles(rows, zero, half, me, pair_ref, pool):
    tiles = []
    for m in range(half):
        at = [me * rows + f for f in range(rows)]
        if half > 1:
            at = [jnp.where(pair_ref[rows + i] == m, i, zero) for i in at]
        tiles.append([pool[i] for i in at])
    return tiles


def restrict(tiles, q, half):
    outs = []
    for m in range(half):
        lhs = jnp.concatenate(tiles[m], axis=0)
        outs.append(
            lax.dot_general(lhs, q, (((0,), (0,)), ((), ())), preferred_element_type=F32)
        )
    return outs


def order_kernel(cols_ref, p_ref, *outs):
    rows, tile = p_ref.shape[:2]
    piece = rows // 2
    for f in range(rows):
        first = pl.multiple_of(jnp.where(cols_ref[0, f] > cols_ref[1, f], tile, 0), tile)
        for t, start in ((0, first), (1, pl.multiple_of(tile - first, tile))):
            outs[f // piece][f % piece, :, t * tile : (t + 1) * tile] = p_ref[f, :, pl.ds(start, tile)]


def hand_out_kernel(subs, pool, near_ref, far_ref):
    rows = near_ref.shape[0]
    odd = lax.rem(lax.axis_index("dom"), 2)
    last = (subs - 1) * rows
    near_ref[...] = pool[pl.ds((1 - odd) * last, rows)]
    far_ref[...] = pool[pl.ds(odd * last, rows)]


def edge_kernel(subs, half, cols_ref, count_ref, pair_ref, a_ref, own_0, own_1, out_ref, turned):
    rows, slots, tile = a_ref.shape[:3]
    first = lax.axis_index("dom") * (subs * rows)
    me = lax.axis_index("sub")
    out_ref[...] = jnp.zeros(out_ref.shape, F32)
    for f in range(rows):
        turned[f] = (own_0, own_1)[f // (rows // 2)][f % (rows // 2)].T
    for f in range(rows):
        for k in range(slots):
            rel = cols_ref[f, k] - first
            live = (k < count_ref[f]) & ((rel < 0) | (rel >= subs * rows))

            @pl.when(live)
            def _():
                at = jnp.where(rel < 0, rel + rows, rel - subs * rows + rows)
                term = jnp.dot(turned[f], a_ref[f, k], preferred_element_type=F32)
                if half == 1:
                    out_ref[at] += term
                else:
                    m = pair_ref[rows + me * rows + f]
                    for start, part in ((m, term[:tile]), (m + half, term[tile:])):
                        out_ref[at, pl.ds(pl.multiple_of(start * tile, tile), tile)] += part


def group_kernel(subs, half, cols_ref, count_ref, pair_ref, a_ref, edge_ref, *rest):
    p_refs, rest = rest[: 2 * subs], rest[2 * subs :]
    outs, (pool, q, mid_ref) = rest[:subs], rest[subs:]
    rows, slots, tile = a_ref.shape[0], a_ref.shape[1], a_ref.shape[2]
    zero = subs * rows
    width = 2 * half * tile
    me = lax.axis_index("sub")
    first = lax.axis_index("dom") * (subs * rows)
    piece = rows // 2
    for k in range(subs):
        for i in range(2):
            pool[pl.ds(lax.bitwise_xor(me, k) * rows + i * piece, piece)] = p_refs[2 * k + i][...]
    pool[zero] = jnp.zeros(pool.shape[1:], pool.dtype)
    for f in range(rows):
        a_row = side_by_side(a_ref, f)
        index = [[None] * slots for _ in range(half)]
        for k in range(slots):
            rel = cols_ref[f, k] - first
            inside = (rel >= 0) & (rel < zero) & (k < count_ref[f])
            safe = jnp.where(inside, rel, 0)
            for m in range(half):
                here = inside if half == 1 else inside & (pair_ref[rows + safe] == m)
                index[m][k] = jnp.where(here, safe, zero)
        for m in range(half):
            block = placed_product(a_row, pool, index[m])
            lo, hi = m * tile, (m + half) * tile
            q[f * tile : (f + 1) * tile, lo : lo + tile] = block[:, :tile]
            q[f * tile : (f + 1) * tile, hi : hi + tile] = block[:, tile:]
    for m, out in enumerate(restrict(own_tiles(rows, zero, half, me, pair_ref, pool), q[...], half)):
        mid_ref[m * tile : (m + 1) * tile] = out[:tile]
        mid_ref[(m + half) * tile : (m + half + 1) * tile] = out[tile:]
    for k in range(subs):
        at = pl.ds(pl.multiple_of(lax.bitwise_xor(me, k) * COARSE_ROWS, COARSE_ROWS), COARSE_ROWS)
        kind = outs[k].dtype
        outs[k][:, :width] = mid_ref[at].astype(kind)
        for c in range(2 * rows):
            outs[k][:, width + c * tile : width + (c + 1) * tile] = edge_ref[c, at].astype(kind)


def sum_kernel(subs, width, *refs):
    part_refs, (mid_ref, edge_ref) = refs[:subs], refs[subs:]
    total = part_refs[0][...]
    for k in range(1, subs):
        total = total + part_refs[k][...].astype(F32)
    mid_ref[...] = total[:, :width].astype(BF16)
    sums = total[:, width:]
    high = sums.astype(BF16)
    edge_ref[:COARSE_ROWS] = high
    edge_ref[COARSE_ROWS:] = (sums - high.astype(F32)).astype(BF16)


def finish_kernel(subs, half, pair_ref, far_ref, near_ref, mid_ref, both_ref, out_ref, edge):
    rows, tile = near_ref.shape[:2]
    width = 2 * half * tile
    odd = lax.rem(lax.axis_index("dom"), 2)
    edge[pl.ds((1 - odd) * rows, rows)] = near_ref[...]
    edge[pl.ds(odd * rows, rows)] = far_ref[...]
    out_ref[:, width : 2 * width] = mid_ref[...]
    both = both_ref[...]
    for side in range(2):
        blocks = [jnp.zeros((COARSE_ROWS, tile), F32) for _ in range(2 * half)]
        tiles = range(side * rows, (side + 1) * rows)
        if half == 1:
            stacked = jnp.concatenate([edge[c] for c in tiles], axis=0)
            lhs = both[:, side * rows * tile : (side + 1) * rows * tile]
            term = jnp.dot(lhs, stacked, preferred_element_type=F32)
            term = term[:COARSE_ROWS] + term[COARSE_ROWS:]
            blocks = [term[:, :tile], term[:, tile:]]
        else:
            for c in tiles:
                lhs = both[:, c * tile : (c + 1) * tile]
                term = jnp.dot(lhs, edge[c], preferred_element_type=F32)
                term = term[:COARSE_ROWS] + term[COARSE_ROWS:]
                m_here = pair_ref[c if side == 0 else subs * rows + c]
                for m in range(half):
                    here = m_here == m
                    blocks[m] = blocks[m] + jnp.where(here, term[:, :tile], 0.0)
                    blocks[m + half] = blocks[m + half] + jnp.where(here, term[:, tile:], 0.0)
        for b in range(2 * half):
            at = 2 * side * width + b * tile
            out_ref[:, at : at + tile] = blocks[b].astype(BF16)


def local(a_tiles, a_cols, a_count, p_tiles, p_cols):
    rows, slots, tile = a_tiles.shape[:3]
    subs, doms = lax.axis_size("sub"), lax.axis_size("dom")
    coarse_group = subs * COARSE_ROWS // tile
    half = coarse_group // 2
    width = coarse_group * tile
    group_tiles = rows * subs

    smem = pl.BlockSpec(memory_space=pltpu.SMEM)
    vmem = pl.BlockSpec(memory_space=pltpu.VMEM)
    p_bytes = rows * tile * 2 * tile * 2
    a_bytes = a_tiles.size * 2
    spare = 3 << 20

    def exchange(value, k):
        return lax.ppermute(value, "sub", [(s, s ^ k) for s in range(subs)])

    own = pl.pallas_call(
        order_kernel,
        out_shape=[jax.ShapeDtypeStruct((rows // 2, tile, 2 * tile), BF16)] * 2,
        in_specs=[smem, vmem],
        out_specs=[vmem] * 2,
        compiler_params=pltpu.CompilerParams(vmem_limit_bytes=spare),
        cost_estimate=pl.CostEstimate(
            flops=1 << 30, bytes_accessed=2 * p_bytes, transcendentals=0
        ),
        name="order_columns",
    )(p_cols.T, p_tiles)

    if half == 1:
        pair = jnp.zeros((1,), jnp.int32)
    else:
        m_own = jnp.min(p_cols, axis=1) - lax.axis_index("dom") * coarse_group
        m_group = lax.all_gather(m_own, "sub", axis=0, tiled=True)
        m_left = lax.ppermute(
            m_group[group_tiles - rows :], "dom", [(d, d + 1) for d in range(doms - 1)]
        )
        m_right = lax.ppermute(m_group[:rows], "dom", [(d + 1, d) for d in range(doms - 1)])
        pair = jnp.concatenate([m_left, m_group, m_right])

    flops = 2 * rows * slots * tile * tile * 2 * tile * half
    edges = pl.pallas_call(
        functools.partial(edge_kernel, subs, half),
        out_shape=jax.ShapeDtypeStruct((2 * rows, width, tile), F32),
        in_specs=[smem, smem, smem, vmem, vmem, vmem],
        out_specs=vmem,
        scratch_shapes=[pltpu.VMEM((rows, 2 * tile, tile), BF16)],
        compiler_params=pltpu.CompilerParams(vmem_limit_bytes=8 * rows * tile * width + spare),
        cost_estimate=pl.CostEstimate(
            flops=flops, bytes_accessed=a_bytes + p_bytes, transcendentals=0
        ),
        name="edge_part",
    )(a_cols, a_count, pair, a_tiles, *own)

    tiles = [list(own)] + [[None, None] for _ in range(subs - 1)]
    for k in range(1, subs):
        low, high = k & -k, 1 << (k.bit_length() - 1)
        tiles[k][0] = exchange(tiles[k ^ low][0], low)
        tiles[k][1] = exchange(tiles[k ^ high][1], high)
    span = width + 2 * rows * tile
    *parts, pool = pl.pallas_call(
        functools.partial(group_kernel, subs, half),
        out_shape=[
            jax.ShapeDtypeStruct((COARSE_ROWS, span), F32 if k == 0 else BF16)
            for k in range(subs)
        ]
        + [jax.ShapeDtypeStruct((group_tiles + 1, tile, 2 * tile), BF16)],
        in_specs=[smem, smem, smem] + [vmem] * (2 * subs + 2),
        out_specs=[vmem] * (subs + 1),
        scratch_shapes=[
            pltpu.VMEM((rows * tile, width), BF16),
            pltpu.VMEM((width, width), F32),
        ],
        compiler_params=pltpu.CompilerParams(
            vmem_limit_bytes=2 * rows * tile * width + 4 * width * width + spare
        ),
        cost_estimate=pl.CostEstimate(
            flops=flops, bytes_accessed=a_bytes + subs * p_bytes, transcendentals=0
        ),
        name="group_part",
    )(a_cols, a_count, pair, a_tiles, edges, *sum(tiles, []))
    received = [exchange(parts[k], k) for k in range(1, subs)]
    to_near, to_far = pl.pallas_call(
        functools.partial(hand_out_kernel, subs),
        out_shape=[jax.ShapeDtypeStruct(p_tiles.shape, BF16)] * 2,
        in_specs=[vmem],
        out_specs=[vmem] * 2,
        compiler_params=pltpu.CompilerParams(vmem_limit_bytes=spare),
        name="hand_out",
    )(pool)
    far = lax.ppermute(
        to_far, "dom", [(d, d - 1 + 2 * (d % 2)) for d in range(1, doms - 1)]
    )
    near = lax.ppermute(to_near, "dom", [(d, d ^ 1) for d in range(doms)])
    mid, both = pl.pallas_call(
        functools.partial(sum_kernel, subs, width),
        out_shape=[
            jax.ShapeDtypeStruct((COARSE_ROWS, width), BF16),
            jax.ShapeDtypeStruct((2 * COARSE_ROWS, span - width), BF16),
        ],
        in_specs=[vmem] * subs,
        out_specs=[vmem] * 2,
        compiler_params=pltpu.CompilerParams(vmem_limit_bytes=spare),
        cost_estimate=pl.CostEstimate(
            flops=1 << 31, bytes_accessed=8 * COARSE_ROWS * span, transcendentals=0
        ),
        name="sum_parts",
    )(parts[0], *received)
    return pl.pallas_call(
        functools.partial(finish_kernel, subs, half),
        out_shape=jax.ShapeDtypeStruct((COARSE_ROWS, 3 * width), BF16),
        in_specs=[smem] + [vmem] * 4,
        out_specs=vmem,
        scratch_shapes=[pltpu.VMEM((2 * rows, tile, 2 * tile), BF16)],
        compiler_params=pltpu.CompilerParams(vmem_limit_bytes=2 * p_bytes + spare),
        cost_estimate=pl.CostEstimate(
            flops=1 << 28, bytes_accessed=4 * p_bytes, transcendentals=0
        ),
        name="finish",
    )(pair, far, near, mid, both)


def solution(mesh):
    placed = (
        P(("dom", "sub"), None, None, None),
        P(("dom", "sub"), None),
        P(("dom", "sub")),
        P(("dom", "sub"), None, None),
        P(("dom", "sub"), None),
    )
    return jax.shard_map(
        local, mesh=mesh, in_specs=placed, out_specs=P(("dom", "sub"), None), check_vma=False
    )
```

```python
import functools

import jax
import jax.numpy as jnp
from jax import lax
from jax.experimental import pallas as pl
from jax.experimental.pallas import tpu as pltpu
from jax.sharding import PartitionSpec as P

COARSE_ROWS = 64
BF16 = jnp.bfloat16
F32 = jnp.float32


def side_by_side(a_ref, f):
    return jnp.concatenate([a_ref[f, k] for k in range(a_ref.shape[1])], axis=1)


def placed_product(a_row, pool, index):
    stacked = jnp.concatenate([pool[i] for i in index], axis=0)
    return jnp.dot(a_row, stacked, preferred_element_type=F32).astype(BF16)


def own_tiles(rows, zero, half, me, pair_ref, pool):
    tiles = []
    for m in range(half):
        at = [me * rows + f for f in range(rows)]
        if half > 1:
            at = [jnp.where(pair_ref[rows + i] == m, i, zero) for i in at]
        tiles.append([pool[i] for i in at])
    return tiles


def restrict(tiles, q, half):
    outs = []
    for m in range(half):
        lhs = jnp.concatenate(tiles[m], axis=0)
        outs.append(
            lax.dot_general(lhs, q, (((0,), (0,)), ((), ())), preferred_element_type=F32)
        )
    return outs


def order_kernel(cols_hbm, p_hbm, *rest):
    outs, (cols_ref, p_ref, sems) = rest[:2], rest[2:]
    rows, tile = p_ref.shape[:2]
    piece = rows // 2
    lists = pltpu.make_async_copy(cols_hbm, cols_ref, sems.at[rows])
    lists.start()
    loads = [pltpu.make_async_copy(p_hbm.at[f], p_ref.at[f], sems.at[f]) for f in range(rows)]
    for load in loads:
        load.start()
    lists.wait()
    for f in range(rows):
        loads[f].wait()
        first = pl.multiple_of(jnp.where(cols_ref[0, f] > cols_ref[1, f], tile, 0), tile)
        for t, start in ((0, first), (1, pl.multiple_of(tile - first, tile))):
            outs[f // piece][f % piece, :, t * tile : (t + 1) * tile] = p_ref[f, :, pl.ds(start, tile)]


def hand_out_kernel(subs, pool, near_ref, far_ref):
    rows = near_ref.shape[0]
    odd = lax.rem(lax.axis_index("dom"), 2)
    last = (subs - 1) * rows
    near_ref[...] = pool[pl.ds((1 - odd) * last, rows)]
    far_ref[...] = pool[pl.ds(odd * last, rows)]


def edge_kernel(subs, half, cols_ref, count_ref, pair_ref, a_hbm, own_0, own_1, *rest):
    out_ref, a_ref, turned, sems = rest
    rows, slots, tile = a_ref.shape[:3]
    first = lax.axis_index("dom") * (subs * rows)
    me = lax.axis_index("sub")
    loads = [pltpu.make_async_copy(a_hbm.at[f], a_ref.at[f], sems.at[f]) for f in range(rows)]
    for load in loads:
        load.start()
    out_ref[...] = jnp.zeros(out_ref.shape, F32)
    for f in range(rows):
        turned[f] = (own_0, own_1)[f // (rows // 2)][f % (rows // 2)].T
    for f in range(rows):
        loads[f].wait()
        for k in range(slots):
            rel = cols_ref[f, k] - first
            live = (k < count_ref[f]) & ((rel < 0) | (rel >= subs * rows))

            @pl.when(live)
            def _():
                at = jnp.where(rel < 0, rel + rows, rel - subs * rows + rows)
                term = jnp.dot(turned[f], a_ref[f, k], preferred_element_type=F32)
                if half == 1:
                    out_ref[at] += term
                else:
                    m = pair_ref[rows + me * rows + f]
                    for start, part in ((m, term[:tile]), (m + half, term[tile:])):
                        out_ref[at, pl.ds(pl.multiple_of(start * tile, tile), tile)] += part


def group_kernel(subs, half, cols_ref, count_ref, pair_ref, a_ref, edge_ref, *rest):
    p_refs, rest = rest[: 2 * subs], rest[2 * subs :]
    outs, (pool, q, mid_ref) = rest[:subs], rest[subs:]
    rows, slots, tile = a_ref.shape[0], a_ref.shape[1], a_ref.shape[2]
    zero = subs * rows
    width = 2 * half * tile
    me = lax.axis_index("sub")
    first = lax.axis_index("dom") * (subs * rows)
    piece = rows // 2
    for k in range(subs):
        for i in range(2):
            pool[pl.ds(lax.bitwise_xor(me, k) * rows + i * piece, piece)] = p_refs[2 * k + i][...]
    pool[zero] = jnp.zeros(pool.shape[1:], pool.dtype)
    for f in range(rows):
        a_row = side_by_side(a_ref, f)
        index = [[None] * slots for _ in range(half)]
        for k in range(slots):
            rel = cols_ref[f, k] - first
            inside = (rel >= 0) & (rel < zero) & (k < count_ref[f])
            safe = jnp.where(inside, rel, 0)
            for m in range(half):
                here = inside if half == 1 else inside & (pair_ref[rows + safe] == m)
                index[m][k] = jnp.where(here, safe, zero)
        for m in range(half):
            block = placed_product(a_row, pool, index[m])
            lo, hi = m * tile, (m + half) * tile
            q[f * tile : (f + 1) * tile, lo : lo + tile] = block[:, :tile]
            q[f * tile : (f + 1) * tile, hi : hi + tile] = block[:, tile:]
    for m, out in enumerate(restrict(own_tiles(rows, zero, half, me, pair_ref, pool), q[...], half)):
        mid_ref[m * tile : (m + 1) * tile] = out[:tile]
        mid_ref[(m + half) * tile : (m + half + 1) * tile] = out[tile:]
    for k in range(subs):
        at = pl.ds(pl.multiple_of(lax.bitwise_xor(me, k) * COARSE_ROWS, COARSE_ROWS), COARSE_ROWS)
        kind = outs[k].dtype
        outs[k][:, :width] = mid_ref[at].astype(kind)
        for c in range(2 * rows):
            outs[k][:, width + c * tile : width + (c + 1) * tile] = edge_ref[c, at].astype(kind)


def sum_kernel(subs, width, *refs):
    part_refs, (mid_ref, edge_ref) = refs[:subs], refs[subs:]
    total = part_refs[0][...]
    for k in range(1, subs):
        total = total + part_refs[k][...].astype(F32)
    mid_ref[...] = total[:, :width].astype(BF16)
    sums = total[:, width:]
    high = sums.astype(BF16)
    edge_ref[:COARSE_ROWS] = high
    edge_ref[COARSE_ROWS:] = (sums - high.astype(F32)).astype(BF16)


def finish_kernel(subs, half, pair_ref, far_ref, near_ref, mid_ref, both_ref, out_ref, edge):
    rows, tile = near_ref.shape[:2]
    width = 2 * half * tile
    odd = lax.rem(lax.axis_index("dom"), 2)
    edge[pl.ds((1 - odd) * rows, rows)] = near_ref[...]
    edge[pl.ds(odd * rows, rows)] = far_ref[...]
    out_ref[:, width : 2 * width] = mid_ref[...]
    both = both_ref[...]
    for side in range(2):
        blocks = [jnp.zeros((COARSE_ROWS, tile), F32) for _ in range(2 * half)]
        tiles = range(side * rows, (side + 1) * rows)
        if half == 1:
            stacked = jnp.concatenate([edge[c] for c in tiles], axis=0)
            lhs = both[:, side * rows * tile : (side + 1) * rows * tile]
            term = jnp.dot(lhs, stacked, preferred_element_type=F32)
            term = term[:COARSE_ROWS] + term[COARSE_ROWS:]
            blocks = [term[:, :tile], term[:, tile:]]
        else:
            for c in tiles:
                lhs = both[:, c * tile : (c + 1) * tile]
                term = jnp.dot(lhs, edge[c], preferred_element_type=F32)
                term = term[:COARSE_ROWS] + term[COARSE_ROWS:]
                m_here = pair_ref[c if side == 0 else subs * rows + c]
                for m in range(half):
                    here = m_here == m
                    blocks[m] = blocks[m] + jnp.where(here, term[:, :tile], 0.0)
                    blocks[m + half] = blocks[m + half] + jnp.where(here, term[:, tile:], 0.0)
        for b in range(2 * half):
            at = 2 * side * width + b * tile
            out_ref[:, at : at + tile] = blocks[b].astype(BF16)


def local(a_tiles, a_cols, a_count, p_tiles, p_cols):
    rows, slots, tile = a_tiles.shape[:3]
    subs, doms = lax.axis_size("sub"), lax.axis_size("dom")
    coarse_group = subs * COARSE_ROWS // tile
    half = coarse_group // 2
    width = coarse_group * tile
    group_tiles = rows * subs

    smem = pl.BlockSpec(memory_space=pltpu.SMEM)
    vmem = pl.BlockSpec(memory_space=pltpu.VMEM)
    p_bytes = rows * tile * 2 * tile * 2
    a_bytes = a_tiles.size * 2
    spare = 3 << 20

    def exchange(value, k):
        return lax.ppermute(value, "sub", [(s, s ^ k) for s in range(subs)])

    own = pl.pallas_call(
        order_kernel,
        out_shape=[jax.ShapeDtypeStruct((rows // 2, tile, 2 * tile), BF16)] * 2,
        in_specs=[pl.BlockSpec(memory_space=pltpu.HBM)] * 2,
        out_specs=[vmem] * 2,
        scratch_shapes=[
            pltpu.SMEM((2, rows), jnp.int32),
            pltpu.VMEM(p_tiles.shape, BF16),
            pltpu.SemaphoreType.DMA((rows + 1,)),
        ],
        compiler_params=pltpu.CompilerParams(vmem_limit_bytes=spare),
        cost_estimate=pl.CostEstimate(
            flops=1 << 30, bytes_accessed=2 * p_bytes, transcendentals=0
        ),
        name="order_columns",
    )(
        pltpu.with_memory_space_constraint(p_cols.T, pltpu.HBM),
        pltpu.with_memory_space_constraint(p_tiles, pltpu.HBM),
    )

    if half == 1:
        pair = jnp.zeros((1,), jnp.int32)
    else:
        m_own = jnp.min(p_cols, axis=1) - lax.axis_index("dom") * coarse_group
        m_group = lax.all_gather(m_own, "sub", axis=0, tiled=True)
        m_left = lax.ppermute(
            m_group[group_tiles - rows :], "dom", [(d, d + 1) for d in range(doms - 1)]
        )
        m_right = lax.ppermute(m_group[:rows], "dom", [(d + 1, d) for d in range(doms - 1)])
        pair = jnp.concatenate([m_left, m_group, m_right])

    flops = 2 * rows * slots * tile * tile * 2 * tile * half
    edges, a_held = pl.pallas_call(
        functools.partial(edge_kernel, subs, half),
        out_shape=[
            jax.ShapeDtypeStruct((2 * rows, width, tile), F32),
            jax.ShapeDtypeStruct(a_tiles.shape, BF16),
        ],
        in_specs=[smem, smem, smem, pl.BlockSpec(memory_space=pltpu.HBM), vmem, vmem],
        out_specs=[vmem] * 2,
        scratch_shapes=[
            pltpu.VMEM((rows, 2 * tile, tile), BF16),
            pltpu.SemaphoreType.DMA((rows,)),
        ],
        compiler_params=pltpu.CompilerParams(vmem_limit_bytes=8 * rows * tile * width + spare),
        cost_estimate=pl.CostEstimate(
            flops=flops, bytes_accessed=a_bytes + p_bytes, transcendentals=0
        ),
        name="edge_part",
    )(a_cols, a_count, pair, pltpu.with_memory_space_constraint(a_tiles, pltpu.HBM), *own)

    tiles = [list(own)] + [[None, None] for _ in range(subs - 1)]
    for k in range(1, subs):
        low, high = k & -k, 1 << (k.bit_length() - 1)
        tiles[k][0] = exchange(tiles[k ^ low][0], low)
        tiles[k][1] = exchange(tiles[k ^ high][1], high)
    span = width + 2 * rows * tile
    *parts, pool = pl.pallas_call(
        functools.partial(group_kernel, subs, half),
        out_shape=[
            jax.ShapeDtypeStruct((COARSE_ROWS, span), F32 if k == 0 else BF16)
            for k in range(subs)
        ]
        + [jax.ShapeDtypeStruct((group_tiles + 1, tile, 2 * tile), BF16)],
        in_specs=[smem, smem, smem] + [vmem] * (2 * subs + 2),
        out_specs=[vmem] * (subs + 1),
        scratch_shapes=[
            pltpu.VMEM((rows * tile, width), BF16),
            pltpu.VMEM((width, width), F32),
        ],
        compiler_params=pltpu.CompilerParams(
            vmem_limit_bytes=2 * rows * tile * width + 4 * width * width + spare
        ),
        cost_estimate=pl.CostEstimate(
            flops=flops, bytes_accessed=a_bytes + subs * p_bytes, transcendentals=0
        ),
        name="group_part",
    )(a_cols, a_count, pair, a_held, edges, *sum(tiles, []))
    received = [exchange(parts[k], k) for k in range(1, subs)]
    to_near, to_far = pl.pallas_call(
        functools.partial(hand_out_kernel, subs),
        out_shape=[jax.ShapeDtypeStruct(p_tiles.shape, BF16)] * 2,
        in_specs=[vmem],
        out_specs=[vmem] * 2,
        compiler_params=pltpu.CompilerParams(vmem_limit_bytes=spare),
        name="hand_out",
    )(pool)
    far = lax.ppermute(
        to_far, "dom", [(d, d - 1 + 2 * (d % 2)) for d in range(1, doms - 1)]
    )
    near = lax.ppermute(to_near, "dom", [(d, d ^ 1) for d in range(doms)])
    mid, both = pl.pallas_call(
        functools.partial(sum_kernel, subs, width),
        out_shape=[
            jax.ShapeDtypeStruct((COARSE_ROWS, width), BF16),
            jax.ShapeDtypeStruct((2 * COARSE_ROWS, span - width), BF16),
        ],
        in_specs=[vmem] * subs,
        out_specs=[vmem] * 2,
        compiler_params=pltpu.CompilerParams(vmem_limit_bytes=spare),
        cost_estimate=pl.CostEstimate(
            flops=1 << 31, bytes_accessed=8 * COARSE_ROWS * span, transcendentals=0
        ),
        name="sum_parts",
    )(parts[0], *received)
    return pl.pallas_call(
        functools.partial(finish_kernel, subs, half),
        out_shape=jax.ShapeDtypeStruct((COARSE_ROWS, 3 * width), BF16),
        in_specs=[smem] + [vmem] * 4,
        out_specs=vmem,
        scratch_shapes=[pltpu.VMEM((2 * rows, tile, 2 * tile), BF16)],
        compiler_params=pltpu.CompilerParams(vmem_limit_bytes=2 * p_bytes + spare),
        cost_estimate=pl.CostEstimate(
            flops=1 << 28, bytes_accessed=4 * p_bytes, transcendentals=0
        ),
        name="finish",
    )(pair, far, near, mid, both)


def solution(mesh):
    placed = (
        P(("dom", "sub"), None, None, None),
        P(("dom", "sub"), None),
        P(("dom", "sub")),
        P(("dom", "sub"), None, None),
        P(("dom", "sub"), None),
    )
    return jax.shard_map(
        local, mesh=mesh, in_specs=placed, out_specs=P(("dom", "sub"), None), check_vma=False
    )
```

```python
import functools

import jax
import jax.numpy as jnp
from jax import lax
from jax.experimental import pallas as pl
from jax.experimental.pallas import tpu as pltpu
from jax.sharding import PartitionSpec as P

COARSE_ROWS = 64
BF16 = jnp.bfloat16
F32 = jnp.float32


def side_by_side(a_ref, f):
    return jnp.concatenate([a_ref[f, k] for k in range(a_ref.shape[1])], axis=1)


def placed_product(a_row, pool, index):
    stacked = jnp.concatenate([pool[i] for i in index], axis=0)
    return jnp.dot(a_row, stacked, preferred_element_type=F32).astype(BF16)


def own_tiles(rows, zero, half, me, pair_ref, pool):
    tiles = []
    for m in range(half):
        at = [me * rows + f for f in range(rows)]
        if half > 1:
            at = [jnp.where(pair_ref[rows + i] == m, i, zero) for i in at]
        tiles.append([pool[i] for i in at])
    return tiles


def restrict(tiles, q, half):
    outs = []
    for m in range(half):
        lhs = jnp.concatenate(tiles[m], axis=0)
        outs.append(
            lax.dot_general(lhs, q, (((0,), (0,)), ((), ())), preferred_element_type=F32)
        )
    return outs


def order_kernel(cols_hbm, p_hbm, *rest):
    outs, (cols_ref, p_ref, sems) = rest[:2], rest[2:]
    rows, tile = p_ref.shape[:2]
    piece = rows // 2
    lists = pltpu.make_async_copy(cols_hbm, cols_ref, sems.at[rows])
    lists.start()
    loads = [pltpu.make_async_copy(p_hbm.at[f], p_ref.at[f], sems.at[f]) for f in range(rows)]
    for load in loads:
        load.start()
    lists.wait()
    for f in range(rows):
        loads[f].wait()
        first = pl.multiple_of(jnp.where(cols_ref[0, f] > cols_ref[1, f], tile, 0), tile)
        for t, start in ((0, first), (1, pl.multiple_of(tile - first, tile))):
            outs[f // piece][f % piece, :, t * tile : (t + 1) * tile] = p_ref[f, :, pl.ds(start, tile)]


def assemble_kernel(subs, *refs):
    p_refs, (pool, near_ref, far_ref) = refs[: 2 * subs], refs[2 * subs :]
    piece = p_refs[0].shape[0]
    rows = 2 * piece
    me, odd = lax.axis_index("sub"), lax.rem(lax.axis_index("dom"), 2)
    for k in range(subs):
        for i in range(2):
            pool[pl.ds(lax.bitwise_xor(me, k) * rows + i * piece, piece)] = p_refs[2 * k + i][...]
    pool[subs * rows] = jnp.zeros(pool.shape[1:], pool.dtype)
    last = (subs - 1) * rows
    near_ref[...] = pool[pl.ds((1 - odd) * last, rows)]
    far_ref[...] = pool[pl.ds(odd * last, rows)]


def owner_rows(me, k):
    start = pl.multiple_of(lax.bitwise_xor(me, k) * COARSE_ROWS, COARSE_ROWS)
    return pl.ds(start, COARSE_ROWS)


def edge_kernel(subs, half, cols_ref, count_ref, pair_ref, a_hbm, own_0, own_1, *rest):
    outs, (a_ref, out_ref, turned, sems) = rest[:subs], rest[subs:]
    rows, slots, tile = a_ref.shape[:3]
    first = lax.axis_index("dom") * (subs * rows)
    me = lax.axis_index("sub")
    loads = [pltpu.make_async_copy(a_hbm.at[f], a_ref.at[f], sems.at[f]) for f in range(rows)]
    for load in loads:
        load.start()
    out_ref[...] = jnp.zeros(out_ref.shape, F32)
    for f in range(rows):
        turned[f] = (own_0, own_1)[f // (rows // 2)][f % (rows // 2)].T
    for f in range(rows):
        loads[f].wait()
        for k in range(slots):
            rel = cols_ref[f, k] - first
            live = (k < count_ref[f]) & ((rel < 0) | (rel >= subs * rows))

            @pl.when(live)
            def _():
                at = jnp.where(rel < 0, rel + rows, rel - subs * rows + rows)
                term = jnp.dot(turned[f], a_ref[f, k], preferred_element_type=F32)
                if half == 1:
                    out_ref[at] += term
                else:
                    m = pair_ref[rows + me * rows + f]
                    for start, part in ((m, term[:tile]), (m + half, term[tile:])):
                        out_ref[at, pl.ds(pl.multiple_of(start * tile, tile), tile)] += part
    for k in range(subs):
        for c in range(2 * rows):
            part = out_ref[c, owner_rows(me, k)]
            outs[k][:, c * tile : (c + 1) * tile] = part.astype(outs[k].dtype)


def group_kernel(subs, half, cols_ref, count_ref, pair_ref, a_ref, pool, *rest):
    outs, (q, mid_ref) = rest[:subs], rest[subs:]
    rows, slots, tile = a_ref.shape[0], a_ref.shape[1], a_ref.shape[2]
    zero = subs * rows
    width = 2 * half * tile
    me = lax.axis_index("sub")
    first = lax.axis_index("dom") * (subs * rows)
    for f in range(rows):
        a_row = side_by_side(a_ref, f)
        index = [[None] * slots for _ in range(half)]
        for k in range(slots):
            rel = cols_ref[f, k] - first
            inside = (rel >= 0) & (rel < zero) & (k < count_ref[f])
            safe = jnp.where(inside, rel, 0)
            for m in range(half):
                here = inside if half == 1 else inside & (pair_ref[rows + safe] == m)
                index[m][k] = jnp.where(here, safe, zero)
        for m in range(half):
            block = placed_product(a_row, pool, index[m])
            lo, hi = m * tile, (m + half) * tile
            q[f * tile : (f + 1) * tile, lo : lo + tile] = block[:, :tile]
            q[f * tile : (f + 1) * tile, hi : hi + tile] = block[:, tile:]
    for m, out in enumerate(restrict(own_tiles(rows, zero, half, me, pair_ref, pool), q[...], half)):
        mid_ref[m * tile : (m + 1) * tile] = out[:tile]
        mid_ref[(m + half) * tile : (m + half + 1) * tile] = out[tile:]
    for k in range(subs):
        outs[k][...] = mid_ref[owner_rows(me, k)].astype(outs[k].dtype)


def total_of(refs):
    total = refs[0][...]
    for ref in refs[1:]:
        total = total + ref[...].astype(F32)
    return total


def sum_kernel(subs, *refs):
    mid_ref, out_ref = refs[2 * subs :]
    mid_ref[...] = total_of(refs[subs : 2 * subs]).astype(BF16)
    total = total_of(refs[:subs])
    high = total.astype(BF16)
    out_ref[:COARSE_ROWS] = high
    out_ref[COARSE_ROWS:] = (total - high.astype(F32)).astype(BF16)


def finish_kernel(subs, half, pair_ref, near_ref, far_ref, mid_ref, both_ref, out_ref, edge):
    rows, tile = near_ref.shape[:2]
    width = 2 * half * tile
    odd = lax.rem(lax.axis_index("dom"), 2)
    edge[pl.ds((1 - odd) * rows, rows)] = near_ref[...]
    edge[pl.ds(odd * rows, rows)] = far_ref[...]
    out_ref[:, width : 2 * width] = mid_ref[...]
    both = both_ref[...]
    for side in range(2):
        blocks = [jnp.zeros((COARSE_ROWS, tile), F32) for _ in range(2 * half)]
        tiles = range(side * rows, (side + 1) * rows)
        if half == 1:
            stacked = jnp.concatenate([edge[c] for c in tiles], axis=0)
            lhs = both[:, side * rows * tile : (side + 1) * rows * tile]
            term = jnp.dot(lhs, stacked, preferred_element_type=F32)
            term = term[:COARSE_ROWS] + term[COARSE_ROWS:]
            blocks = [term[:, :tile], term[:, tile:]]
        else:
            for c in tiles:
                lhs = both[:, c * tile : (c + 1) * tile]
                term = jnp.dot(lhs, edge[c], preferred_element_type=F32)
                term = term[:COARSE_ROWS] + term[COARSE_ROWS:]
                m_here = pair_ref[c if side == 0 else subs * rows + c]
                for m in range(half):
                    here = m_here == m
                    blocks[m] = blocks[m] + jnp.where(here, term[:, :tile], 0.0)
                    blocks[m + half] = blocks[m + half] + jnp.where(here, term[:, tile:], 0.0)
        for b in range(2 * half):
            at = 2 * side * width + b * tile
            out_ref[:, at : at + tile] = blocks[b].astype(BF16)


def local(a_tiles, a_cols, a_count, p_tiles, p_cols):
    rows, slots, tile = a_tiles.shape[:3]
    subs, doms = lax.axis_size("sub"), lax.axis_size("dom")
    coarse_group = subs * COARSE_ROWS // tile
    half = coarse_group // 2
    width = coarse_group * tile
    group_tiles = rows * subs

    smem = pl.BlockSpec(memory_space=pltpu.SMEM)
    vmem = pl.BlockSpec(memory_space=pltpu.VMEM)
    p_bytes = rows * tile * 2 * tile * 2
    a_bytes = a_tiles.size * 2
    spare = 3 << 20

    def exchange(value, k):
        return lax.ppermute(value, "sub", [(s, s ^ k) for s in range(subs)])

    own = pl.pallas_call(
        order_kernel,
        out_shape=[jax.ShapeDtypeStruct((rows // 2, tile, 2 * tile), BF16)] * 2,
        in_specs=[pl.BlockSpec(memory_space=pltpu.HBM)] * 2,
        out_specs=[vmem] * 2,
        scratch_shapes=[
            pltpu.SMEM((2, rows), jnp.int32),
            pltpu.VMEM(p_tiles.shape, BF16),
            pltpu.SemaphoreType.DMA((rows + 1,)),
        ],
        compiler_params=pltpu.CompilerParams(vmem_limit_bytes=spare),
        cost_estimate=pl.CostEstimate(
            flops=1 << 30, bytes_accessed=2 * p_bytes, transcendentals=0
        ),
        name="order_columns",
    )(
        pltpu.with_memory_space_constraint(p_cols.T, pltpu.HBM),
        pltpu.with_memory_space_constraint(p_tiles, pltpu.HBM),
    )

    if half == 1:
        pair = jnp.zeros((1,), jnp.int32)
    else:
        m_own = jnp.min(p_cols, axis=1) - lax.axis_index("dom") * coarse_group
        m_group = lax.all_gather(m_own, "sub", axis=0, tiled=True)
        m_left = lax.ppermute(
            m_group[group_tiles - rows :], "dom", [(d, d + 1) for d in range(doms - 1)]
        )
        m_right = lax.ppermute(m_group[:rows], "dom", [(d + 1, d) for d in range(doms - 1)])
        pair = jnp.concatenate([m_left, m_group, m_right])

    flops = 2 * rows * slots * tile * tile * 2 * tile * half
    span = 2 * rows * tile
    kinds = [F32] + [BF16] * (subs - 1)
    *edges, a_held = pl.pallas_call(
        functools.partial(edge_kernel, subs, half),
        out_shape=[jax.ShapeDtypeStruct((COARSE_ROWS, span), kind) for kind in kinds]
        + [jax.ShapeDtypeStruct(a_tiles.shape, BF16)],
        in_specs=[smem, smem, smem, pl.BlockSpec(memory_space=pltpu.HBM), vmem, vmem],
        out_specs=[vmem] * (subs + 1),
        scratch_shapes=[
            pltpu.VMEM((2 * rows, width, tile), F32),
            pltpu.VMEM((rows, 2 * tile, tile), BF16),
            pltpu.SemaphoreType.DMA((rows,)),
        ],
        compiler_params=pltpu.CompilerParams(vmem_limit_bytes=8 * rows * tile * width + spare),
        cost_estimate=pl.CostEstimate(
            flops=flops, bytes_accessed=a_bytes + p_bytes, transcendentals=0
        ),
        name="edge_part",
    )(a_cols, a_count, pair, pltpu.with_memory_space_constraint(a_tiles, pltpu.HBM), *own)

    tiles = [list(own)] + [[None, None] for _ in range(subs - 1)]
    for k in range(1, subs):
        low, high = k & -k, 1 << (k.bit_length() - 1)
        tiles[k][0] = exchange(tiles[k ^ low][0], low)
        tiles[k][1] = exchange(tiles[k ^ high][1], high)
    edge_terms = edges[:1] + [exchange(edges[k], k) for k in range(1, subs)]
    pool, to_near, to_far = pl.pallas_call(
        functools.partial(assemble_kernel, subs),
        out_shape=[
            jax.ShapeDtypeStruct((n, tile, 2 * tile), BF16) for n in (group_tiles + 1, rows, rows)
        ],
        in_specs=[vmem] * (2 * subs),
        out_specs=[vmem] * 3,
        compiler_params=pltpu.CompilerParams(vmem_limit_bytes=spare),
        cost_estimate=pl.CostEstimate(flops=1 << 20, bytes_accessed=1 << 20, transcendentals=0),
        name="assemble",
    )(*sum(tiles, []))
    far = lax.ppermute(to_far, "dom", [(d, d - 1 + 2 * (d % 2)) for d in range(1, doms - 1)])
    near = lax.ppermute(to_near, "dom", [(d, d ^ 1) for d in range(doms)])
    mids = pl.pallas_call(
        functools.partial(group_kernel, subs, half),
        out_shape=[jax.ShapeDtypeStruct((COARSE_ROWS, width), kind) for kind in kinds],
        in_specs=[smem, smem, smem, vmem, vmem],
        out_specs=[vmem] * subs,
        scratch_shapes=[
            pltpu.VMEM((rows * tile, width), BF16),
            pltpu.VMEM((width, width), F32),
        ],
        compiler_params=pltpu.CompilerParams(
            vmem_limit_bytes=2 * rows * tile * width + 4 * width * width + spare
        ),
        cost_estimate=pl.CostEstimate(flops=1 << 20, bytes_accessed=1 << 20, transcendentals=0),
        name="group_part",
    )(a_cols, a_count, pair, a_held, pool)
    mid_terms = [mids[0]] + [exchange(mids[k], k) for k in range(1, subs)]
    mid, both = pl.pallas_call(
        functools.partial(sum_kernel, subs),
        out_shape=[
            jax.ShapeDtypeStruct((COARSE_ROWS, width), BF16),
            jax.ShapeDtypeStruct((2 * COARSE_ROWS, span), BF16),
        ],
        in_specs=[vmem] * (2 * subs),
        out_specs=[vmem] * 2,
        compiler_params=pltpu.CompilerParams(vmem_limit_bytes=spare),
        cost_estimate=pl.CostEstimate(flops=7 << 28, bytes_accessed=1 << 20, transcendentals=0),
        name="sum_parts",
    )(*edge_terms, *mid_terms)
    return pl.pallas_call(
        functools.partial(finish_kernel, subs, half),
        out_shape=jax.ShapeDtypeStruct((COARSE_ROWS, 3 * width), BF16),
        in_specs=[smem] + [vmem] * 4,
        out_specs=vmem,
        scratch_shapes=[pltpu.VMEM((2 * rows, tile, 2 * tile), BF16)],
        compiler_params=pltpu.CompilerParams(vmem_limit_bytes=2 * p_bytes + spare),
        cost_estimate=pl.CostEstimate(flops=1 << 20, bytes_accessed=1 << 20, transcendentals=0),
        name="finish",
    )(pair, near, far, mid, both)


def solution(mesh):
    placed = (
        P(("dom", "sub"), None, None, None),
        P(("dom", "sub"), None),
        P(("dom", "sub")),
        P(("dom", "sub"), None, None),
        P(("dom", "sub"), None),
    )
    return jax.shard_map(
        local, mesh=mesh, in_specs=placed, out_specs=P(("dom", "sub"), None), check_vma=False
    )
```

```python
import functools

import jax
import jax.numpy as jnp
from jax import lax
from jax.experimental import pallas as pl
from jax.experimental.pallas import tpu as pltpu
from jax.sharding import PartitionSpec as P

COARSE_ROWS = 64
BF16 = jnp.bfloat16
F32 = jnp.float32


def side_by_side(a_ref, f):
    return jnp.concatenate([a_ref[f, k] for k in range(a_ref.shape[1])], axis=1)


def placed_product(a_row, pool, index):
    stacked = jnp.concatenate([pool[i] for i in index], axis=0)
    return jnp.dot(a_row, stacked, preferred_element_type=F32).astype(BF16)


def own_tiles(rows, zero, half, me, pair_ref, pool):
    tiles = []
    for m in range(half):
        at = [me * rows + f for f in range(rows)]
        if half > 1:
            at = [jnp.where(pair_ref[rows + i] == m, i, zero) for i in at]
        tiles.append([pool[i] for i in at])
    return tiles


def restrict(tiles, q, half):
    outs = []
    for m in range(half):
        lhs = jnp.concatenate(tiles[m], axis=0)
        outs.append(
            lax.dot_general(lhs, q, (((0,), (0,)), ((), ())), preferred_element_type=F32)
        )
    return outs


def order_kernel(cols_hbm, p_hbm, *rest):
    outs, (cols_ref, p_ref, sems) = rest[:2], rest[2:]
    rows, tile = p_ref.shape[:2]
    piece = rows // 2
    lists = pltpu.make_async_copy(cols_hbm, cols_ref, sems.at[rows])
    lists.start()
    loads = [pltpu.make_async_copy(p_hbm.at[f], p_ref.at[f], sems.at[f]) for f in range(rows)]
    for load in loads:
        load.start()
    lists.wait()
    for f in range(rows):
        loads[f].wait()
        first = pl.multiple_of(jnp.where(cols_ref[0, f] > cols_ref[1, f], tile, 0), tile)
        for t, start in ((0, first), (1, pl.multiple_of(tile - first, tile))):
            outs[f // piece][f % piece, :, t * tile : (t + 1) * tile] = p_ref[f, :, pl.ds(start, tile)]


def hand_out_kernel(subs, pool, near_ref, far_ref):
    rows = near_ref.shape[0]
    odd = lax.rem(lax.axis_index("dom"), 2)
    last = (subs - 1) * rows
    near_ref[...] = pool[pl.ds((1 - odd) * last, rows)]
    far_ref[...] = pool[pl.ds(odd * last, rows)]


def edge_kernel(subs, half, cols_ref, count_ref, pair_ref, a_hbm, own_0, own_1, *rest):
    out_ref, a_ref, turned, sems = rest
    rows, slots, tile = a_ref.shape[:3]
    first = lax.axis_index("dom") * (subs * rows)
    me = lax.axis_index("sub")
    loads = [pltpu.make_async_copy(a_hbm.at[f], a_ref.at[f], sems.at[f]) for f in range(rows)]
    for load in loads:
        load.start()
    out_ref[...] = jnp.zeros(out_ref.shape, F32)
    for f in range(rows):
        turned[f] = (own_0, own_1)[f // (rows // 2)][f % (rows // 2)].T
    for f in range(rows):
        loads[f].wait()
        for k in range(slots):
            rel = cols_ref[f, k] - first
            live = (k < count_ref[f]) & ((rel < 0) | (rel >= subs * rows))

            @pl.when(live)
            def _():
                at = jnp.where(rel < 0, rel + rows, rel - subs * rows + rows)
                term = jnp.dot(turned[f], a_ref[f, k], preferred_element_type=F32)
                if half == 1:
                    out_ref[at] += term
                else:
                    m = pair_ref[rows + me * rows + f]
                    for start, part in ((m, term[:tile]), (m + half, term[tile:])):
                        out_ref[at, pl.ds(pl.multiple_of(start * tile, tile), tile)] += part


def group_kernel(subs, half, cols_ref, count_ref, pair_ref, a_ref, edge_ref, *rest):
    p_refs, rest = rest[: 2 * subs], rest[2 * subs :]
    outs, (pool, q, mid_ref) = rest[:subs], rest[subs:]
    rows, slots, tile = a_ref.shape[0], a_ref.shape[1], a_ref.shape[2]
    zero = subs * rows
    width = 2 * half * tile
    me = lax.axis_index("sub")
    first = lax.axis_index("dom") * (subs * rows)
    piece = rows // 2
    for k in range(subs):
        for i in range(2):
            pool[pl.ds(lax.bitwise_xor(me, k) * rows + i * piece, piece)] = p_refs[2 * k + i][...]
    pool[zero] = jnp.zeros(pool.shape[1:], pool.dtype)
    for f in range(rows):
        a_row = side_by_side(a_ref, f)
        index = [[None] * slots for _ in range(half)]
        for k in range(slots):
            rel = cols_ref[f, k] - first
            inside = (rel >= 0) & (rel < zero) & (k < count_ref[f])
            safe = jnp.where(inside, rel, 0)
            for m in range(half):
                here = inside if half == 1 else inside & (pair_ref[rows + safe] == m)
                index[m][k] = jnp.where(here, safe, zero)
        for m in range(half):
            block = placed_product(a_row, pool, index[m])
            lo, hi = m * tile, (m + half) * tile
            q[f * tile : (f + 1) * tile, lo : lo + tile] = block[:, :tile]
            q[f * tile : (f + 1) * tile, hi : hi + tile] = block[:, tile:]
    for m, out in enumerate(restrict(own_tiles(rows, zero, half, me, pair_ref, pool), q[...], half)):
        mid_ref[m * tile : (m + 1) * tile] = out[:tile]
        mid_ref[(m + half) * tile : (m + half + 1) * tile] = out[tile:]
    for k in range(subs):
        at = pl.ds(pl.multiple_of(lax.bitwise_xor(me, k) * COARSE_ROWS, COARSE_ROWS), COARSE_ROWS)
        kind = outs[k].dtype
        outs[k][:, :width] = mid_ref[at].astype(kind)
        for c in range(2 * rows):
            outs[k][:, width + c * tile : width + (c + 1) * tile] = edge_ref[c, at].astype(kind)


def halo_product(subs, half, side, pair_ref, terms, p_ref):
    rows, tile = p_ref.shape[:2]
    if half == 1:
        stacked = jnp.concatenate([p_ref[t] for t in range(rows)], axis=0)
        out = jnp.dot(terms, stacked, preferred_element_type=F32)
        out = out[:COARSE_ROWS] + out[COARSE_ROWS:]
        return [out[:, :tile], out[:, tile:]]
    blocks = [jnp.zeros((COARSE_ROWS, tile), F32) for _ in range(2 * half)]
    for t in range(rows):
        lhs = terms[:, t * tile : (t + 1) * tile]
        out = jnp.dot(lhs, p_ref[t], preferred_element_type=F32)
        out = out[:COARSE_ROWS] + out[COARSE_ROWS:]
        m_here = pair_ref[side * (subs + 1) * rows + t]
        for m in range(half):
            blocks[m] = blocks[m] + jnp.where(m_here == m, out[:, :tile], 0.0)
            blocks[m + half] = blocks[m + half] + jnp.where(m_here == m, out[:, tile:], 0.0)
    return blocks


def sum_kernel(*refs):
    total = refs[0][...]
    for ref in refs[1:-1]:
        total = total + ref[...].astype(F32)
    refs[-1][...] = total


def near_kernel(subs, half, pair_ref, near_ref, sum_ref, last_ref, *rest):
    mid_ref, side_ref, terms_ref, total = rest
    rows, tile = near_ref.shape[:2]
    width, span = 2 * half * tile, rows * tile
    odd = lax.rem(lax.axis_index("dom"), 2)
    total[...] = sum_ref[...] + last_ref[...].astype(F32)
    mid_ref[...] = total[:, :width].astype(BF16)

    def terms(side):
        value = total[:, pl.ds(pl.multiple_of(width + side * span, tile), span)]
        high = value.astype(BF16)
        return jnp.concatenate([high, (value - high.astype(F32)).astype(BF16)], axis=0)

    terms_ref[...] = terms(odd)
    blocks = halo_product(subs, half, 1 - odd, pair_ref, terms(1 - odd), near_ref)
    for b in range(2 * half):
        side_ref[:, b * tile : (b + 1) * tile] = blocks[b].astype(BF16)


def finish_kernel(subs, half, pair_ref, far_ref, terms_ref, mid_ref, side_ref, out_ref):
    tile = far_ref.shape[1]
    width = 2 * half * tile
    odd = lax.rem(lax.axis_index("dom"), 2)
    out_ref[:, width : 2 * width] = mid_ref[...]
    out_ref[:, pl.ds(pl.multiple_of((1 - odd) * 2 * width, tile), width)] = side_ref[...]
    blocks = halo_product(subs, half, odd, pair_ref, terms_ref[...], far_ref)
    for b in range(2 * half):
        at = pl.multiple_of(odd * 2 * width + b * tile, tile)
        out_ref[:, pl.ds(at, tile)] = blocks[b].astype(BF16)


def local(a_tiles, a_cols, a_count, p_tiles, p_cols):
    rows, slots, tile = a_tiles.shape[:3]
    subs, doms = lax.axis_size("sub"), lax.axis_size("dom")
    coarse_group = subs * COARSE_ROWS // tile
    half = coarse_group // 2
    width = coarse_group * tile
    group_tiles = rows * subs

    smem = pl.BlockSpec(memory_space=pltpu.SMEM)
    vmem = pl.BlockSpec(memory_space=pltpu.VMEM)
    p_bytes = rows * tile * 2 * tile * 2
    a_bytes = a_tiles.size * 2
    spare = 3 << 20

    def exchange(value, k):
        return lax.ppermute(value, "sub", [(s, s ^ k) for s in range(subs)])

    own = pl.pallas_call(
        order_kernel,
        out_shape=[jax.ShapeDtypeStruct((rows // 2, tile, 2 * tile), BF16)] * 2,
        in_specs=[pl.BlockSpec(memory_space=pltpu.HBM)] * 2,
        out_specs=[vmem] * 2,
        scratch_shapes=[
            pltpu.SMEM((2, rows), jnp.int32),
            pltpu.VMEM(p_tiles.shape, BF16),
            pltpu.SemaphoreType.DMA((rows + 1,)),
        ],
        compiler_params=pltpu.CompilerParams(vmem_limit_bytes=spare),
        cost_estimate=pl.CostEstimate(
            flops=1 << 30, bytes_accessed=2 * p_bytes, transcendentals=0
        ),
        name="order_columns",
    )(
        pltpu.with_memory_space_constraint(p_cols.T, pltpu.HBM),
        pltpu.with_memory_space_constraint(p_tiles, pltpu.HBM),
    )

    if half == 1:
        pair = jnp.zeros((1,), jnp.int32)
    else:
        m_own = jnp.min(p_cols, axis=1) - lax.axis_index("dom") * coarse_group
        m_group = lax.all_gather(m_own, "sub", axis=0, tiled=True)
        m_left = lax.ppermute(
            m_group[group_tiles - rows :], "dom", [(d, d + 1) for d in range(doms - 1)]
        )
        m_right = lax.ppermute(m_group[:rows], "dom", [(d + 1, d) for d in range(doms - 1)])
        pair = jnp.concatenate([m_left, m_group, m_right])

    flops = 2 * rows * slots * tile * tile * 2 * tile * half
    edges, a_held = pl.pallas_call(
        functools.partial(edge_kernel, subs, half),
        out_shape=[
            jax.ShapeDtypeStruct((2 * rows, width, tile), F32),
            jax.ShapeDtypeStruct(a_tiles.shape, BF16),
        ],
        in_specs=[smem, smem, smem, pl.BlockSpec(memory_space=pltpu.HBM), vmem, vmem],
        out_specs=[vmem] * 2,
        scratch_shapes=[
            pltpu.VMEM((rows, 2 * tile, tile), BF16),
            pltpu.SemaphoreType.DMA((rows,)),
        ],
        compiler_params=pltpu.CompilerParams(vmem_limit_bytes=8 * rows * tile * width + spare),
        cost_estimate=pl.CostEstimate(
            flops=flops, bytes_accessed=a_bytes + p_bytes, transcendentals=0
        ),
        name="edge_part",
    )(a_cols, a_count, pair, pltpu.with_memory_space_constraint(a_tiles, pltpu.HBM), *own)

    tiles = [list(own)] + [[None, None] for _ in range(subs - 1)]
    for k in range(1, subs):
        low, high = k & -k, 1 << (k.bit_length() - 1)
        tiles[k][0] = exchange(tiles[k ^ low][0], low)
        tiles[k][1] = exchange(tiles[k ^ high][1], high)
    span = width + 2 * rows * tile
    *parts, pool = pl.pallas_call(
        functools.partial(group_kernel, subs, half),
        out_shape=[
            jax.ShapeDtypeStruct((COARSE_ROWS, span), F32 if k == 0 else BF16)
            for k in range(subs)
        ]
        + [jax.ShapeDtypeStruct((group_tiles + 1, tile, 2 * tile), BF16)],
        in_specs=[smem, smem, smem] + [vmem] * (2 * subs + 2),
        out_specs=[vmem] * (subs + 1),
        scratch_shapes=[
            pltpu.VMEM((rows * tile, width), BF16),
            pltpu.VMEM((width, width), F32),
        ],
        compiler_params=pltpu.CompilerParams(
            vmem_limit_bytes=2 * rows * tile * width + 4 * width * width + spare
        ),
        cost_estimate=pl.CostEstimate(
            flops=flops, bytes_accessed=a_bytes + subs * p_bytes, transcendentals=0
        ),
        name="group_part",
    )(a_cols, a_count, pair, a_held, edges, *sum(tiles, []))
    received = [exchange(parts[k], k) for k in range(1, subs)]
    to_near, to_far = pl.pallas_call(
        functools.partial(hand_out_kernel, subs),
        out_shape=[jax.ShapeDtypeStruct(p_tiles.shape, BF16)] * 2,
        in_specs=[vmem],
        out_specs=[vmem] * 2,
        compiler_params=pltpu.CompilerParams(vmem_limit_bytes=spare),
        name="hand_out",
    )(pool)
    far = lax.ppermute(
        to_far, "dom", [(d, d - 1 + 2 * (d % 2)) for d in range(1, doms - 1)]
    )
    near = lax.ppermute(to_near, "dom", [(d, d ^ 1) for d in range(doms)])
    sums = pl.pallas_call(
        sum_kernel,
        out_shape=jax.ShapeDtypeStruct((COARSE_ROWS, span), F32),
        in_specs=[vmem] * (subs - 1),
        out_specs=vmem,
        compiler_params=pltpu.CompilerParams(vmem_limit_bytes=spare),
        cost_estimate=pl.CostEstimate(flops=3 << 29, bytes_accessed=1 << 20, transcendentals=0),
        name="sum_parts",
    )(parts[0], *received[:-1])
    mid, side, terms = pl.pallas_call(
        functools.partial(near_kernel, subs, half),
        out_shape=[
            jax.ShapeDtypeStruct((COARSE_ROWS, width), BF16),
            jax.ShapeDtypeStruct((COARSE_ROWS, width), BF16),
            jax.ShapeDtypeStruct((2 * COARSE_ROWS, rows * tile), BF16),
        ],
        in_specs=[smem] + [vmem] * 3,
        out_specs=[vmem] * 3,
        scratch_shapes=[pltpu.VMEM((COARSE_ROWS, span), F32)],
        compiler_params=pltpu.CompilerParams(vmem_limit_bytes=2 * p_bytes + spare),
        cost_estimate=pl.CostEstimate(flops=1 << 20, bytes_accessed=1 << 20, transcendentals=0),
        name="near_part",
    )(pair, near, sums, received[-1])
    return pl.pallas_call(
        functools.partial(finish_kernel, subs, half),
        out_shape=jax.ShapeDtypeStruct((COARSE_ROWS, 3 * width), BF16),
        in_specs=[smem] + [vmem] * 4,
        out_specs=vmem,
        compiler_params=pltpu.CompilerParams(vmem_limit_bytes=2 * p_bytes + spare),
        cost_estimate=pl.CostEstimate(flops=1 << 20, bytes_accessed=1 << 20, transcendentals=0),
        name="far_part",
    )(pair, far, terms, mid, side)


def solution(mesh):
    placed = (
        P(("dom", "sub"), None, None, None),
        P(("dom", "sub"), None),
        P(("dom", "sub")),
        P(("dom", "sub"), None, None),
        P(("dom", "sub"), None),
    )
    return jax.shard_map(
        local, mesh=mesh, in_specs=placed, out_specs=P(("dom", "sub"), None), check_vma=False
    )
```

```python
import functools

import jax
import jax.numpy as jnp
from jax import lax
from jax.experimental import pallas as pl
from jax.experimental.pallas import tpu as pltpu
from jax.sharding import PartitionSpec as P

COARSE_ROWS = 64
BF16 = jnp.bfloat16
F32 = jnp.float32


def side_by_side(a_ref, f):
    return jnp.concatenate([a_ref[f, k] for k in range(a_ref.shape[1])], axis=1)


def placed_product(a_row, pool, index):
    stacked = jnp.concatenate([pool[i] for i in index], axis=0)
    return jnp.dot(a_row, stacked, preferred_element_type=F32).astype(BF16)


def own_tiles(rows, zero, half, me, pair_ref, pool):
    tiles = []
    for m in range(half):
        at = [me * rows + f for f in range(rows)]
        if half > 1:
            at = [jnp.where(pair_ref[rows + i] == m, i, zero) for i in at]
        tiles.append([pool[i] for i in at])
    return tiles


def restrict(tiles, q, half):
    outs = []
    for m in range(half):
        lhs = jnp.concatenate(tiles[m], axis=0)
        outs.append(
            lax.dot_general(lhs, q, (((0,), (0,)), ((), ())), preferred_element_type=F32)
        )
    return outs


def order_kernel(cols_hbm, p_hbm, *rest):
    outs, (cols_ref, p_ref, sems) = rest[:2], rest[2:]
    rows, tile = p_ref.shape[:2]
    piece = rows // 2
    lists = pltpu.make_async_copy(cols_hbm, cols_ref, sems.at[rows])
    lists.start()
    loads = [pltpu.make_async_copy(p_hbm.at[f], p_ref.at[f], sems.at[f]) for f in range(rows)]
    for load in loads:
        load.start()
    lists.wait()
    for f in range(rows):
        loads[f].wait()
        first = pl.multiple_of(jnp.where(cols_ref[0, f] > cols_ref[1, f], tile, 0), tile)
        for t, start in ((0, first), (1, pl.multiple_of(tile - first, tile))):
            outs[f // piece][f % piece, :, t * tile : (t + 1) * tile] = p_ref[f, :, pl.ds(start, tile)]


def hand_out_kernel(subs, pool, near_ref, far_ref):
    rows = near_ref.shape[0]
    odd = lax.rem(lax.axis_index("dom"), 2)
    last = (subs - 1) * rows
    near_ref[...] = pool[pl.ds((1 - odd) * last, rows)]
    far_ref[...] = pool[pl.ds(odd * last, rows)]


def edge_kernel(subs, half, cols_ref, count_ref, pair_ref, a_hbm, own_0, own_1, *rest):
    out_ref, a_ref, turned, sems = rest
    rows, slots, tile = a_ref.shape[:3]
    first = lax.axis_index("dom") * (subs * rows)
    me = lax.axis_index("sub")
    loads = [pltpu.make_async_copy(a_hbm.at[f], a_ref.at[f], sems.at[f]) for f in range(rows)]
    for load in loads:
        load.start()
    out_ref[...] = jnp.zeros(out_ref.shape, F32)
    for f in range(rows):
        turned[f] = (own_0, own_1)[f // (rows // 2)][f % (rows // 2)].T
    for f in range(rows):
        loads[f].wait()
        for k in range(slots):
            rel = cols_ref[f, k] - first
            live = (k < count_ref[f]) & ((rel < 0) | (rel >= subs * rows))

            @pl.when(live)
            def _():
                at = jnp.where(rel < 0, rel + rows, rel - subs * rows + rows)
                term = jnp.dot(turned[f], a_ref[f, k], preferred_element_type=F32)
                if half == 1:
                    out_ref[at] += term
                else:
                    m = pair_ref[rows + me * rows + f]
                    for start, part in ((m, term[:tile]), (m + half, term[tile:])):
                        out_ref[at, pl.ds(pl.multiple_of(start * tile, tile), tile)] += part


def terms_kernel(subs, cols_ref, count_ref, a_hbm, own_0, own_1, *rest):
    edges, (high_ref, low_ref, a_ref, total, turned, sems) = rest[:subs], rest[subs:]
    rows, slots, tile = a_ref.shape[:3]
    tiles = total.shape[0] - 1
    me = lax.axis_index("sub")
    base = lax.axis_index("dom") * (subs * rows) - rows
    loads = [pltpu.make_async_copy(a_hbm.at[f], a_ref.at[f], sems.at[f]) for f in range(rows)]
    for load in loads:
        load.start()
    total[...] = jnp.zeros(total.shape, F32)
    for f in range(rows):
        turned[f] = (own_0, own_1)[f // (rows // 2)][f % (rows // 2)].T
    for f in range(rows):
        loads[f].wait()
        for k in range(slots):
            at = jnp.where(k < count_ref[f], cols_ref[f, k] - base, tiles)
            total[at] += jnp.dot(turned[f], a_ref[f, k], preferred_element_type=F32)
    for c in range(subs * rows):
        value = total[rows + c]
        high = value.astype(BF16)
        high_ref[c] = high
        low_ref[c] = (value - high.astype(F32)).astype(BF16)
    for k in range(subs):
        start = pl.multiple_of(lax.bitwise_xor(me, k) * COARSE_ROWS, COARSE_ROWS)
        for i, c in enumerate([*range(rows), *range(tiles - rows, tiles)]):
            part = total[c, pl.ds(start, COARSE_ROWS)]
            edges[k][:, i * tile : (i + 1) * tile] = part.astype(edges[k].dtype)


def terms_product(rows, sources, high_ref, low_ref, p_refs):
    me = lax.axis_index("sub")
    both = []
    for ref in (high_ref, low_ref):
        at = [lax.bitwise_xor(me, k) * rows + f for k in sources for f in range(rows)]
        both.append(jnp.concatenate([ref[i] for i in at], axis=1))
    stacked = jnp.concatenate([ref[i] for ref in p_refs for i in range(ref.shape[0])], axis=0)
    out = jnp.dot(jnp.concatenate(both, axis=0), stacked, preferred_element_type=F32)
    height = high_ref.shape[1]
    return out[:height] + out[height:]


def early_kernel(rows, sources, high_ref, low_ref, *rest):
    rest[-1][...] = terms_product(rows, sources, high_ref, low_ref, rest[:-1])


def late_kernel(subs, rows, sources, high_ref, low_ref, early_ref, *rest):
    p_refs, rest = rest[: 2 * len(sources)], rest[2 * len(sources) :]
    edges, outs, mid = rest[:subs], rest[subs:-1], rest[-1]
    width = mid.shape[1]
    mid[...] = early_ref[...] + terms_product(rows, sources, high_ref, low_ref, p_refs)
    me = lax.axis_index("sub")
    for k in range(subs):
        start = pl.multiple_of(lax.bitwise_xor(me, k) * COARSE_ROWS, COARSE_ROWS)
        outs[k][:, :width] = mid[pl.ds(start, COARSE_ROWS)].astype(outs[k].dtype)
        outs[k][:, width:] = edges[k][...]


def hand_out_pieces_kernel(subs, *refs):
    p_refs, (near_ref, far_ref, ends) = refs[: 2 * subs], refs[2 * subs :]
    rows, piece = near_ref.shape[0], p_refs[0].shape[0]
    me, odd = lax.axis_index("sub"), lax.rem(lax.axis_index("dom"), 2)
    for k in range(subs):
        for at, who in ((0, 0), (rows, subs - 1)):

            @pl.when(me == who ^ k)
            def _():
                for i in range(2):
                    ends[at + i * piece : at + (i + 1) * piece] = p_refs[2 * k + i][...]

    near_ref[...] = ends[pl.ds((1 - odd) * rows, rows)]
    far_ref[...] = ends[pl.ds(odd * rows, rows)]


def group_kernel(subs, half, cols_ref, count_ref, pair_ref, a_ref, edge_ref, *rest):
    p_refs, rest = rest[: 2 * subs], rest[2 * subs :]
    outs, (pool, q, mid_ref) = rest[:subs], rest[subs:]
    rows, slots, tile = a_ref.shape[0], a_ref.shape[1], a_ref.shape[2]
    zero = subs * rows
    width = 2 * half * tile
    me = lax.axis_index("sub")
    first = lax.axis_index("dom") * (subs * rows)
    piece = rows // 2
    for k in range(subs):
        for i in range(2):
            pool[pl.ds(lax.bitwise_xor(me, k) * rows + i * piece, piece)] = p_refs[2 * k + i][...]
    pool[zero] = jnp.zeros(pool.shape[1:], pool.dtype)
    for f in range(rows):
        a_row = side_by_side(a_ref, f)
        index = [[None] * slots for _ in range(half)]
        for k in range(slots):
            rel = cols_ref[f, k] - first
            inside = (rel >= 0) & (rel < zero) & (k < count_ref[f])
            safe = jnp.where(inside, rel, 0)
            for m in range(half):
                here = inside if half == 1 else inside & (pair_ref[rows + safe] == m)
                index[m][k] = jnp.where(here, safe, zero)
        for m in range(half):
            block = placed_product(a_row, pool, index[m])
            lo, hi = m * tile, (m + half) * tile
            q[f * tile : (f + 1) * tile, lo : lo + tile] = block[:, :tile]
            q[f * tile : (f + 1) * tile, hi : hi + tile] = block[:, tile:]
    for m, out in enumerate(restrict(own_tiles(rows, zero, half, me, pair_ref, pool), q[...], half)):
        mid_ref[m * tile : (m + 1) * tile] = out[:tile]
        mid_ref[(m + half) * tile : (m + half + 1) * tile] = out[tile:]
    for k in range(subs):
        at = pl.ds(pl.multiple_of(lax.bitwise_xor(me, k) * COARSE_ROWS, COARSE_ROWS), COARSE_ROWS)
        kind = outs[k].dtype
        outs[k][:, :width] = mid_ref[at].astype(kind)
        for c in range(2 * rows):
            outs[k][:, width + c * tile : width + (c + 1) * tile] = edge_ref[c, at].astype(kind)


def sum_kernel(subs, width, *refs):
    part_refs, (mid_ref, edge_ref) = refs[:subs], refs[subs:]
    total = part_refs[0][...]
    for k in range(1, subs):
        total = total + part_refs[k][...].astype(F32)
    mid_ref[...] = total[:, :width].astype(BF16)
    sums = total[:, width:]
    high = sums.astype(BF16)
    edge_ref[:COARSE_ROWS] = high
    edge_ref[COARSE_ROWS:] = (sums - high.astype(F32)).astype(BF16)


def finish_kernel(subs, half, pair_ref, far_ref, near_ref, mid_ref, both_ref, out_ref, edge):
    rows, tile = near_ref.shape[:2]
    width = 2 * half * tile
    odd = lax.rem(lax.axis_index("dom"), 2)
    edge[pl.ds((1 - odd) * rows, rows)] = near_ref[...]
    edge[pl.ds(odd * rows, rows)] = far_ref[...]
    out_ref[:, width : 2 * width] = mid_ref[...]
    both = both_ref[...]
    for side in range(2):
        blocks = [jnp.zeros((COARSE_ROWS, tile), F32) for _ in range(2 * half)]
        tiles = range(side * rows, (side + 1) * rows)
        if half == 1:
            stacked = jnp.concatenate([edge[c] for c in tiles], axis=0)
            lhs = both[:, side * rows * tile : (side + 1) * rows * tile]
            term = jnp.dot(lhs, stacked, preferred_element_type=F32)
            term = term[:COARSE_ROWS] + term[COARSE_ROWS:]
            blocks = [term[:, :tile], term[:, tile:]]
        else:
            for c in tiles:
                lhs = both[:, c * tile : (c + 1) * tile]
                term = jnp.dot(lhs, edge[c], preferred_element_type=F32)
                term = term[:COARSE_ROWS] + term[COARSE_ROWS:]
                m_here = pair_ref[c if side == 0 else subs * rows + c]
                for m in range(half):
                    here = m_here == m
                    blocks[m] = blocks[m] + jnp.where(here, term[:, :tile], 0.0)
                    blocks[m + half] = blocks[m + half] + jnp.where(here, term[:, tile:], 0.0)
        for b in range(2 * half):
            at = 2 * side * width + b * tile
            out_ref[:, at : at + tile] = blocks[b].astype(BF16)


def narrow_parts(a_tiles, a_cols, a_count, own, tiles, span):
    rows, slots, tile = a_tiles.shape[:3]
    subs = lax.axis_size("sub")
    width = 2 * tile
    smem = pl.BlockSpec(memory_space=pltpu.SMEM)
    vmem = pl.BlockSpec(memory_space=pltpu.VMEM)
    kinds = [F32] + [BF16] * (subs - 1)
    spare = 3 << 20
    products = 2 * width * rows * tile * width
    *edges, high, low = pl.pallas_call(
        functools.partial(terms_kernel, subs),
        out_shape=[jax.ShapeDtypeStruct((COARSE_ROWS, span - width), kind) for kind in kinds]
        + [jax.ShapeDtypeStruct((subs * rows, width, tile), BF16)] * 2,
        in_specs=[smem, smem, pl.BlockSpec(memory_space=pltpu.HBM), vmem, vmem],
        out_specs=[vmem] * (subs + 2),
        scratch_shapes=[
            pltpu.VMEM(a_tiles.shape, BF16),
            pltpu.VMEM(((subs + 2) * rows + 1, width, tile), F32),
            pltpu.VMEM((rows, width, tile), BF16),
            pltpu.SemaphoreType.DMA((rows,)),
        ],
        compiler_params=pltpu.CompilerParams(
            vmem_limit_bytes=2 * a_tiles.size + 4 * ((subs + 2) * rows + 1) * width * tile + spare
        ),
        cost_estimate=pl.CostEstimate(
            flops=1 << 31, bytes_accessed=2 * a_tiles.size, transcendentals=0
        ),
        name="terms",
    )(a_cols, a_count, pltpu.with_memory_space_constraint(a_tiles, pltpu.HBM), *own)
    first, last = list(range(subs - 1)), [subs - 1]
    early = pl.pallas_call(
        functools.partial(early_kernel, rows, first),
        out_shape=jax.ShapeDtypeStruct((width, width), F32),
        in_specs=[vmem] * (2 + 2 * len(first)),
        out_specs=vmem,
        compiler_params=pltpu.CompilerParams(vmem_limit_bytes=spare),
        cost_estimate=pl.CostEstimate(
            flops=2 * len(first) * products, bytes_accessed=1 << 20, transcendentals=0
        ),
        name="early_part",
    )(high, low, *[piece for k in first for piece in tiles[k]])
    return pl.pallas_call(
        functools.partial(late_kernel, subs, rows, last),
        out_shape=[jax.ShapeDtypeStruct((COARSE_ROWS, span), kind) for kind in kinds],
        in_specs=[vmem] * (3 + 2 * len(last) + subs),
        out_specs=[vmem] * subs,
        scratch_shapes=[pltpu.VMEM((width, width), F32)],
        compiler_params=pltpu.CompilerParams(vmem_limit_bytes=spare),
        cost_estimate=pl.CostEstimate(
            flops=2 * products, bytes_accessed=1 << 20, transcendentals=0
        ),
        name="late_part",
    )(high, low, early, *tiles[-1], *edges)


def local(a_tiles, a_cols, a_count, p_tiles, p_cols):
    rows, slots, tile = a_tiles.shape[:3]
    subs, doms = lax.axis_size("sub"), lax.axis_size("dom")
    coarse_group = subs * COARSE_ROWS // tile
    half = coarse_group // 2
    width = coarse_group * tile
    group_tiles = rows * subs

    smem = pl.BlockSpec(memory_space=pltpu.SMEM)
    vmem = pl.BlockSpec(memory_space=pltpu.VMEM)
    p_bytes = rows * tile * 2 * tile * 2
    a_bytes = a_tiles.size * 2
    spare = 3 << 20

    def exchange(value, k):
        return lax.ppermute(value, "sub", [(s, s ^ k) for s in range(subs)])

    own = pl.pallas_call(
        order_kernel,
        out_shape=[jax.ShapeDtypeStruct((rows // 2, tile, 2 * tile), BF16)] * 2,
        in_specs=[pl.BlockSpec(memory_space=pltpu.HBM)] * 2,
        out_specs=[vmem] * 2,
        scratch_shapes=[
            pltpu.SMEM((2, rows), jnp.int32),
            pltpu.VMEM(p_tiles.shape, BF16),
            pltpu.SemaphoreType.DMA((rows + 1,)),
        ],
        compiler_params=pltpu.CompilerParams(vmem_limit_bytes=spare),
        cost_estimate=pl.CostEstimate(
            flops=1 << 30, bytes_accessed=2 * p_bytes, transcendentals=0
        ),
        name="order_columns",
    )(
        pltpu.with_memory_space_constraint(p_cols.T, pltpu.HBM),
        pltpu.with_memory_space_constraint(p_tiles, pltpu.HBM),
    )

    tiles = [list(own)] + [[None, None] for _ in range(subs - 1)]
    for k in range(1, subs):
        low, high = k & -k, 1 << (k.bit_length() - 1)
        tiles[k][0] = exchange(tiles[k ^ low][0], low)
        tiles[k][1] = exchange(tiles[k ^ high][1], high)
    span = width + 2 * rows * tile
    if half == 1:
        pair = jnp.zeros((1,), jnp.int32)
    else:
        m_own = jnp.min(p_cols, axis=1) - lax.axis_index("dom") * coarse_group
        m_group = lax.all_gather(m_own, "sub", axis=0, tiled=True)
        m_left = lax.ppermute(
            m_group[group_tiles - rows :], "dom", [(d, d + 1) for d in range(doms - 1)]
        )
        m_right = lax.ppermute(m_group[:rows], "dom", [(d + 1, d) for d in range(doms - 1)])
        pair = jnp.concatenate([m_left, m_group, m_right])

    flat = [piece for pieces in tiles for piece in pieces]
    if half == 1:
        parts = narrow_parts(a_tiles, a_cols, a_count, own, tiles, span)
        to_near, to_far = pl.pallas_call(
            functools.partial(hand_out_pieces_kernel, subs),
            out_shape=[jax.ShapeDtypeStruct(p_tiles.shape, BF16)] * 2,
            in_specs=[vmem] * (2 * subs),
            out_specs=[vmem] * 2,
            scratch_shapes=[pltpu.VMEM((2 * rows, tile, 2 * tile), BF16)],
            compiler_params=pltpu.CompilerParams(vmem_limit_bytes=spare),
            name="hand_out",
        )(*flat)
    else:
        flops = 2 * rows * slots * tile * tile * 2 * tile * half
        edges, a_held = pl.pallas_call(
            functools.partial(edge_kernel, subs, half),
            out_shape=[
                jax.ShapeDtypeStruct((2 * rows, width, tile), F32),
                jax.ShapeDtypeStruct(a_tiles.shape, BF16),
            ],
            in_specs=[smem, smem, smem, pl.BlockSpec(memory_space=pltpu.HBM), vmem, vmem],
            out_specs=[vmem] * 2,
            scratch_shapes=[
                pltpu.VMEM((rows, 2 * tile, tile), BF16),
                pltpu.SemaphoreType.DMA((rows,)),
            ],
            compiler_params=pltpu.CompilerParams(vmem_limit_bytes=8 * rows * tile * width + spare),
            cost_estimate=pl.CostEstimate(
                flops=flops, bytes_accessed=a_bytes + p_bytes, transcendentals=0
            ),
            name="edge_part",
        )(a_cols, a_count, pair, pltpu.with_memory_space_constraint(a_tiles, pltpu.HBM), *own)

        *parts, pool = pl.pallas_call(
            functools.partial(group_kernel, subs, half),
            out_shape=[
                jax.ShapeDtypeStruct((COARSE_ROWS, span), F32 if k == 0 else BF16)
                for k in range(subs)
            ]
            + [jax.ShapeDtypeStruct((group_tiles + 1, tile, 2 * tile), BF16)],
            in_specs=[smem, smem, smem] + [vmem] * (2 * subs + 2),
            out_specs=[vmem] * (subs + 1),
            scratch_shapes=[
                pltpu.VMEM((rows * tile, width), BF16),
                pltpu.VMEM((width, width), F32),
            ],
            compiler_params=pltpu.CompilerParams(
                vmem_limit_bytes=2 * rows * tile * width + 4 * width * width + spare
            ),
            cost_estimate=pl.CostEstimate(
                flops=flops, bytes_accessed=a_bytes + subs * p_bytes, transcendentals=0
            ),
            name="group_part",
        )(a_cols, a_count, pair, a_held, edges, *flat)
        to_near, to_far = pl.pallas_call(
            functools.partial(hand_out_kernel, subs),
            out_shape=[jax.ShapeDtypeStruct(p_tiles.shape, BF16)] * 2,
            in_specs=[vmem],
            out_specs=[vmem] * 2,
            compiler_params=pltpu.CompilerParams(vmem_limit_bytes=spare),
            name="hand_out",
        )(pool)
    received = [exchange(parts[k], k) for k in range(1, subs)]
    far = lax.ppermute(
        to_far, "dom", [(d, d - 1 + 2 * (d % 2)) for d in range(1, doms - 1)]
    )
    near = lax.ppermute(to_near, "dom", [(d, d ^ 1) for d in range(doms)])
    mid, both = pl.pallas_call(
        functools.partial(sum_kernel, subs, width),
        out_shape=[
            jax.ShapeDtypeStruct((COARSE_ROWS, width), BF16),
            jax.ShapeDtypeStruct((2 * COARSE_ROWS, span - width), BF16),
        ],
        in_specs=[vmem] * subs,
        out_specs=[vmem] * 2,
        compiler_params=pltpu.CompilerParams(vmem_limit_bytes=spare),
        cost_estimate=pl.CostEstimate(
            flops=1 << 31, bytes_accessed=8 * COARSE_ROWS * span, transcendentals=0
        ),
        name="sum_parts",
    )(parts[0], *received)
    return pl.pallas_call(
        functools.partial(finish_kernel, subs, half),
        out_shape=jax.ShapeDtypeStruct((COARSE_ROWS, 3 * width), BF16),
        in_specs=[smem] + [vmem] * 4,
        out_specs=vmem,
        scratch_shapes=[pltpu.VMEM((2 * rows, tile, 2 * tile), BF16)],
        compiler_params=pltpu.CompilerParams(vmem_limit_bytes=2 * p_bytes + spare),
        cost_estimate=pl.CostEstimate(
            flops=1 << 28, bytes_accessed=4 * p_bytes, transcendentals=0
        ),
        name="finish",
    )(pair, far, near, mid, both)


def solution(mesh):
    placed = (
        P(("dom", "sub"), None, None, None),
        P(("dom", "sub"), None),
        P(("dom", "sub")),
        P(("dom", "sub"), None, None),
        P(("dom", "sub"), None),
    )
    return jax.shard_map(
        local, mesh=mesh, in_specs=placed, out_specs=P(("dom", "sub"), None), check_vma=False
    )
```

```python
import functools

import jax
import jax.numpy as jnp
from jax import lax
from jax.experimental import pallas as pl
from jax.experimental.pallas import tpu as pltpu
from jax.sharding import PartitionSpec as P

COARSE_ROWS = 64
BF16 = jnp.bfloat16
F32 = jnp.float32


def side_by_side(a_ref, f):
    return jnp.concatenate([a_ref[f, k] for k in range(a_ref.shape[1])], axis=1)


def placed_product(a_row, pool, index):
    stacked = jnp.concatenate([pool[i] for i in index], axis=0)
    return jnp.dot(a_row, stacked, preferred_element_type=F32).astype(BF16)


def own_tiles(rows, zero, half, me, pair_ref, pool):
    tiles = []
    for m in range(half):
        at = [me * rows + f for f in range(rows)]
        if half > 1:
            at = [jnp.where(pair_ref[rows + i] == m, i, zero) for i in at]
        tiles.append([pool[i] for i in at])
    return tiles


def restrict(tiles, q, half):
    outs = []
    for m in range(half):
        lhs = jnp.concatenate(tiles[m], axis=0)
        outs.append(
            lax.dot_general(lhs, q, (((0,), (0,)), ((), ())), preferred_element_type=F32)
        )
    return outs


def order_kernel(cols_hbm, p_hbm, *rest):
    outs, (cols_ref, p_ref, sems) = rest[:2], rest[2:]
    rows, tile = p_ref.shape[:2]
    piece = rows // 2
    lists = pltpu.make_async_copy(cols_hbm, cols_ref, sems.at[rows])
    lists.start()
    loads = [pltpu.make_async_copy(p_hbm.at[f], p_ref.at[f], sems.at[f]) for f in range(rows)]
    for load in loads:
        load.start()
    lists.wait()
    for f in range(rows):
        loads[f].wait()
        first = pl.multiple_of(jnp.where(cols_ref[0, f] > cols_ref[1, f], tile, 0), tile)
        for t, start in ((0, first), (1, pl.multiple_of(tile - first, tile))):
            outs[f // piece][f % piece, :, t * tile : (t + 1) * tile] = p_ref[f, :, pl.ds(start, tile)]


def hand_out_kernel(subs, pool, near_ref, far_ref):
    rows = near_ref.shape[0]
    odd = lax.rem(lax.axis_index("dom"), 2)
    last = (subs - 1) * rows
    near_ref[...] = pool[pl.ds((1 - odd) * last, rows)]
    far_ref[...] = pool[pl.ds(odd * last, rows)]


def edge_kernel(subs, half, cols_ref, count_ref, pair_ref, a_hbm, own_0, own_1, *rest):
    out_ref, a_ref, turned, sems = rest
    rows, slots, tile = a_ref.shape[:3]
    first = lax.axis_index("dom") * (subs * rows)
    me = lax.axis_index("sub")
    loads = [pltpu.make_async_copy(a_hbm.at[f], a_ref.at[f], sems.at[f]) for f in range(rows)]
    for load in loads:
        load.start()
    out_ref[...] = jnp.zeros(out_ref.shape, F32)
    for f in range(rows):
        turned[f] = (own_0, own_1)[f // (rows // 2)][f % (rows // 2)].T
    for f in range(rows):
        loads[f].wait()
        for k in range(slots):
            rel = cols_ref[f, k] - first
            live = (k < count_ref[f]) & ((rel < 0) | (rel >= subs * rows))

            @pl.when(live)
            def _():
                at = jnp.where(rel < 0, rel + rows, rel - subs * rows + rows)
                term = jnp.dot(turned[f], a_ref[f, k], preferred_element_type=F32)
                if half == 1:
                    out_ref[at] += term
                else:
                    m = pair_ref[rows + me * rows + f]
                    for start, part in ((m, term[:tile]), (m + half, term[tile:])):
                        out_ref[at, pl.ds(pl.multiple_of(start * tile, tile), tile)] += part


def terms_kernel(subs, cols_ref, count_ref, a_hbm, own_0, own_1, *rest):
    edges, (high_ref, low_ref, a_ref, total, turned, sems) = rest[:subs], rest[subs:]
    rows, slots, tile = a_ref.shape[:3]
    tiles = total.shape[0] - 1
    me = lax.axis_index("sub")
    base = lax.axis_index("dom") * (subs * rows) - rows
    loads = [pltpu.make_async_copy(a_hbm.at[f], a_ref.at[f], sems.at[f]) for f in range(rows)]
    for load in loads:
        load.start()
    total[...] = jnp.zeros(total.shape, F32)
    for f in range(rows):
        turned[f] = (own_0, own_1)[f // (rows // 2)][f % (rows // 2)].T
    for f in range(rows):
        loads[f].wait()
        for k in range(slots):
            at = jnp.where(k < count_ref[f], cols_ref[f, k] - base, tiles)
            total[at] += jnp.dot(turned[f], a_ref[f, k], preferred_element_type=F32)
    for c in range(subs * rows):
        value = total[rows + c]
        high = value.astype(BF16)
        high_ref[c] = high
        low_ref[c] = (value - high.astype(F32)).astype(BF16)
    for k in range(subs):
        start = pl.multiple_of(lax.bitwise_xor(me, k) * COARSE_ROWS, COARSE_ROWS)
        for i, c in enumerate([*range(rows), *range(tiles - rows, tiles)]):
            part = total[c, pl.ds(start, COARSE_ROWS)]
            edges[k][:, i * tile : (i + 1) * tile] = part.astype(edges[k].dtype)


def terms_product(rows, sources, high_ref, low_ref, p_refs):
    me = lax.axis_index("sub")
    both = []
    for ref in (high_ref, low_ref):
        at = [lax.bitwise_xor(me, k) * rows + f for k in sources for f in range(rows)]
        both.append(jnp.concatenate([ref[i] for i in at], axis=1))
    stacked = jnp.concatenate([ref[i] for ref in p_refs for i in range(ref.shape[0])], axis=0)
    out = jnp.dot(jnp.concatenate(both, axis=0), stacked, preferred_element_type=F32)
    height = high_ref.shape[1]
    return out[:height] + out[height:]


def early_kernel(rows, sources, high_ref, low_ref, *rest):
    rest[-1][...] = terms_product(rows, sources, high_ref, low_ref, rest[:-1])


def late_kernel(subs, rows, sources, high_ref, low_ref, early_ref, *rest):
    p_refs, rest = rest[: 2 * len(sources)], rest[2 * len(sources) :]
    edges, outs, mid = rest[:subs], rest[subs:-1], rest[-1]
    width = mid.shape[1]
    mid[...] = early_ref[...] + terms_product(rows, sources, high_ref, low_ref, p_refs)
    me = lax.axis_index("sub")
    for k in range(subs):
        start = pl.multiple_of(lax.bitwise_xor(me, k) * COARSE_ROWS, COARSE_ROWS)
        outs[k][:, :width] = mid[pl.ds(start, COARSE_ROWS)].astype(outs[k].dtype)
        outs[k][:, width:] = edges[k][...]


def hand_out_pieces_kernel(subs, *refs):
    p_refs, (near_ref, far_ref, ends) = refs[: 2 * subs], refs[2 * subs :]
    rows, piece = near_ref.shape[0], p_refs[0].shape[0]
    me, odd = lax.axis_index("sub"), lax.rem(lax.axis_index("dom"), 2)
    for k in range(subs):
        for at, who in ((0, 0), (rows, subs - 1)):

            @pl.when(me == who ^ k)
            def _():
                for i in range(2):
                    ends[at + i * piece : at + (i + 1) * piece] = p_refs[2 * k + i][...]

    near_ref[...] = ends[pl.ds((1 - odd) * rows, rows)]
    far_ref[...] = ends[pl.ds(odd * rows, rows)]


def group_kernel(subs, half, cols_ref, count_ref, pair_ref, a_ref, edge_ref, *rest):
    p_refs, rest = rest[: 2 * subs], rest[2 * subs :]
    outs, (pool, q, mid_ref) = rest[:subs], rest[subs:]
    rows, slots, tile = a_ref.shape[0], a_ref.shape[1], a_ref.shape[2]
    zero = subs * rows
    width = 2 * half * tile
    me = lax.axis_index("sub")
    first = lax.axis_index("dom") * (subs * rows)
    piece = rows // 2
    for k in range(subs):
        for i in range(2):
            pool[pl.ds(lax.bitwise_xor(me, k) * rows + i * piece, piece)] = p_refs[2 * k + i][...]
    pool[zero] = jnp.zeros(pool.shape[1:], pool.dtype)
    for f in range(rows):
        a_row = side_by_side(a_ref, f)
        index = [[None] * slots for _ in range(half)]
        for k in range(slots):
            rel = cols_ref[f, k] - first
            inside = (rel >= 0) & (rel < zero) & (k < count_ref[f])
            safe = jnp.where(inside, rel, 0)
            for m in range(half):
                here = inside if half == 1 else inside & (pair_ref[rows + safe] == m)
                index[m][k] = jnp.where(here, safe, zero)
        for m in range(half):
            block = placed_product(a_row, pool, index[m])
            lo, hi = m * tile, (m + half) * tile
            q[f * tile : (f + 1) * tile, lo : lo + tile] = block[:, :tile]
            q[f * tile : (f + 1) * tile, hi : hi + tile] = block[:, tile:]
    for m, out in enumerate(restrict(own_tiles(rows, zero, half, me, pair_ref, pool), q[...], half)):
        mid_ref[m * tile : (m + 1) * tile] = out[:tile]
        mid_ref[(m + half) * tile : (m + half + 1) * tile] = out[tile:]
    for k in range(subs):
        at = pl.ds(pl.multiple_of(lax.bitwise_xor(me, k) * COARSE_ROWS, COARSE_ROWS), COARSE_ROWS)
        kind = outs[k].dtype
        outs[k][:, :width] = mid_ref[at].astype(kind)
        for c in range(2 * rows):
            outs[k][:, width + c * tile : width + (c + 1) * tile] = edge_ref[c, at].astype(kind)


def halo_product(subs, half, side, pair_ref, terms, p_ref):
    rows, tile = p_ref.shape[:2]
    if half == 1:
        stacked = jnp.concatenate([p_ref[t] for t in range(rows)], axis=0)
        out = jnp.dot(terms, stacked, preferred_element_type=F32)
        out = out[:COARSE_ROWS] + out[COARSE_ROWS:]
        return [out[:, :tile], out[:, tile:]]
    blocks = [jnp.zeros((COARSE_ROWS, tile), F32) for _ in range(2 * half)]
    for t in range(rows):
        lhs = terms[:, t * tile : (t + 1) * tile]
        out = jnp.dot(lhs, p_ref[t], preferred_element_type=F32)
        out = out[:COARSE_ROWS] + out[COARSE_ROWS:]
        m_here = pair_ref[side * (subs + 1) * rows + t]
        for m in range(half):
            blocks[m] = blocks[m] + jnp.where(m_here == m, out[:, :tile], 0.0)
            blocks[m + half] = blocks[m + half] + jnp.where(m_here == m, out[:, tile:], 0.0)
    return blocks


def sum_kernel(*refs):
    total = refs[0][...]
    for ref in refs[1:-1]:
        total = total + ref[...].astype(F32)
    refs[-1][...] = total


def near_kernel(subs, half, pair_ref, near_ref, sum_ref, last_ref, *rest):
    mid_ref, side_ref, terms_ref, total = rest
    rows, tile = near_ref.shape[:2]
    width, span = 2 * half * tile, rows * tile
    odd = lax.rem(lax.axis_index("dom"), 2)
    total[...] = sum_ref[...] + last_ref[...].astype(F32)
    mid_ref[...] = total[:, :width].astype(BF16)

    def terms(side):
        value = total[:, pl.ds(pl.multiple_of(width + side * span, tile), span)]
        high = value.astype(BF16)
        return jnp.concatenate([high, (value - high.astype(F32)).astype(BF16)], axis=0)

    terms_ref[...] = terms(odd)
    blocks = halo_product(subs, half, 1 - odd, pair_ref, terms(1 - odd), near_ref)
    for b in range(2 * half):
        side_ref[:, b * tile : (b + 1) * tile] = blocks[b].astype(BF16)


def finish_kernel(subs, half, pair_ref, far_ref, terms_ref, mid_ref, side_ref, out_ref):
    tile = far_ref.shape[1]
    width = 2 * half * tile
    odd = lax.rem(lax.axis_index("dom"), 2)
    out_ref[:, width : 2 * width] = mid_ref[...]
    out_ref[:, pl.ds(pl.multiple_of((1 - odd) * 2 * width, tile), width)] = side_ref[...]
    blocks = halo_product(subs, half, odd, pair_ref, terms_ref[...], far_ref)
    for b in range(2 * half):
        at = pl.multiple_of(odd * 2 * width + b * tile, tile)
        out_ref[:, pl.ds(at, tile)] = blocks[b].astype(BF16)


def narrow_parts(a_tiles, a_cols, a_count, own, tiles, span):
    rows, slots, tile = a_tiles.shape[:3]
    subs = lax.axis_size("sub")
    width = 2 * tile
    smem = pl.BlockSpec(memory_space=pltpu.SMEM)
    vmem = pl.BlockSpec(memory_space=pltpu.VMEM)
    kinds = [F32] + [BF16] * (subs - 1)
    spare = 3 << 20
    products = 2 * width * rows * tile * width
    *edges, high, low = pl.pallas_call(
        functools.partial(terms_kernel, subs),
        out_shape=[jax.ShapeDtypeStruct((COARSE_ROWS, span - width), kind) for kind in kinds]
        + [jax.ShapeDtypeStruct((subs * rows, width, tile), BF16)] * 2,
        in_specs=[smem, smem, pl.BlockSpec(memory_space=pltpu.HBM), vmem, vmem],
        out_specs=[vmem] * (subs + 2),
        scratch_shapes=[
            pltpu.VMEM(a_tiles.shape, BF16),
            pltpu.VMEM(((subs + 2) * rows + 1, width, tile), F32),
            pltpu.VMEM((rows, width, tile), BF16),
            pltpu.SemaphoreType.DMA((rows,)),
        ],
        compiler_params=pltpu.CompilerParams(
            vmem_limit_bytes=2 * a_tiles.size + 4 * ((subs + 2) * rows + 1) * width * tile + spare
        ),
        cost_estimate=pl.CostEstimate(
            flops=1 << 31, bytes_accessed=2 * a_tiles.size, transcendentals=0
        ),
        name="terms",
    )(a_cols, a_count, pltpu.with_memory_space_constraint(a_tiles, pltpu.HBM), *own)
    first, last = list(range(subs - 1)), [subs - 1]
    early = pl.pallas_call(
        functools.partial(early_kernel, rows, first),
        out_shape=jax.ShapeDtypeStruct((width, width), F32),
        in_specs=[vmem] * (2 + 2 * len(first)),
        out_specs=vmem,
        compiler_params=pltpu.CompilerParams(vmem_limit_bytes=spare),
        cost_estimate=pl.CostEstimate(
            flops=2 * len(first) * products, bytes_accessed=1 << 20, transcendentals=0
        ),
        name="early_part",
    )(high, low, *[piece for k in first for piece in tiles[k]])
    return pl.pallas_call(
        functools.partial(late_kernel, subs, rows, last),
        out_shape=[jax.ShapeDtypeStruct((COARSE_ROWS, span), kind) for kind in kinds],
        in_specs=[vmem] * (3 + 2 * len(last) + subs),
        out_specs=[vmem] * subs,
        scratch_shapes=[pltpu.VMEM((width, width), F32)],
        compiler_params=pltpu.CompilerParams(vmem_limit_bytes=spare),
        cost_estimate=pl.CostEstimate(
            flops=2 * products, bytes_accessed=1 << 20, transcendentals=0
        ),
        name="late_part",
    )(high, low, early, *tiles[-1], *edges)


def local(a_tiles, a_cols, a_count, p_tiles, p_cols):
    rows, slots, tile = a_tiles.shape[:3]
    subs, doms = lax.axis_size("sub"), lax.axis_size("dom")
    coarse_group = subs * COARSE_ROWS // tile
    half = coarse_group // 2
    width = coarse_group * tile
    group_tiles = rows * subs

    smem = pl.BlockSpec(memory_space=pltpu.SMEM)
    vmem = pl.BlockSpec(memory_space=pltpu.VMEM)
    p_bytes = rows * tile * 2 * tile * 2
    a_bytes = a_tiles.size * 2
    spare = 3 << 20

    def exchange(value, k):
        return lax.ppermute(value, "sub", [(s, s ^ k) for s in range(subs)])

    own = pl.pallas_call(
        order_kernel,
        out_shape=[jax.ShapeDtypeStruct((rows // 2, tile, 2 * tile), BF16)] * 2,
        in_specs=[pl.BlockSpec(memory_space=pltpu.HBM)] * 2,
        out_specs=[vmem] * 2,
        scratch_shapes=[
            pltpu.SMEM((2, rows), jnp.int32),
            pltpu.VMEM(p_tiles.shape, BF16),
            pltpu.SemaphoreType.DMA((rows + 1,)),
        ],
        compiler_params=pltpu.CompilerParams(vmem_limit_bytes=spare),
        cost_estimate=pl.CostEstimate(
            flops=1 << 30, bytes_accessed=2 * p_bytes, transcendentals=0
        ),
        name="order_columns",
    )(
        pltpu.with_memory_space_constraint(p_cols.T, pltpu.HBM),
        pltpu.with_memory_space_constraint(p_tiles, pltpu.HBM),
    )

    tiles = [list(own)] + [[None, None] for _ in range(subs - 1)]
    for k in range(1, subs):
        low, high = k & -k, 1 << (k.bit_length() - 1)
        tiles[k][0] = exchange(tiles[k ^ low][0], low)
        tiles[k][1] = exchange(tiles[k ^ high][1], high)
    span = width + 2 * rows * tile
    if half == 1:
        pair = jnp.zeros((1,), jnp.int32)
    else:
        m_own = jnp.min(p_cols, axis=1) - lax.axis_index("dom") * coarse_group
        m_group = lax.all_gather(m_own, "sub", axis=0, tiled=True)
        m_left = lax.ppermute(
            m_group[group_tiles - rows :], "dom", [(d, d + 1) for d in range(doms - 1)]
        )
        m_right = lax.ppermute(m_group[:rows], "dom", [(d + 1, d) for d in range(doms - 1)])
        pair = jnp.concatenate([m_left, m_group, m_right])

    flat = [piece for pieces in tiles for piece in pieces]
    if half == 1:
        parts = narrow_parts(a_tiles, a_cols, a_count, own, tiles, span)
        to_near, to_far = pl.pallas_call(
            functools.partial(hand_out_pieces_kernel, subs),
            out_shape=[jax.ShapeDtypeStruct(p_tiles.shape, BF16)] * 2,
            in_specs=[vmem] * (2 * subs),
            out_specs=[vmem] * 2,
            scratch_shapes=[pltpu.VMEM((2 * rows, tile, 2 * tile), BF16)],
            compiler_params=pltpu.CompilerParams(vmem_limit_bytes=spare),
            name="hand_out",
        )(*flat)
    else:
        flops = 2 * rows * slots * tile * tile * 2 * tile * half
        edges, a_held = pl.pallas_call(
            functools.partial(edge_kernel, subs, half),
            out_shape=[
                jax.ShapeDtypeStruct((2 * rows, width, tile), F32),
                jax.ShapeDtypeStruct(a_tiles.shape, BF16),
            ],
            in_specs=[smem, smem, smem, pl.BlockSpec(memory_space=pltpu.HBM), vmem, vmem],
            out_specs=[vmem] * 2,
            scratch_shapes=[
                pltpu.VMEM((rows, 2 * tile, tile), BF16),
                pltpu.SemaphoreType.DMA((rows,)),
            ],
            compiler_params=pltpu.CompilerParams(vmem_limit_bytes=8 * rows * tile * width + spare),
            cost_estimate=pl.CostEstimate(
                flops=flops, bytes_accessed=a_bytes + p_bytes, transcendentals=0
            ),
            name="edge_part",
        )(a_cols, a_count, pair, pltpu.with_memory_space_constraint(a_tiles, pltpu.HBM), *own)

        *parts, pool = pl.pallas_call(
            functools.partial(group_kernel, subs, half),
            out_shape=[
                jax.ShapeDtypeStruct((COARSE_ROWS, span), F32 if k == 0 else BF16)
                for k in range(subs)
            ]
            + [jax.ShapeDtypeStruct((group_tiles + 1, tile, 2 * tile), BF16)],
            in_specs=[smem, smem, smem] + [vmem] * (2 * subs + 2),
            out_specs=[vmem] * (subs + 1),
            scratch_shapes=[
                pltpu.VMEM((rows * tile, width), BF16),
                pltpu.VMEM((width, width), F32),
            ],
            compiler_params=pltpu.CompilerParams(
                vmem_limit_bytes=2 * rows * tile * width + 4 * width * width + spare
            ),
            cost_estimate=pl.CostEstimate(
                flops=flops, bytes_accessed=a_bytes + subs * p_bytes, transcendentals=0
            ),
            name="group_part",
        )(a_cols, a_count, pair, a_held, edges, *flat)
        to_near, to_far = pl.pallas_call(
            functools.partial(hand_out_kernel, subs),
            out_shape=[jax.ShapeDtypeStruct(p_tiles.shape, BF16)] * 2,
            in_specs=[vmem],
            out_specs=[vmem] * 2,
            compiler_params=pltpu.CompilerParams(vmem_limit_bytes=spare),
            name="hand_out",
        )(pool)
    received = [exchange(parts[k], k) for k in [*range(subs - 1, subs // 2, -1), *range(1, subs // 2), subs // 2]]
    far = lax.ppermute(
        to_far, "dom", [(d, d - 1 + 2 * (d % 2)) for d in range(1, doms - 1)]
    )
    near = lax.ppermute(to_near, "dom", [(d, d ^ 1) for d in range(doms)])
    sums = pl.pallas_call(
        sum_kernel,
        out_shape=jax.ShapeDtypeStruct((COARSE_ROWS, span), F32),
        in_specs=[vmem] * (subs - 1),
        out_specs=vmem,
        compiler_params=pltpu.CompilerParams(vmem_limit_bytes=spare),
        cost_estimate=pl.CostEstimate(flops=3 << 29, bytes_accessed=1 << 20, transcendentals=0),
        name="sum_parts",
    )(parts[0], *received[:-1])
    mid, side, terms = pl.pallas_call(
        functools.partial(near_kernel, subs, half),
        out_shape=[
            jax.ShapeDtypeStruct((COARSE_ROWS, width), BF16),
            jax.ShapeDtypeStruct((COARSE_ROWS, width), BF16),
            jax.ShapeDtypeStruct((2 * COARSE_ROWS, rows * tile), BF16),
        ],
        in_specs=[smem] + [vmem] * 3,
        out_specs=[vmem] * 3,
        scratch_shapes=[pltpu.VMEM((COARSE_ROWS, span), F32)],
        compiler_params=pltpu.CompilerParams(vmem_limit_bytes=2 * p_bytes + spare),
        cost_estimate=pl.CostEstimate(flops=1 << 20, bytes_accessed=1 << 20, transcendentals=0),
        name="near_part",
    )(pair, near, sums, received[-1])
    return pl.pallas_call(
        functools.partial(finish_kernel, subs, half),
        out_shape=jax.ShapeDtypeStruct((COARSE_ROWS, 3 * width), BF16),
        in_specs=[smem] + [vmem] * 4,
        out_specs=vmem,
        compiler_params=pltpu.CompilerParams(vmem_limit_bytes=2 * p_bytes + spare),
        cost_estimate=pl.CostEstimate(flops=1 << 20, bytes_accessed=1 << 20, transcendentals=0),
        name="far_part",
    )(pair, far, terms, mid, side)


def solution(mesh):
    placed = (
        P(("dom", "sub"), None, None, None),
        P(("dom", "sub"), None),
        P(("dom", "sub")),
        P(("dom", "sub"), None, None),
        P(("dom", "sub"), None),
    )
    return jax.shard_map(
        local, mesh=mesh, in_specs=placed, out_specs=P(("dom", "sub"), None), check_vma=False
    )
```

```python
import functools

import jax
import jax.numpy as jnp
from jax import lax
from jax.experimental import pallas as pl
from jax.experimental.pallas import tpu as pltpu
from jax.sharding import PartitionSpec as P

COARSE_ROWS = 64
BF16 = jnp.bfloat16
F32 = jnp.float32


def side_by_side(a_ref, f):
    return jnp.concatenate([a_ref[f, k] for k in range(a_ref.shape[1])], axis=1)


def placed_product(a_row, pool, index):
    stacked = jnp.concatenate([pool[i] for i in index], axis=0)
    return jnp.dot(a_row, stacked, preferred_element_type=F32).astype(BF16)


def own_tiles(rows, zero, half, me, pair_ref, pool):
    tiles = []
    for m in range(half):
        at = [me * rows + f for f in range(rows)]
        if half > 1:
            at = [jnp.where(pair_ref[rows + i] == m, i, zero) for i in at]
        tiles.append([pool[i] for i in at])
    return tiles


def restrict(tiles, q, half):
    outs = []
    for m in range(half):
        lhs = jnp.concatenate(tiles[m], axis=0)
        outs.append(
            lax.dot_general(lhs, q, (((0,), (0,)), ((), ())), preferred_element_type=F32)
        )
    return outs


def order_kernel(cols_hbm, p_hbm, *rest):
    outs, (cols_ref, p_ref, sems) = rest[:2], rest[2:]
    rows, tile = p_ref.shape[:2]
    piece = rows // 2
    lists = pltpu.make_async_copy(cols_hbm, cols_ref, sems.at[rows])
    lists.start()
    loads = [pltpu.make_async_copy(p_hbm.at[f], p_ref.at[f], sems.at[f]) for f in range(rows)]
    for load in loads:
        load.start()
    lists.wait()
    for f in range(rows):
        loads[f].wait()
        first = pl.multiple_of(jnp.where(cols_ref[0, f] > cols_ref[1, f], tile, 0), tile)
        for t, start in ((0, first), (1, pl.multiple_of(tile - first, tile))):
            outs[f // piece][f % piece, :, t * tile : (t + 1) * tile] = p_ref[f, :, pl.ds(start, tile)]


def hand_out_kernel(subs, pool, near_ref, far_ref):
    rows = near_ref.shape[0]
    odd = lax.rem(lax.axis_index("dom"), 2)
    last = (subs - 1) * rows
    near_ref[...] = pool[pl.ds((1 - odd) * last, rows)]
    far_ref[...] = pool[pl.ds(odd * last, rows)]


def edge_kernel(subs, half, cols_ref, count_ref, pair_ref, a_hbm, own_0, own_1, *rest):
    out_ref, a_ref, turned, sems = rest
    rows, slots, tile = a_ref.shape[:3]
    first = lax.axis_index("dom") * (subs * rows)
    me = lax.axis_index("sub")
    loads = [pltpu.make_async_copy(a_hbm.at[f], a_ref.at[f], sems.at[f]) for f in range(rows)]
    for load in loads:
        load.start()
    out_ref[...] = jnp.zeros(out_ref.shape, F32)
    for f in range(rows):
        turned[f] = (own_0, own_1)[f // (rows // 2)][f % (rows // 2)].T
    for f in range(rows):
        loads[f].wait()
        for k in range(slots):
            rel = cols_ref[f, k] - first
            live = (k < count_ref[f]) & ((rel < 0) | (rel >= subs * rows))

            @pl.when(live)
            def _():
                at = jnp.where(rel < 0, rel + rows, rel - subs * rows + rows)
                term = jnp.dot(turned[f], a_ref[f, k], preferred_element_type=F32)
                if half == 1:
                    out_ref[at] += term
                else:
                    m = pair_ref[rows + me * rows + f]
                    for start, part in ((m, term[:tile]), (m + half, term[tile:])):
                        out_ref[at, pl.ds(pl.multiple_of(start * tile, tile), tile)] += part


def terms_kernel(subs, cols_ref, count_ref, a_hbm, own_0, own_1, *rest):
    edges, (high_ref, low_ref, a_ref, total, turned, sems) = rest[:subs], rest[subs:]
    rows, slots, tile = a_ref.shape[:3]
    tiles = total.shape[0] - 1
    me = lax.axis_index("sub")
    base = lax.axis_index("dom") * (subs * rows) - rows
    loads = [pltpu.make_async_copy(a_hbm.at[f], a_ref.at[f], sems.at[f]) for f in range(rows)]
    for load in loads:
        load.start()
    total[...] = jnp.zeros(total.shape, F32)
    for f in range(rows):
        turned[f] = (own_0, own_1)[f // (rows // 2)][f % (rows // 2)].T
    for f in range(rows):
        loads[f].wait()
        for k in range(slots):
            at = jnp.where(k < count_ref[f], cols_ref[f, k] - base, tiles)
            total[at] += jnp.dot(turned[f], a_ref[f, k], preferred_element_type=F32)
    for c in range(subs * rows):
        value = total[rows + c]
        high = value.astype(BF16)
        high_ref[c] = high
        low_ref[c] = (value - high.astype(F32)).astype(BF16)
    for k in range(subs):
        start = pl.multiple_of(lax.bitwise_xor(me, k) * COARSE_ROWS, COARSE_ROWS)
        for i, c in enumerate([*range(rows), *range(tiles - rows, tiles)]):
            part = total[c, pl.ds(start, COARSE_ROWS)]
            edges[k][:, i * tile : (i + 1) * tile] = part.astype(edges[k].dtype)


def terms_product(rows, sources, high_ref, low_ref, p_refs):
    me = lax.axis_index("sub")
    both = []
    for ref in (high_ref, low_ref):
        at = [lax.bitwise_xor(me, k) * rows + f for k in sources for f in range(rows)]
        both.append(jnp.concatenate([ref[i] for i in at], axis=1))
    stacked = jnp.concatenate([ref[i] for ref in p_refs for i in range(ref.shape[0])], axis=0)
    out = jnp.dot(jnp.concatenate(both, axis=0), stacked, preferred_element_type=F32)
    height = high_ref.shape[1]
    return out[:height] + out[height:]


def early_kernel(rows, sources, high_ref, low_ref, *rest):
    rest[-1][...] = terms_product(rows, sources, high_ref, low_ref, rest[:-1])


def late_kernel(subs, rows, sources, high_ref, low_ref, early_ref, *rest):
    p_refs, rest = rest[: 2 * len(sources)], rest[2 * len(sources) :]
    edges, outs, mid = rest[:subs], rest[subs:-1], rest[-1]
    width = mid.shape[1]
    mid[...] = early_ref[...] + terms_product(rows, sources, high_ref, low_ref, p_refs)
    me = lax.axis_index("sub")
    for k in range(subs):
        start = pl.multiple_of(lax.bitwise_xor(me, k) * COARSE_ROWS, COARSE_ROWS)
        outs[k][:, :width] = mid[pl.ds(start, COARSE_ROWS)].astype(outs[k].dtype)
        outs[k][:, width:] = edges[k][...]


def hand_out_pieces_kernel(subs, *refs):
    p_refs, (near_ref, far_ref, ends) = refs[: 2 * subs], refs[2 * subs :]
    rows, piece = near_ref.shape[0], p_refs[0].shape[0]
    me, odd = lax.axis_index("sub"), lax.rem(lax.axis_index("dom"), 2)
    for k in range(subs):
        for at, who in ((0, 0), (rows, subs - 1)):

            @pl.when(me == who ^ k)
            def _():
                for i in range(2):
                    ends[at + i * piece : at + (i + 1) * piece] = p_refs[2 * k + i][...]

    near_ref[...] = ends[pl.ds((1 - odd) * rows, rows)]
    far_ref[...] = ends[pl.ds(odd * rows, rows)]


def group_kernel(subs, half, cols_ref, count_ref, pair_ref, a_ref, edge_ref, *rest):
    p_refs, rest = rest[: 2 * subs], rest[2 * subs :]
    outs, (pool, q, mid_ref) = rest[:subs], rest[subs:]
    rows, slots, tile = a_ref.shape[0], a_ref.shape[1], a_ref.shape[2]
    zero = subs * rows
    width = 2 * half * tile
    me = lax.axis_index("sub")
    first = lax.axis_index("dom") * (subs * rows)
    piece = rows // 2
    for k in range(subs):
        for i in range(2):
            pool[pl.ds(lax.bitwise_xor(me, k) * rows + i * piece, piece)] = p_refs[2 * k + i][...]
    pool[zero] = jnp.zeros(pool.shape[1:], pool.dtype)
    for f in range(rows):
        a_row = side_by_side(a_ref, f)
        index = [[None] * slots for _ in range(half)]
        for k in range(slots):
            rel = cols_ref[f, k] - first
            inside = (rel >= 0) & (rel < zero) & (k < count_ref[f])
            safe = jnp.where(inside, rel, 0)
            for m in range(half):
                here = inside if half == 1 else inside & (pair_ref[rows + safe] == m)
                index[m][k] = jnp.where(here, safe, zero)
        for m in range(half):
            block = placed_product(a_row, pool, index[m])
            lo, hi = m * tile, (m + half) * tile
            q[f * tile : (f + 1) * tile, lo : lo + tile] = block[:, :tile]
            q[f * tile : (f + 1) * tile, hi : hi + tile] = block[:, tile:]
    for m, out in enumerate(restrict(own_tiles(rows, zero, half, me, pair_ref, pool), q[...], half)):
        mid_ref[m * tile : (m + 1) * tile] = out[:tile]
        mid_ref[(m + half) * tile : (m + half + 1) * tile] = out[tile:]
    for k in range(subs):
        at = pl.ds(pl.multiple_of(lax.bitwise_xor(me, k) * COARSE_ROWS, COARSE_ROWS), COARSE_ROWS)
        kind = outs[k].dtype
        outs[k][:, :width] = mid_ref[at].astype(kind)
        for c in range(2 * rows):
            outs[k][:, width + c * tile : width + (c + 1) * tile] = edge_ref[c, at].astype(kind)


def sum_kernel(subs, width, *refs):
    part_refs, (mid_ref, edge_ref) = refs[:subs], refs[subs:]
    total = part_refs[0][...]
    for k in range(1, subs):
        total = total + part_refs[k][...].astype(F32)
    mid_ref[...] = total[:, :width].astype(BF16)
    sums = total[:, width:]
    high = sums.astype(BF16)
    edge_ref[:COARSE_ROWS] = high
    edge_ref[COARSE_ROWS:] = (sums - high.astype(F32)).astype(BF16)


def finish_kernel(subs, half, pair_ref, far_ref, near_ref, mid_ref, both_ref, out_ref, edge):
    rows, tile = near_ref.shape[:2]
    width = 2 * half * tile
    odd = lax.rem(lax.axis_index("dom"), 2)
    edge[pl.ds((1 - odd) * rows, rows)] = near_ref[...]
    edge[pl.ds(odd * rows, rows)] = far_ref[...]
    out_ref[:, width : 2 * width] = mid_ref[...]
    both = both_ref[...]
    for side in range(2):
        blocks = [jnp.zeros((COARSE_ROWS, tile), F32) for _ in range(2 * half)]
        tiles = range(side * rows, (side + 1) * rows)
        if half == 1:
            stacked = jnp.concatenate([edge[c] for c in tiles], axis=0)
            lhs = both[:, side * rows * tile : (side + 1) * rows * tile]
            term = jnp.dot(lhs, stacked, preferred_element_type=F32)
            term = term[:COARSE_ROWS] + term[COARSE_ROWS:]
            blocks = [term[:, :tile], term[:, tile:]]
        else:
            for c in tiles:
                lhs = both[:, c * tile : (c + 1) * tile]
                term = jnp.dot(lhs, edge[c], preferred_element_type=F32)
                term = term[:COARSE_ROWS] + term[COARSE_ROWS:]
                m_here = pair_ref[c if side == 0 else subs * rows + c]
                for m in range(half):
                    here = m_here == m
                    blocks[m] = blocks[m] + jnp.where(here, term[:, :tile], 0.0)
                    blocks[m + half] = blocks[m + half] + jnp.where(here, term[:, tile:], 0.0)
        for b in range(2 * half):
            at = 2 * side * width + b * tile
            out_ref[:, at : at + tile] = blocks[b].astype(BF16)


def narrow_terms(a_tiles, a_cols, a_count, own):
    rows, slots, tile = a_tiles.shape[:3]
    subs = lax.axis_size("sub")
    width = 2 * tile
    span = width + 2 * rows * tile
    smem = pl.BlockSpec(memory_space=pltpu.SMEM)
    vmem = pl.BlockSpec(memory_space=pltpu.VMEM)
    kinds = [F32] + [BF16] * (subs - 1)
    spare = 3 << 20
    return pl.pallas_call(
        functools.partial(terms_kernel, subs),
        out_shape=[jax.ShapeDtypeStruct((COARSE_ROWS, span - width), kind) for kind in kinds]
        + [jax.ShapeDtypeStruct((subs * rows, width, tile), BF16)] * 2,
        in_specs=[smem, smem, pl.BlockSpec(memory_space=pltpu.HBM), vmem, vmem],
        out_specs=[vmem] * (subs + 2),
        scratch_shapes=[
            pltpu.VMEM(a_tiles.shape, BF16),
            pltpu.VMEM(((subs + 2) * rows + 1, width, tile), F32),
            pltpu.VMEM((rows, width, tile), BF16),
            pltpu.SemaphoreType.DMA((rows,)),
        ],
        compiler_params=pltpu.CompilerParams(
            vmem_limit_bytes=2 * a_tiles.size + 4 * ((subs + 2) * rows + 1) * width * tile + spare
        ),
        cost_estimate=pl.CostEstimate(
            flops=1 << 31, bytes_accessed=2 * a_tiles.size, transcendentals=0
        ),
        name="terms",
    )(a_cols, a_count, pltpu.with_memory_space_constraint(a_tiles, pltpu.HBM), *own)


def narrow_parts(edges, high, low, tiles):
    subs, (rows, width, tile) = len(edges), high.shape
    rows //= subs
    span = width + edges[0].shape[1]
    vmem = pl.BlockSpec(memory_space=pltpu.VMEM)
    kinds = [F32] + [BF16] * (subs - 1)
    spare = 3 << 20
    products = 2 * width * rows * tile * width
    first, last = list(range(subs - 1)), [subs - 1]
    early = pl.pallas_call(
        functools.partial(early_kernel, rows, first),
        out_shape=jax.ShapeDtypeStruct((width, width), F32),
        in_specs=[vmem] * (2 + 2 * len(first)),
        out_specs=vmem,
        compiler_params=pltpu.CompilerParams(vmem_limit_bytes=spare),
        cost_estimate=pl.CostEstimate(
            flops=2 * len(first) * products, bytes_accessed=1 << 20, transcendentals=0
        ),
        name="early_part",
    )(high, low, *[piece for k in first for piece in tiles[k]])
    return pl.pallas_call(
        functools.partial(late_kernel, subs, rows, last),
        out_shape=[jax.ShapeDtypeStruct((COARSE_ROWS, span), kind) for kind in kinds],
        in_specs=[vmem] * (3 + 2 * len(last) + subs),
        out_specs=[vmem] * subs,
        scratch_shapes=[pltpu.VMEM((width, width), F32)],
        compiler_params=pltpu.CompilerParams(vmem_limit_bytes=spare),
        cost_estimate=pl.CostEstimate(
            flops=2 * products, bytes_accessed=1 << 20, transcendentals=0
        ),
        name="late_part",
    )(high, low, early, *tiles[-1], *edges)


def local(a_tiles, a_cols, a_count, p_tiles, p_cols):
    rows, slots, tile = a_tiles.shape[:3]
    subs, doms = lax.axis_size("sub"), lax.axis_size("dom")
    coarse_group = subs * COARSE_ROWS // tile
    half = coarse_group // 2
    width = coarse_group * tile
    group_tiles = rows * subs

    smem = pl.BlockSpec(memory_space=pltpu.SMEM)
    vmem = pl.BlockSpec(memory_space=pltpu.VMEM)
    p_bytes = rows * tile * 2 * tile * 2
    a_bytes = a_tiles.size * 2
    spare = 3 << 20

    def exchange(value, k):
        return lax.ppermute(value, "sub", [(s, s ^ k) for s in range(subs)])

    own = pl.pallas_call(
        order_kernel,
        out_shape=[jax.ShapeDtypeStruct((rows // 2, tile, 2 * tile), BF16)] * 2,
        in_specs=[pl.BlockSpec(memory_space=pltpu.HBM)] * 2,
        out_specs=[vmem] * 2,
        scratch_shapes=[
            pltpu.SMEM((2, rows), jnp.int32),
            pltpu.VMEM(p_tiles.shape, BF16),
            pltpu.SemaphoreType.DMA((rows + 1,)),
        ],
        compiler_params=pltpu.CompilerParams(vmem_limit_bytes=spare),
        cost_estimate=pl.CostEstimate(
            flops=1 << 30, bytes_accessed=2 * p_bytes, transcendentals=0
        ),
        name="order_columns",
    )(
        pltpu.with_memory_space_constraint(p_cols.T, pltpu.HBM),
        pltpu.with_memory_space_constraint(p_tiles, pltpu.HBM),
    )

    tiles = [list(own)] + [[None, None] for _ in range(subs - 1)]
    if half == 1:
        *edges, high, low = narrow_terms(a_tiles, a_cols, a_count, own)
    for k in range(1, subs):
        if half == 1 and k == subs - 1:
            tiles[2][0], high = lax.optimization_barrier((tiles[2][0], high))
        first, last = k & -k, 1 << (k.bit_length() - 1)
        tiles[k][0] = exchange(tiles[k ^ first][0], first)
        tiles[k][1] = exchange(tiles[k ^ last][1], last)
    span = width + 2 * rows * tile
    if half == 1:
        pair = jnp.zeros((1,), jnp.int32)
    else:
        m_own = jnp.min(p_cols, axis=1) - lax.axis_index("dom") * coarse_group
        m_group = lax.all_gather(m_own, "sub", axis=0, tiled=True)
        m_left = lax.ppermute(
            m_group[group_tiles - rows :], "dom", [(d, d + 1) for d in range(doms - 1)]
        )
        m_right = lax.ppermute(m_group[:rows], "dom", [(d + 1, d) for d in range(doms - 1)])
        pair = jnp.concatenate([m_left, m_group, m_right])

    flat = [piece for pieces in tiles for piece in pieces]
    if half == 1:
        parts = narrow_parts(edges, high, low, tiles)
        to_near, to_far = pl.pallas_call(
            functools.partial(hand_out_pieces_kernel, subs),
            out_shape=[jax.ShapeDtypeStruct(p_tiles.shape, BF16)] * 2,
            in_specs=[vmem] * (2 * subs),
            out_specs=[vmem] * 2,
            scratch_shapes=[pltpu.VMEM((2 * rows, tile, 2 * tile), BF16)],
            compiler_params=pltpu.CompilerParams(vmem_limit_bytes=spare),
            name="hand_out",
        )(*flat)
    else:
        flops = 2 * rows * slots * tile * tile * 2 * tile * half
        edges, a_held = pl.pallas_call(
            functools.partial(edge_kernel, subs, half),
            out_shape=[
                jax.ShapeDtypeStruct((2 * rows, width, tile), F32),
                jax.ShapeDtypeStruct(a_tiles.shape, BF16),
            ],
            in_specs=[smem, smem, smem, pl.BlockSpec(memory_space=pltpu.HBM), vmem, vmem],
            out_specs=[vmem] * 2,
            scratch_shapes=[
                pltpu.VMEM((rows, 2 * tile, tile), BF16),
                pltpu.SemaphoreType.DMA((rows,)),
            ],
            compiler_params=pltpu.CompilerParams(vmem_limit_bytes=8 * rows * tile * width + spare),
            cost_estimate=pl.CostEstimate(
                flops=flops, bytes_accessed=a_bytes + p_bytes, transcendentals=0
            ),
            name="edge_part",
        )(a_cols, a_count, pair, pltpu.with_memory_space_constraint(a_tiles, pltpu.HBM), *own)

        *parts, pool = pl.pallas_call(
            functools.partial(group_kernel, subs, half),
            out_shape=[
                jax.ShapeDtypeStruct((COARSE_ROWS, span), F32 if k == 0 else BF16)
                for k in range(subs)
            ]
            + [jax.ShapeDtypeStruct((group_tiles + 1, tile, 2 * tile), BF16)],
            in_specs=[smem, smem, smem] + [vmem] * (2 * subs + 2),
            out_specs=[vmem] * (subs + 1),
            scratch_shapes=[
                pltpu.VMEM((rows * tile, width), BF16),
                pltpu.VMEM((width, width), F32),
            ],
            compiler_params=pltpu.CompilerParams(
                vmem_limit_bytes=2 * rows * tile * width + 4 * width * width + spare
            ),
            cost_estimate=pl.CostEstimate(
                flops=flops, bytes_accessed=a_bytes + subs * p_bytes, transcendentals=0
            ),
            name="group_part",
        )(a_cols, a_count, pair, a_held, edges, *flat)
        to_near, to_far = pl.pallas_call(
            functools.partial(hand_out_kernel, subs),
            out_shape=[jax.ShapeDtypeStruct(p_tiles.shape, BF16)] * 2,
            in_specs=[vmem],
            out_specs=[vmem] * 2,
            compiler_params=pltpu.CompilerParams(vmem_limit_bytes=spare),
            name="hand_out",
        )(pool)
    received = [exchange(parts[k], k) for k in range(1, subs)]
    far = lax.ppermute(
        to_far, "dom", [(d, d - 1 + 2 * (d % 2)) for d in range(1, doms - 1)]
    )
    near = lax.ppermute(to_near, "dom", [(d, d ^ 1) for d in range(doms)])
    mid, both = pl.pallas_call(
        functools.partial(sum_kernel, subs, width),
        out_shape=[
            jax.ShapeDtypeStruct((COARSE_ROWS, width), BF16),
            jax.ShapeDtypeStruct((2 * COARSE_ROWS, span - width), BF16),
        ],
        in_specs=[vmem] * subs,
        out_specs=[vmem] * 2,
        compiler_params=pltpu.CompilerParams(vmem_limit_bytes=spare),
        cost_estimate=pl.CostEstimate(
            flops=1 << 31, bytes_accessed=8 * COARSE_ROWS * span, transcendentals=0
        ),
        name="sum_parts",
    )(parts[0], *received)
    return pl.pallas_call(
        functools.partial(finish_kernel, subs, half),
        out_shape=jax.ShapeDtypeStruct((COARSE_ROWS, 3 * width), BF16),
        in_specs=[smem] + [vmem] * 4,
        out_specs=vmem,
        scratch_shapes=[pltpu.VMEM((2 * rows, tile, 2 * tile), BF16)],
        compiler_params=pltpu.CompilerParams(vmem_limit_bytes=2 * p_bytes + spare),
        cost_estimate=pl.CostEstimate(
            flops=1 << 28, bytes_accessed=4 * p_bytes, transcendentals=0
        ),
        name="finish",
    )(pair, far, near, mid, both)


def solution(mesh):
    placed = (
        P(("dom", "sub"), None, None, None),
        P(("dom", "sub"), None),
        P(("dom", "sub")),
        P(("dom", "sub"), None, None),
        P(("dom", "sub"), None),
    )
    return jax.shard_map(
        local, mesh=mesh, in_specs=placed, out_specs=P(("dom", "sub"), None), check_vma=False
    )
```

```python
import functools

import jax
import jax.numpy as jnp
from jax import lax
from jax.experimental import pallas as pl
from jax.experimental.pallas import tpu as pltpu
from jax.sharding import PartitionSpec as P

COARSE_ROWS = 64
BF16 = jnp.bfloat16
F32 = jnp.float32


def side_by_side(a_ref, f):
    return jnp.concatenate([a_ref[f, k] for k in range(a_ref.shape[1])], axis=1)


def placed_product(a_row, pool, index):
    stacked = jnp.concatenate([pool[i] for i in index], axis=0)
    return jnp.dot(a_row, stacked, preferred_element_type=F32).astype(BF16)


def own_tiles(rows, zero, half, me, pair_ref, pool):
    tiles = []
    for m in range(half):
        at = [me * rows + f for f in range(rows)]
        if half > 1:
            at = [jnp.where(pair_ref[rows + i] == m, i, zero) for i in at]
        tiles.append([pool[i] for i in at])
    return tiles


def restrict(tiles, q, half):
    outs = []
    for m in range(half):
        lhs = jnp.concatenate(tiles[m], axis=0)
        outs.append(
            lax.dot_general(lhs, q, (((0,), (0,)), ((), ())), preferred_element_type=F32)
        )
    return outs


def order_kernel(cols_hbm, p_hbm, *rest):
    outs, (cols_ref, p_ref, sems) = rest[:2], rest[2:]
    rows, tile = p_ref.shape[:2]
    piece = rows // 2
    lists = pltpu.make_async_copy(cols_hbm, cols_ref, sems.at[rows])
    lists.start()
    loads = [pltpu.make_async_copy(p_hbm.at[f], p_ref.at[f], sems.at[f]) for f in range(rows)]
    for load in loads:
        load.start()
    lists.wait()
    for f in range(rows):
        loads[f].wait()
        first = pl.multiple_of(jnp.where(cols_ref[0, f] > cols_ref[1, f], tile, 0), tile)
        for t, start in ((0, first), (1, pl.multiple_of(tile - first, tile))):
            outs[f // piece][f % piece, :, t * tile : (t + 1) * tile] = p_ref[f, :, pl.ds(start, tile)]


def hand_out_kernel(subs, pool, near_ref, far_ref):
    rows = near_ref.shape[0]
    odd = lax.rem(lax.axis_index("dom"), 2)
    last = (subs - 1) * rows
    near_ref[...] = pool[pl.ds((1 - odd) * last, rows)]
    far_ref[...] = pool[pl.ds(odd * last, rows)]


def edge_kernel(subs, half, cols_ref, count_ref, pair_ref, a_hbm, own_0, own_1, *rest):
    out_ref, a_ref, turned, sems = rest
    rows, slots, tile = a_ref.shape[:3]
    first = lax.axis_index("dom") * (subs * rows)
    me = lax.axis_index("sub")
    loads = [pltpu.make_async_copy(a_hbm.at[f], a_ref.at[f], sems.at[f]) for f in range(rows)]
    for load in loads:
        load.start()
    out_ref[...] = jnp.zeros(out_ref.shape, F32)
    for f in range(rows):
        turned[f] = (own_0, own_1)[f // (rows // 2)][f % (rows // 2)].T
    for f in range(rows):
        loads[f].wait()
        for k in range(slots):
            rel = cols_ref[f, k] - first
            live = (k < count_ref[f]) & ((rel < 0) | (rel >= subs * rows))

            @pl.when(live)
            def _():
                at = jnp.where(rel < 0, rel + rows, rel - subs * rows + rows)
                term = jnp.dot(turned[f], a_ref[f, k], preferred_element_type=F32)
                if half == 1:
                    out_ref[at] += term
                else:
                    m = pair_ref[rows + me * rows + f]
                    for start, part in ((m, term[:tile]), (m + half, term[tile:])):
                        out_ref[at, pl.ds(pl.multiple_of(start * tile, tile), tile)] += part


def terms_kernel(subs, cols_ref, count_ref, a_hbm, own_0, own_1, *rest):
    edges, (high_ref, low_ref, a_ref, total, turned, sems) = rest[:subs], rest[subs:]
    rows, slots, tile = a_ref.shape[:3]
    tiles = total.shape[0] - 1
    me = lax.axis_index("sub")
    base = lax.axis_index("dom") * (subs * rows) - rows
    loads = [pltpu.make_async_copy(a_hbm.at[f], a_ref.at[f], sems.at[f]) for f in range(rows)]
    for load in loads:
        load.start()
    total[...] = jnp.zeros(total.shape, F32)
    for f in range(rows):
        turned[f] = (own_0, own_1)[f // (rows // 2)][f % (rows // 2)].T
    for f in range(rows):
        loads[f].wait()
        for k in range(slots):
            at = jnp.where(k < count_ref[f], cols_ref[f, k] - base, tiles)
            total[at] += jnp.dot(turned[f], a_ref[f, k], preferred_element_type=F32)
    for c in range(subs * rows):
        value = total[rows + c]
        high = value.astype(BF16)
        high_ref[c] = high
        low_ref[c] = (value - high.astype(F32)).astype(BF16)
    for k in range(subs):
        start = pl.multiple_of(lax.bitwise_xor(me, k) * COARSE_ROWS, COARSE_ROWS)
        for i, c in enumerate([*range(rows), *range(tiles - rows, tiles)]):
            part = total[c, pl.ds(start, COARSE_ROWS)]
            edges[k][:, i * tile : (i + 1) * tile] = part.astype(edges[k].dtype)


def terms_product(rows, sources, high_ref, low_ref, p_refs):
    me = lax.axis_index("sub")
    both = []
    for ref in (high_ref, low_ref):
        at = [lax.bitwise_xor(me, k) * rows + f for k in sources for f in range(rows)]
        both.append(jnp.concatenate([ref[i] for i in at], axis=1))
    stacked = jnp.concatenate([ref[i] for ref in p_refs for i in range(ref.shape[0])], axis=0)
    out = jnp.dot(jnp.concatenate(both, axis=0), stacked, preferred_element_type=F32)
    height = high_ref.shape[1]
    return out[:height] + out[height:]


def early_kernel(rows, sources, high_ref, low_ref, *rest):
    rest[-1][...] = terms_product(rows, sources, high_ref, low_ref, rest[:-1])


def late_kernel(subs, rows, sources, high_ref, low_ref, early_ref, *rest):
    p_refs, rest = rest[: 2 * subs], rest[2 * subs :]
    edges, outs, (near_ref, far_ref, mid, ends) = rest[:subs], rest[subs:-4], rest[-4:]
    width, piece = mid.shape[1], p_refs[0].shape[0]
    me, odd = lax.axis_index("sub"), lax.rem(lax.axis_index("dom"), 2)
    last = [p_refs[2 * k + i] for k in sources for i in range(2)]
    mid[...] = early_ref[...] + terms_product(rows, sources, high_ref, low_ref, last)
    for k in range(subs):
        start = pl.multiple_of(lax.bitwise_xor(me, k) * COARSE_ROWS, COARSE_ROWS)
        outs[k][:, :width] = mid[pl.ds(start, COARSE_ROWS)].astype(outs[k].dtype)
        outs[k][:, width:] = edges[k][...]
    for k in range(subs):
        for at, who in ((0, 0), (rows, subs - 1)):

            @pl.when(me == who ^ k)
            def _():
                for i in range(2):
                    ends[at + i * piece : at + (i + 1) * piece] = p_refs[2 * k + i][...]

    near_ref[...] = ends[pl.ds((1 - odd) * rows, rows)]
    far_ref[...] = ends[pl.ds(odd * rows, rows)]


def group_kernel(subs, half, cols_ref, count_ref, pair_ref, a_ref, edge_ref, *rest):
    p_refs, rest = rest[: 2 * subs], rest[2 * subs :]
    outs, (pool, q, mid_ref) = rest[:subs], rest[subs:]
    rows, slots, tile = a_ref.shape[0], a_ref.shape[1], a_ref.shape[2]
    zero = subs * rows
    width = 2 * half * tile
    me = lax.axis_index("sub")
    first = lax.axis_index("dom") * (subs * rows)
    piece = rows // 2
    for k in range(subs):
        for i in range(2):
            pool[pl.ds(lax.bitwise_xor(me, k) * rows + i * piece, piece)] = p_refs[2 * k + i][...]
    pool[zero] = jnp.zeros(pool.shape[1:], pool.dtype)
    for f in range(rows):
        a_row = side_by_side(a_ref, f)
        index = [[None] * slots for _ in range(half)]
        for k in range(slots):
            rel = cols_ref[f, k] - first
            inside = (rel >= 0) & (rel < zero) & (k < count_ref[f])
            safe = jnp.where(inside, rel, 0)
            for m in range(half):
                here = inside if half == 1 else inside & (pair_ref[rows + safe] == m)
                index[m][k] = jnp.where(here, safe, zero)
        for m in range(half):
            block = placed_product(a_row, pool, index[m])
            lo, hi = m * tile, (m + half) * tile
            q[f * tile : (f + 1) * tile, lo : lo + tile] = block[:, :tile]
            q[f * tile : (f + 1) * tile, hi : hi + tile] = block[:, tile:]
    for m, out in enumerate(restrict(own_tiles(rows, zero, half, me, pair_ref, pool), q[...], half)):
        mid_ref[m * tile : (m + 1) * tile] = out[:tile]
        mid_ref[(m + half) * tile : (m + half + 1) * tile] = out[tile:]
    for k in range(subs):
        at = pl.ds(pl.multiple_of(lax.bitwise_xor(me, k) * COARSE_ROWS, COARSE_ROWS), COARSE_ROWS)
        kind = outs[k].dtype
        outs[k][:, :width] = mid_ref[at].astype(kind)
        for c in range(2 * rows):
            outs[k][:, width + c * tile : width + (c + 1) * tile] = edge_ref[c, at].astype(kind)


def sum_kernel(subs, width, *refs):
    part_refs, (mid_ref, edge_ref) = refs[:subs], refs[subs:]
    total = part_refs[0][...]
    for k in range(1, subs):
        total = total + part_refs[k][...].astype(F32)
    mid_ref[...] = total[:, :width].astype(BF16)
    sums = total[:, width:]
    high = sums.astype(BF16)
    edge_ref[:COARSE_ROWS] = high
    edge_ref[COARSE_ROWS:] = (sums - high.astype(F32)).astype(BF16)


def finish_kernel(subs, half, *refs):
    pair_ref = refs[0] if half > 1 else None
    far_ref, near_ref, mid_ref, both_ref, out_ref, edge = refs[-6:]
    rows, tile = near_ref.shape[:2]
    width = 2 * half * tile
    odd = lax.rem(lax.axis_index("dom"), 2)
    edge[pl.ds((1 - odd) * rows, rows)] = near_ref[...]
    edge[pl.ds(odd * rows, rows)] = far_ref[...]
    out_ref[:, width : 2 * width] = mid_ref[...]
    both = both_ref[...]
    for side in range(2):
        blocks = [jnp.zeros((COARSE_ROWS, tile), F32) for _ in range(2 * half)]
        tiles = range(side * rows, (side + 1) * rows)
        if half == 1:
            stacked = jnp.concatenate([edge[c] for c in tiles], axis=0)
            lhs = both[:, side * rows * tile : (side + 1) * rows * tile]
            term = jnp.dot(lhs, stacked, preferred_element_type=F32)
            term = term[:COARSE_ROWS] + term[COARSE_ROWS:]
            blocks = [term[:, :tile], term[:, tile:]]
        else:
            for c in tiles:
                lhs = both[:, c * tile : (c + 1) * tile]
                term = jnp.dot(lhs, edge[c], preferred_element_type=F32)
                term = term[:COARSE_ROWS] + term[COARSE_ROWS:]
                m_here = pair_ref[c if side == 0 else subs * rows + c]
                for m in range(half):
                    here = m_here == m
                    blocks[m] = blocks[m] + jnp.where(here, term[:, :tile], 0.0)
                    blocks[m + half] = blocks[m + half] + jnp.where(here, term[:, tile:], 0.0)
        for b in range(2 * half):
            at = 2 * side * width + b * tile
            out_ref[:, at : at + tile] = blocks[b].astype(BF16)


def narrow_parts(a_tiles, a_cols, a_count, own, tiles, span):
    rows, slots, tile = a_tiles.shape[:3]
    subs = lax.axis_size("sub")
    width = 2 * tile
    smem = pl.BlockSpec(memory_space=pltpu.SMEM)
    vmem = pl.BlockSpec(memory_space=pltpu.VMEM)
    kinds = [F32] + [BF16] * (subs - 1)
    spare = 3 << 20
    products = 2 * width * rows * tile * width
    *edges, high, low = pl.pallas_call(
        functools.partial(terms_kernel, subs),
        out_shape=[jax.ShapeDtypeStruct((COARSE_ROWS, span - width), kind) for kind in kinds]
        + [jax.ShapeDtypeStruct((subs * rows, width, tile), BF16)] * 2,
        in_specs=[smem, smem, pl.BlockSpec(memory_space=pltpu.HBM), vmem, vmem],
        out_specs=[vmem] * (subs + 2),
        scratch_shapes=[
            pltpu.VMEM(a_tiles.shape, BF16),
            pltpu.VMEM(((subs + 2) * rows + 1, width, tile), F32),
            pltpu.VMEM((rows, width, tile), BF16),
            pltpu.SemaphoreType.DMA((rows,)),
        ],
        compiler_params=pltpu.CompilerParams(
            vmem_limit_bytes=2 * a_tiles.size + 4 * ((subs + 2) * rows + 1) * width * tile + spare
        ),
        cost_estimate=pl.CostEstimate(
            flops=1 << 31, bytes_accessed=2 * a_tiles.size, transcendentals=0
        ),
        name="terms",
    )(a_cols, a_count, pltpu.with_memory_space_constraint(a_tiles, pltpu.HBM), *own)
    first, last = list(range(subs - 1)), [subs - 1]
    early = pl.pallas_call(
        functools.partial(early_kernel, rows, first),
        out_shape=jax.ShapeDtypeStruct((width, width), F32),
        in_specs=[vmem] * (2 + 2 * len(first)),
        out_specs=vmem,
        compiler_params=pltpu.CompilerParams(vmem_limit_bytes=spare),
        cost_estimate=pl.CostEstimate(
            flops=2 * len(first) * products, bytes_accessed=1 << 20, transcendentals=0
        ),
        name="early_part",
    )(high, low, *[piece for k in first for piece in tiles[k]])
    return pl.pallas_call(
        functools.partial(late_kernel, subs, rows, last),
        out_shape=[jax.ShapeDtypeStruct((COARSE_ROWS, span), kind) for kind in kinds]
        + [jax.ShapeDtypeStruct((rows, tile, width), BF16)] * 2,
        in_specs=[vmem] * (3 + 3 * subs),
        out_specs=[vmem] * (subs + 2),
        scratch_shapes=[
            pltpu.VMEM((width, width), F32),
            pltpu.VMEM((2 * rows, tile, width), BF16),
        ],
        compiler_params=pltpu.CompilerParams(vmem_limit_bytes=spare),
        cost_estimate=pl.CostEstimate(
            flops=2 * products, bytes_accessed=1 << 20, transcendentals=0
        ),
        name="late_part",
    )(high, low, early, *[piece for pieces in tiles for piece in pieces], *edges)


def local(a_tiles, a_cols, a_count, p_tiles, p_cols):
    rows, slots, tile = a_tiles.shape[:3]
    subs, doms = lax.axis_size("sub"), lax.axis_size("dom")
    coarse_group = subs * COARSE_ROWS // tile
    half = coarse_group // 2
    width = coarse_group * tile
    group_tiles = rows * subs

    smem = pl.BlockSpec(memory_space=pltpu.SMEM)
    vmem = pl.BlockSpec(memory_space=pltpu.VMEM)
    p_bytes = rows * tile * 2 * tile * 2
    a_bytes = a_tiles.size * 2
    spare = 3 << 20

    def exchange(value, k):
        return lax.ppermute(value, "sub", [(s, s ^ k) for s in range(subs)])

    own = pl.pallas_call(
        order_kernel,
        out_shape=[jax.ShapeDtypeStruct((rows // 2, tile, 2 * tile), BF16)] * 2,
        in_specs=[pl.BlockSpec(memory_space=pltpu.HBM)] * 2,
        out_specs=[vmem] * 2,
        scratch_shapes=[
            pltpu.SMEM((2, rows), jnp.int32),
            pltpu.VMEM(p_tiles.shape, BF16),
            pltpu.SemaphoreType.DMA((rows + 1,)),
        ],
        compiler_params=pltpu.CompilerParams(vmem_limit_bytes=spare),
        cost_estimate=pl.CostEstimate(
            flops=1 << 30, bytes_accessed=2 * p_bytes, transcendentals=0
        ),
        name="order_columns",
    )(
        pltpu.with_memory_space_constraint(p_cols.T, pltpu.HBM),
        pltpu.with_memory_space_constraint(p_tiles, pltpu.HBM),
    )

    tiles = [list(own)] + [[None, None] for _ in range(subs - 1)]
    for k in range(1, subs):
        low, high = k & -k, 1 << (k.bit_length() - 1)
        tiles[k][0] = exchange(tiles[k ^ low][0], low)
        tiles[k][1] = exchange(tiles[k ^ high][1], high)
    span = width + 2 * rows * tile
    pairs = []
    if half > 1:
        m_own = jnp.min(p_cols, axis=1) - lax.axis_index("dom") * coarse_group
        m_group = lax.all_gather(m_own, "sub", axis=0, tiled=True)
        m_left = lax.ppermute(
            m_group[group_tiles - rows :], "dom", [(d, d + 1) for d in range(doms - 1)]
        )
        m_right = lax.ppermute(m_group[:rows], "dom", [(d + 1, d) for d in range(doms - 1)])
        pair = jnp.concatenate([m_left, m_group, m_right])
        pairs = [pair]

    flat = [piece for pieces in tiles for piece in pieces]
    if half == 1:
        *parts, to_near, to_far = narrow_parts(a_tiles, a_cols, a_count, own, tiles, span)
    else:
        flops = 2 * rows * slots * tile * tile * 2 * tile * half
        edges, a_held = pl.pallas_call(
            functools.partial(edge_kernel, subs, half),
            out_shape=[
                jax.ShapeDtypeStruct((2 * rows, width, tile), F32),
                jax.ShapeDtypeStruct(a_tiles.shape, BF16),
            ],
            in_specs=[smem, smem, smem, pl.BlockSpec(memory_space=pltpu.HBM), vmem, vmem],
            out_specs=[vmem] * 2,
            scratch_shapes=[
                pltpu.VMEM((rows, 2 * tile, tile), BF16),
                pltpu.SemaphoreType.DMA((rows,)),
            ],
            compiler_params=pltpu.CompilerParams(vmem_limit_bytes=8 * rows * tile * width + spare),
            cost_estimate=pl.CostEstimate(
                flops=flops, bytes_accessed=a_bytes + p_bytes, transcendentals=0
            ),
            name="edge_part",
        )(a_cols, a_count, pair, pltpu.with_memory_space_constraint(a_tiles, pltpu.HBM), *own)

        *parts, pool = pl.pallas_call(
            functools.partial(group_kernel, subs, half),
            out_shape=[
                jax.ShapeDtypeStruct((COARSE_ROWS, span), F32 if k == 0 else BF16)
                for k in range(subs)
            ]
            + [jax.ShapeDtypeStruct((group_tiles + 1, tile, 2 * tile), BF16)],
            in_specs=[smem, smem, smem] + [vmem] * (2 * subs + 2),
            out_specs=[vmem] * (subs + 1),
            scratch_shapes=[
                pltpu.VMEM((rows * tile, width), BF16),
                pltpu.VMEM((width, width), F32),
            ],
            compiler_params=pltpu.CompilerParams(
                vmem_limit_bytes=2 * rows * tile * width + 4 * width * width + spare
            ),
            cost_estimate=pl.CostEstimate(
                flops=flops, bytes_accessed=a_bytes + subs * p_bytes, transcendentals=0
            ),
            name="group_part",
        )(a_cols, a_count, pair, a_held, edges, *flat)
        to_near, to_far = pl.pallas_call(
            functools.partial(hand_out_kernel, subs),
            out_shape=[jax.ShapeDtypeStruct(p_tiles.shape, BF16)] * 2,
            in_specs=[vmem],
            out_specs=[vmem] * 2,
            compiler_params=pltpu.CompilerParams(vmem_limit_bytes=spare),
            name="hand_out",
        )(pool)
    received = [exchange(parts[k], k) for k in range(subs - 1, 0, -1)]
    far = lax.ppermute(
        to_far, "dom", [(d, d - 1 + 2 * (d % 2)) for d in range(1, doms - 1)]
    )
    near = lax.ppermute(to_near, "dom", [(d, d ^ 1) for d in range(doms)])
    mid, both = pl.pallas_call(
        functools.partial(sum_kernel, subs, width),
        out_shape=[
            jax.ShapeDtypeStruct((COARSE_ROWS, width), BF16),
            jax.ShapeDtypeStruct((2 * COARSE_ROWS, span - width), BF16),
        ],
        in_specs=[vmem] * subs,
        out_specs=[vmem] * 2,
        compiler_params=pltpu.CompilerParams(vmem_limit_bytes=spare),
        cost_estimate=pl.CostEstimate(
            flops=1 << 31, bytes_accessed=8 * COARSE_ROWS * span, transcendentals=0
        ),
        name="sum_parts",
    )(parts[0], *received)
    return pl.pallas_call(
        functools.partial(finish_kernel, subs, half),
        out_shape=jax.ShapeDtypeStruct((COARSE_ROWS, 3 * width), BF16),
        in_specs=[smem] * len(pairs) + [vmem] * 4,
        out_specs=vmem,
        scratch_shapes=[pltpu.VMEM((2 * rows, tile, 2 * tile), BF16)],
        compiler_params=pltpu.CompilerParams(vmem_limit_bytes=2 * p_bytes + spare),
        cost_estimate=pl.CostEstimate(
            flops=1 << 28, bytes_accessed=4 * p_bytes, transcendentals=0
        ),
        name="finish",
    )(*pairs, far, near, mid, both)


def solution(mesh):
    placed = (
        P(("dom", "sub"), None, None, None),
        P(("dom", "sub"), None),
        P(("dom", "sub")),
        P(("dom", "sub"), None, None),
        P(("dom", "sub"), None),
    )
    return jax.shard_map(
        local, mesh=mesh, in_specs=placed, out_specs=P(("dom", "sub"), None), check_vma=False
    )
```

```python
import functools

import jax
import jax.numpy as jnp
from jax import lax
from jax.experimental import pallas as pl
from jax.experimental.pallas import tpu as pltpu
from jax.sharding import PartitionSpec as P

COARSE_ROWS = 64
BF16 = jnp.bfloat16
F32 = jnp.float32


def side_by_side(a_ref, f):
    return jnp.concatenate([a_ref[f, k] for k in range(a_ref.shape[1])], axis=1)


def placed_product(a_row, pool, index):
    stacked = jnp.concatenate([pool[i] for i in index], axis=0)
    return jnp.dot(a_row, stacked, preferred_element_type=F32).astype(BF16)


def own_tiles(rows, zero, half, me, pair_ref, pool):
    tiles = []
    for m in range(half):
        at = [me * rows + f for f in range(rows)]
        if half > 1:
            at = [jnp.where(pair_ref[rows + i] == m, i, zero) for i in at]
        tiles.append([pool[i] for i in at])
    return tiles


def restrict(tiles, q, half):
    outs = []
    for m in range(half):
        lhs = jnp.concatenate(tiles[m], axis=0)
        outs.append(
            lax.dot_general(lhs, q, (((0,), (0,)), ((), ())), preferred_element_type=F32)
        )
    return outs


def order_kernel(cols_hbm, p_hbm, *rest):
    outs, (cols_ref, p_ref, sems) = rest[:2], rest[2:]
    rows, tile = p_ref.shape[:2]
    piece = rows // 2
    lists = pltpu.make_async_copy(cols_hbm, cols_ref, sems.at[rows])
    lists.start()
    loads = [pltpu.make_async_copy(p_hbm.at[f], p_ref.at[f], sems.at[f]) for f in range(rows)]
    for load in loads:
        load.start()
    lists.wait()
    for f in range(rows):
        loads[f].wait()
        first = pl.multiple_of(jnp.where(cols_ref[0, f] > cols_ref[1, f], tile, 0), tile)
        for t, start in ((0, first), (1, pl.multiple_of(tile - first, tile))):
            outs[f // piece][f % piece, :, t * tile : (t + 1) * tile] = p_ref[f, :, pl.ds(start, tile)]


def hand_out_kernel(subs, pool, near_ref, far_ref):
    rows = near_ref.shape[0]
    odd = lax.rem(lax.axis_index("dom"), 2)
    last = (subs - 1) * rows
    near_ref[...] = pool[pl.ds((1 - odd) * last, rows)]
    far_ref[...] = pool[pl.ds(odd * last, rows)]


def edge_kernel(subs, half, cols_ref, count_ref, pair_ref, a_hbm, own_0, own_1, *rest):
    out_ref, a_ref, turned, sems = rest
    rows, slots, tile = a_ref.shape[:3]
    first = lax.axis_index("dom") * (subs * rows)
    me = lax.axis_index("sub")
    loads = [pltpu.make_async_copy(a_hbm.at[f], a_ref.at[f], sems.at[f]) for f in range(rows)]
    for load in loads:
        load.start()
    out_ref[...] = jnp.zeros(out_ref.shape, F32)
    for f in range(rows):
        turned[f] = (own_0, own_1)[f // (rows // 2)][f % (rows // 2)].T
    for f in range(rows):
        loads[f].wait()
        for k in range(slots):
            rel = cols_ref[f, k] - first
            live = (k < count_ref[f]) & ((rel < 0) | (rel >= subs * rows))

            @pl.when(live)
            def _():
                at = jnp.where(rel < 0, rel + rows, rel - subs * rows + rows)
                term = jnp.dot(turned[f], a_ref[f, k], preferred_element_type=F32)
                if half == 1:
                    out_ref[at] += term
                else:
                    m = pair_ref[rows + me * rows + f]
                    for start, part in ((m, term[:tile]), (m + half, term[tile:])):
                        out_ref[at, pl.ds(pl.multiple_of(start * tile, tile), tile)] += part


def terms_kernel(subs, cols_ref, count_ref, a_hbm, own_0, own_1, *rest):
    edges, (high_ref, low_ref, a_ref, total, turned, sems) = rest[:subs], rest[subs:]
    rows, slots, tile = a_ref.shape[:3]
    tiles = total.shape[0] - 1
    me = lax.axis_index("sub")
    base = lax.axis_index("dom") * (subs * rows) - rows
    loads = [pltpu.make_async_copy(a_hbm.at[f], a_ref.at[f], sems.at[f]) for f in range(rows)]
    for load in loads:
        load.start()
    total[...] = jnp.zeros(total.shape, F32)
    for f in range(rows):
        turned[f] = (own_0, own_1)[f // (rows // 2)][f % (rows // 2)].T
    for f in range(rows):
        loads[f].wait()
        for k in range(slots):
            at = jnp.where(k < count_ref[f], cols_ref[f, k] - base, tiles)
            total[at] += jnp.dot(turned[f], a_ref[f, k], preferred_element_type=F32)
    for c in range(subs * rows):
        value = total[rows + c]
        high = value.astype(BF16)
        high_ref[c] = high
        low_ref[c] = (value - high.astype(F32)).astype(BF16)
    for k in range(subs):
        start = pl.multiple_of(lax.bitwise_xor(me, k) * COARSE_ROWS, COARSE_ROWS)
        for i, c in enumerate([*range(rows), *range(tiles - rows, tiles)]):
            part = total[c, pl.ds(start, COARSE_ROWS)]
            edges[k][:, i * tile : (i + 1) * tile] = part.astype(edges[k].dtype)


def terms_product(rows, sources, high_ref, low_ref, p_refs):
    me = lax.axis_index("sub")
    both = []
    for ref in (high_ref, low_ref):
        at = [lax.bitwise_xor(me, k) * rows + f for k in sources for f in range(rows)]
        both.append(jnp.concatenate([ref[i] for i in at], axis=1))
    stacked = jnp.concatenate([ref[i] for ref in p_refs for i in range(ref.shape[0])], axis=0)
    out = jnp.dot(jnp.concatenate(both, axis=0), stacked, preferred_element_type=F32)
    height = high_ref.shape[1]
    return out[:height] + out[height:]


def early_kernel(rows, sources, high_ref, low_ref, *rest):
    rest[-1][...] = terms_product(rows, sources, high_ref, low_ref, rest[:-1])


def late_kernel(subs, rows, sources, high_ref, low_ref, early_ref, *rest):
    p_refs, rest = rest[: 2 * len(sources)], rest[2 * len(sources) :]
    edges, outs, mid = rest[:subs], rest[subs:-1], rest[-1]
    width = mid.shape[1]
    mid[...] = early_ref[...] + terms_product(rows, sources, high_ref, low_ref, p_refs)
    me = lax.axis_index("sub")
    for k in range(subs):
        start = pl.multiple_of(lax.bitwise_xor(me, k) * COARSE_ROWS, COARSE_ROWS)
        outs[k][:, :width] = mid[pl.ds(start, COARSE_ROWS)].astype(outs[k].dtype)
        outs[k][:, width:] = edges[k][...]


def hand_out_pieces_kernel(subs, _, *refs):
    p_refs, (near_ref, far_ref, ends) = refs[: 2 * subs], refs[2 * subs :]
    rows, piece = near_ref.shape[0], p_refs[0].shape[0]
    me, odd = lax.axis_index("sub"), lax.rem(lax.axis_index("dom"), 2)
    for k in range(subs):
        for at, who in ((0, 0), (rows, subs - 1)):

            @pl.when(me == who ^ k)
            def _():
                for i in range(2):
                    ends[at + i * piece : at + (i + 1) * piece] = p_refs[2 * k + i][...]

    near_ref[...] = ends[pl.ds((1 - odd) * rows, rows)]
    far_ref[...] = ends[pl.ds(odd * rows, rows)]


def group_kernel(subs, half, cols_ref, count_ref, pair_ref, a_ref, edge_ref, *rest):
    p_refs, rest = rest[: 2 * subs], rest[2 * subs :]
    outs, (pool, q, mid_ref) = rest[:subs], rest[subs:]
    rows, slots, tile = a_ref.shape[0], a_ref.shape[1], a_ref.shape[2]
    zero = subs * rows
    width = 2 * half * tile
    me = lax.axis_index("sub")
    first = lax.axis_index("dom") * (subs * rows)
    piece = rows // 2
    for k in range(subs):
        for i in range(2):
            pool[pl.ds(lax.bitwise_xor(me, k) * rows + i * piece, piece)] = p_refs[2 * k + i][...]
    pool[zero] = jnp.zeros(pool.shape[1:], pool.dtype)
    for f in range(rows):
        a_row = side_by_side(a_ref, f)
        index = [[None] * slots for _ in range(half)]
        for k in range(slots):
            rel = cols_ref[f, k] - first
            inside = (rel >= 0) & (rel < zero) & (k < count_ref[f])
            safe = jnp.where(inside, rel, 0)
            for m in range(half):
                here = inside if half == 1 else inside & (pair_ref[rows + safe] == m)
                index[m][k] = jnp.where(here, safe, zero)
        for m in range(half):
            block = placed_product(a_row, pool, index[m])
            lo, hi = m * tile, (m + half) * tile
            q[f * tile : (f + 1) * tile, lo : lo + tile] = block[:, :tile]
            q[f * tile : (f + 1) * tile, hi : hi + tile] = block[:, tile:]
    for m, out in enumerate(restrict(own_tiles(rows, zero, half, me, pair_ref, pool), q[...], half)):
        mid_ref[m * tile : (m + 1) * tile] = out[:tile]
        mid_ref[(m + half) * tile : (m + half + 1) * tile] = out[tile:]
    for k in range(subs):
        at = pl.ds(pl.multiple_of(lax.bitwise_xor(me, k) * COARSE_ROWS, COARSE_ROWS), COARSE_ROWS)
        kind = outs[k].dtype
        outs[k][:, :width] = mid_ref[at].astype(kind)
        for c in range(2 * rows):
            outs[k][:, width + c * tile : width + (c + 1) * tile] = edge_ref[c, at].astype(kind)


def halo_product(subs, half, side, pair_ref, terms, p_ref):
    rows, tile = p_ref.shape[:2]
    if half == 1:
        stacked = jnp.concatenate([p_ref[t] for t in range(rows)], axis=0)
        out = jnp.dot(terms, stacked, preferred_element_type=F32)
        out = out[:COARSE_ROWS] + out[COARSE_ROWS:]
        return [out[:, :tile], out[:, tile:]]
    blocks = [jnp.zeros((COARSE_ROWS, tile), F32) for _ in range(2 * half)]
    for t in range(rows):
        lhs = terms[:, t * tile : (t + 1) * tile]
        out = jnp.dot(lhs, p_ref[t], preferred_element_type=F32)
        out = out[:COARSE_ROWS] + out[COARSE_ROWS:]
        m_here = pair_ref[side * (subs + 1) * rows + t]
        for m in range(half):
            blocks[m] = blocks[m] + jnp.where(m_here == m, out[:, :tile], 0.0)
            blocks[m + half] = blocks[m + half] + jnp.where(m_here == m, out[:, tile:], 0.0)
    return blocks


def sum_kernel(_, *refs):
    total = refs[0][...]
    for ref in refs[1:-1]:
        total = total + ref[...].astype(F32)
    refs[-1][...] = total


def near_kernel(subs, half, pair_ref, near_ref, sum_ref, last_ref, *rest):
    mid_ref, side_ref, terms_ref, total = rest
    rows, tile = near_ref.shape[:2]
    width, span = 2 * half * tile, rows * tile
    odd = lax.rem(lax.axis_index("dom"), 2)
    total[...] = sum_ref[...] + last_ref[...].astype(F32)
    mid_ref[...] = total[:, :width].astype(BF16)

    def terms(side):
        value = total[:, pl.ds(pl.multiple_of(width + side * span, tile), span)]
        high = value.astype(BF16)
        return jnp.concatenate([high, (value - high.astype(F32)).astype(BF16)], axis=0)

    terms_ref[...] = terms(odd)
    blocks = halo_product(subs, half, 1 - odd, pair_ref, terms(1 - odd), near_ref)
    for b in range(2 * half):
        side_ref[:, b * tile : (b + 1) * tile] = blocks[b].astype(BF16)


def finish_kernel(subs, half, pair_ref, far_ref, terms_ref, mid_ref, side_ref, out_ref):
    tile = far_ref.shape[1]
    width = 2 * half * tile
    odd = lax.rem(lax.axis_index("dom"), 2)
    out_ref[:, width : 2 * width] = mid_ref[...]
    out_ref[:, pl.ds(pl.multiple_of((1 - odd) * 2 * width, tile), width)] = side_ref[...]
    blocks = halo_product(subs, half, odd, pair_ref, terms_ref[...], far_ref)
    for b in range(2 * half):
        at = pl.multiple_of(odd * 2 * width + b * tile, tile)
        out_ref[:, pl.ds(at, tile)] = blocks[b].astype(BF16)


def narrow_parts(a_tiles, a_cols, a_count, own, tiles, span):
    rows, slots, tile = a_tiles.shape[:3]
    subs = lax.axis_size("sub")
    width = 2 * tile
    smem = pl.BlockSpec(memory_space=pltpu.SMEM)
    vmem = pl.BlockSpec(memory_space=pltpu.VMEM)
    kinds = [F32] + [BF16] * (subs - 1)
    spare = 3 << 20
    products = 2 * width * rows * tile * width
    *edges, high, low = pl.pallas_call(
        functools.partial(terms_kernel, subs),
        out_shape=[jax.ShapeDtypeStruct((COARSE_ROWS, span - width), kind) for kind in kinds]
        + [jax.ShapeDtypeStruct((subs * rows, width, tile), BF16)] * 2,
        in_specs=[smem, smem, pl.BlockSpec(memory_space=pltpu.HBM), vmem, vmem],
        out_specs=[vmem] * (subs + 2),
        scratch_shapes=[
            pltpu.VMEM(a_tiles.shape, BF16),
            pltpu.VMEM(((subs + 2) * rows + 1, width, tile), F32),
            pltpu.VMEM((rows, width, tile), BF16),
            pltpu.SemaphoreType.DMA((rows,)),
        ],
        compiler_params=pltpu.CompilerParams(
            vmem_limit_bytes=2 * a_tiles.size + 4 * ((subs + 2) * rows + 1) * width * tile + spare
        ),
        cost_estimate=pl.CostEstimate(
            flops=1 << 31, bytes_accessed=2 * a_tiles.size, transcendentals=0
        ),
        name="terms",
    )(a_cols, a_count, pltpu.with_memory_space_constraint(a_tiles, pltpu.HBM), *own)
    first, last = list(range(subs - 1)), [subs - 1]
    early = pl.pallas_call(
        functools.partial(early_kernel, rows, first),
        out_shape=jax.ShapeDtypeStruct((width, width), F32),
        in_specs=[vmem] * (2 + 2 * len(first)),
        out_specs=vmem,
        compiler_params=pltpu.CompilerParams(vmem_limit_bytes=spare),
        cost_estimate=pl.CostEstimate(
            flops=2 * len(first) * products, bytes_accessed=1 << 20, transcendentals=0
        ),
        name="early_part",
    )(high, low, *[piece for k in first for piece in tiles[k]])
    parts = pl.pallas_call(
        functools.partial(late_kernel, subs, rows, last),
        out_shape=[jax.ShapeDtypeStruct((COARSE_ROWS, span), kind) for kind in kinds],
        in_specs=[vmem] * (3 + 2 * len(last) + subs),
        out_specs=[vmem] * subs,
        scratch_shapes=[pltpu.VMEM((width, width), F32)],
        compiler_params=pltpu.CompilerParams(vmem_limit_bytes=spare),
        cost_estimate=pl.CostEstimate(
            flops=2 * products, bytes_accessed=1 << 20, transcendentals=0
        ),
        name="late_part",
    )(high, low, early, *tiles[-1], *edges)
    return [*parts, early]


def local(a_tiles, a_cols, a_count, p_tiles, p_cols):
    rows, slots, tile = a_tiles.shape[:3]
    subs, doms = lax.axis_size("sub"), lax.axis_size("dom")
    coarse_group = subs * COARSE_ROWS // tile
    half = coarse_group // 2
    width = coarse_group * tile
    group_tiles = rows * subs

    smem = pl.BlockSpec(memory_space=pltpu.SMEM)
    vmem = pl.BlockSpec(memory_space=pltpu.VMEM)
    p_bytes = rows * tile * 2 * tile * 2
    a_bytes = a_tiles.size * 2
    spare = 3 << 20

    def exchange(value, k):
        return lax.ppermute(value, "sub", [(s, s ^ k) for s in range(subs)])

    own = pl.pallas_call(
        order_kernel,
        out_shape=[jax.ShapeDtypeStruct((rows // 2, tile, 2 * tile), BF16)] * 2,
        in_specs=[pl.BlockSpec(memory_space=pltpu.HBM)] * 2,
        out_specs=[vmem] * 2,
        scratch_shapes=[
            pltpu.SMEM((2, rows), jnp.int32),
            pltpu.VMEM(p_tiles.shape, BF16),
            pltpu.SemaphoreType.DMA((rows + 1,)),
        ],
        compiler_params=pltpu.CompilerParams(vmem_limit_bytes=spare),
        cost_estimate=pl.CostEstimate(
            flops=1 << 30, bytes_accessed=2 * p_bytes, transcendentals=0
        ),
        name="order_columns",
    )(
        pltpu.with_memory_space_constraint(p_cols.T, pltpu.HBM),
        pltpu.with_memory_space_constraint(p_tiles, pltpu.HBM),
    )

    tiles = [list(own)] + [[None, None] for _ in range(subs - 1)]
    for k in range(1, subs):
        low, high = k & -k, 1 << (k.bit_length() - 1)
        tiles[k][0] = exchange(tiles[k ^ low][0], low)
        tiles[k][1] = exchange(tiles[k ^ high][1], high)
    span = width + 2 * rows * tile
    if half == 1:
        pair = jnp.zeros((1,), jnp.int32)
    else:
        m_own = jnp.min(p_cols, axis=1) - lax.axis_index("dom") * coarse_group
        m_group = lax.all_gather(m_own, "sub", axis=0, tiled=True)
        m_left = lax.ppermute(
            m_group[group_tiles - rows :], "dom", [(d, d + 1) for d in range(doms - 1)]
        )
        m_right = lax.ppermute(m_group[:rows], "dom", [(d + 1, d) for d in range(doms - 1)])
        pair = jnp.concatenate([m_left, m_group, m_right])

    flat = [piece for pieces in tiles for piece in pieces]
    if half == 1:
        *parts, early = narrow_parts(a_tiles, a_cols, a_count, own, tiles, span)
        to_near, to_far = pl.pallas_call(
            functools.partial(hand_out_pieces_kernel, subs),
            out_shape=[jax.ShapeDtypeStruct(p_tiles.shape, BF16)] * 2,
            in_specs=[pl.BlockSpec(memory_space=pl.ANY)] + [vmem] * (2 * subs),
            out_specs=[vmem] * 2,
            scratch_shapes=[pltpu.VMEM((2 * rows, tile, 2 * tile), BF16)],
            compiler_params=pltpu.CompilerParams(vmem_limit_bytes=spare),
            name="hand_out",
        )(early, *flat)
    else:
        flops = 2 * rows * slots * tile * tile * 2 * tile * half
        edges, a_held = pl.pallas_call(
            functools.partial(edge_kernel, subs, half),
            out_shape=[
                jax.ShapeDtypeStruct((2 * rows, width, tile), F32),
                jax.ShapeDtypeStruct(a_tiles.shape, BF16),
            ],
            in_specs=[smem, smem, smem, pl.BlockSpec(memory_space=pltpu.HBM), vmem, vmem],
            out_specs=[vmem] * 2,
            scratch_shapes=[
                pltpu.VMEM((rows, 2 * tile, tile), BF16),
                pltpu.SemaphoreType.DMA((rows,)),
            ],
            compiler_params=pltpu.CompilerParams(vmem_limit_bytes=8 * rows * tile * width + spare),
            cost_estimate=pl.CostEstimate(
                flops=flops, bytes_accessed=a_bytes + p_bytes, transcendentals=0
            ),
            name="edge_part",
        )(a_cols, a_count, pair, pltpu.with_memory_space_constraint(a_tiles, pltpu.HBM), *own)

        *parts, pool = pl.pallas_call(
            functools.partial(group_kernel, subs, half),
            out_shape=[
                jax.ShapeDtypeStruct((COARSE_ROWS, span), F32 if k == 0 else BF16)
                for k in range(subs)
            ]
            + [jax.ShapeDtypeStruct((group_tiles + 1, tile, 2 * tile), BF16)],
            in_specs=[smem, smem, smem] + [vmem] * (2 * subs + 2),
            out_specs=[vmem] * (subs + 1),
            scratch_shapes=[
                pltpu.VMEM((rows * tile, width), BF16),
                pltpu.VMEM((width, width), F32),
            ],
            compiler_params=pltpu.CompilerParams(
                vmem_limit_bytes=2 * rows * tile * width + 4 * width * width + spare
            ),
            cost_estimate=pl.CostEstimate(
                flops=flops, bytes_accessed=a_bytes + subs * p_bytes, transcendentals=0
            ),
            name="group_part",
        )(a_cols, a_count, pair, a_held, edges, *flat)
        to_near, to_far = pl.pallas_call(
            functools.partial(hand_out_kernel, subs),
            out_shape=[jax.ShapeDtypeStruct(p_tiles.shape, BF16)] * 2,
            in_specs=[vmem],
            out_specs=[vmem] * 2,
            compiler_params=pltpu.CompilerParams(vmem_limit_bytes=spare),
            name="hand_out",
        )(pool)
    received = [exchange(parts[k], k) for k in [*range(subs - 1, subs // 2, -1), *range(1, subs // 2), subs // 2]]
    far = lax.ppermute(
        to_far, "dom", [(d, d - 1 + 2 * (d % 2)) for d in range(1, doms - 1)]
    )
    near = lax.ppermute(to_near, "dom", [(d, d ^ 1) for d in range(doms)])
    sums = pl.pallas_call(
        sum_kernel,
        out_shape=jax.ShapeDtypeStruct((COARSE_ROWS, span), F32),
        in_specs=[pl.BlockSpec(memory_space=pl.ANY)] + [vmem] * (subs - 1),
        out_specs=vmem,
        compiler_params=pltpu.CompilerParams(vmem_limit_bytes=spare),
        cost_estimate=pl.CostEstimate(flops=3 << 29, bytes_accessed=1 << 20, transcendentals=0),
        name="sum_parts",
    )(near, parts[0], *received[:-1])
    mid, side, terms = pl.pallas_call(
        functools.partial(near_kernel, subs, half),
        out_shape=[
            jax.ShapeDtypeStruct((COARSE_ROWS, width), BF16),
            jax.ShapeDtypeStruct((COARSE_ROWS, width), BF16),
            jax.ShapeDtypeStruct((2 * COARSE_ROWS, rows * tile), BF16),
        ],
        in_specs=[smem] + [vmem] * 3,
        out_specs=[vmem] * 3,
        scratch_shapes=[pltpu.VMEM((COARSE_ROWS, span), F32)],
        compiler_params=pltpu.CompilerParams(vmem_limit_bytes=2 * p_bytes + spare),
        cost_estimate=pl.CostEstimate(flops=1 << 20, bytes_accessed=1 << 20, transcendentals=0),
        name="near_part",
    )(pair, near, sums, received[-1])
    return pl.pallas_call(
        functools.partial(finish_kernel, subs, half),
        out_shape=jax.ShapeDtypeStruct((COARSE_ROWS, 3 * width), BF16),
        in_specs=[smem] + [vmem] * 4,
        out_specs=vmem,
        compiler_params=pltpu.CompilerParams(vmem_limit_bytes=2 * p_bytes + spare),
        cost_estimate=pl.CostEstimate(flops=1 << 20, bytes_accessed=1 << 20, transcendentals=0),
        name="far_part",
    )(pair, far, terms, mid, side)


def solution(mesh):
    placed = (
        P(("dom", "sub"), None, None, None),
        P(("dom", "sub"), None),
        P(("dom", "sub")),
        P(("dom", "sub"), None, None),
        P(("dom", "sub"), None),
    )
    return jax.shard_map(
        local, mesh=mesh, in_specs=placed, out_specs=P(("dom", "sub"), None), check_vma=False
    )
```

```python
import functools

import jax
import jax.numpy as jnp
from jax import lax
from jax.experimental import pallas as pl
from jax.experimental.pallas import tpu as pltpu
from jax.sharding import PartitionSpec as P

COARSE_ROWS = 64
BF16 = jnp.bfloat16
F32 = jnp.float32


def side_by_side(a_ref, f):
    return jnp.concatenate([a_ref[f, k] for k in range(a_ref.shape[1])], axis=1)


def placed_product(a_row, pool, index):
    stacked = jnp.concatenate([pool[i] for i in index], axis=0)
    return jnp.dot(a_row, stacked, preferred_element_type=F32).astype(BF16)


def own_tiles(rows, zero, half, me, pair_ref, pool):
    tiles = []
    for m in range(half):
        at = [me * rows + f for f in range(rows)]
        if half > 1:
            at = [jnp.where(pair_ref[rows + i] == m, i, zero) for i in at]
        tiles.append([pool[i] for i in at])
    return tiles


def restrict(tiles, q, half):
    outs = []
    for m in range(half):
        lhs = jnp.concatenate(tiles[m], axis=0)
        outs.append(
            lax.dot_general(lhs, q, (((0,), (0,)), ((), ())), preferred_element_type=F32)
        )
    return outs


def order_kernel(with_a, cols_hbm, p_hbm, *rest):
    if with_a:
        (a_hbm, *outs, a_ref), (cols_ref, p_ref, sems) = rest[:-3], rest[-3:]
    else:
        outs, (cols_ref, p_ref, sems) = rest[:-3], rest[-3:]
    rows, tile = p_ref.shape[:2]
    piece = rows // 2
    odd = lax.rem(lax.axis_index("dom"), 2) == 1
    lists = pltpu.make_async_copy(cols_hbm, cols_ref, sems.at[rows])
    lists.start()
    loads = [pltpu.make_async_copy(p_hbm.at[f], p_ref.at[f], sems.at[f]) for f in range(rows)]
    for load in loads:
        load.start()
    if with_a:

        @pl.when(odd)
        def _():
            pltpu.make_async_copy(a_hbm, a_ref, sems.at[rows + 1]).start()

    lists.wait()
    for f in range(rows):
        loads[f].wait()
        first = pl.multiple_of(jnp.where(cols_ref[0, f] > cols_ref[1, f], tile, 0), tile)
        for t, start in ((0, first), (1, pl.multiple_of(tile - first, tile))):
            outs[f // piece][f % piece, :, t * tile : (t + 1) * tile] = p_ref[f, :, pl.ds(start, tile)]
    if with_a:

        @pl.when(odd)
        def _():
            pltpu.make_async_copy(a_hbm, a_ref, sems.at[rows + 1]).wait()


def hand_out_kernel(subs, pool, near_ref, far_ref):
    rows = near_ref.shape[0]
    odd = lax.rem(lax.axis_index("dom"), 2)
    last = (subs - 1) * rows
    near_ref[...] = pool[pl.ds((1 - odd) * last, rows)]
    far_ref[...] = pool[pl.ds(odd * last, rows)]


def edge_kernel(subs, half, cols_ref, count_ref, pair_ref, a_hbm, own_0, own_1, *rest):
    out_ref, a_ref, turned, sems = rest
    rows, slots, tile = a_ref.shape[:3]
    first = lax.axis_index("dom") * (subs * rows)
    me = lax.axis_index("sub")
    loads = [pltpu.make_async_copy(a_hbm.at[f], a_ref.at[f], sems.at[f]) for f in range(rows)]
    for load in loads:
        load.start()
    out_ref[...] = jnp.zeros(out_ref.shape, F32)
    for f in range(rows):
        turned[f] = (own_0, own_1)[f // (rows // 2)][f % (rows // 2)].T
    for f in range(rows):
        loads[f].wait()
        for k in range(slots):
            rel = cols_ref[f, k] - first
            live = (k < count_ref[f]) & ((rel < 0) | (rel >= subs * rows))

            @pl.when(live)
            def _():
                at = jnp.where(rel < 0, rel + rows, rel - subs * rows + rows)
                term = jnp.dot(turned[f], a_ref[f, k], preferred_element_type=F32)
                if half == 1:
                    out_ref[at] += term
                else:
                    m = pair_ref[rows + me * rows + f]
                    for start, part in ((m, term[:tile]), (m + half, term[tile:])):
                        out_ref[at, pl.ds(pl.multiple_of(start * tile, tile), tile)] += part


def terms_kernel(subs, cols_ref, count_ref, a_hbm, a_held, own_0, own_1, *rest):
    edges, (high_ref, low_ref, a_ref, total, turned, sems) = rest[:subs], rest[subs:]
    rows, slots, tile = a_ref.shape[:3]
    tiles = total.shape[0] - 1
    me = lax.axis_index("sub")
    base = lax.axis_index("dom") * (subs * rows) - rows
    odd = lax.rem(lax.axis_index("dom"), 2)
    loads = [pltpu.make_async_copy(a_hbm.at[f], a_ref.at[f], sems.at[f]) for f in range(rows)]
    for source, here in ((a_held, odd == 1), (a_hbm, odd == 0)):

        @pl.when(here)
        def _():
            for f in range(rows):
                pltpu.make_async_copy(source.at[f], a_ref.at[f], sems.at[f]).start()

    total[...] = jnp.zeros(total.shape, F32)
    for f in range(rows):
        turned[f] = (own_0, own_1)[f // (rows // 2)][f % (rows // 2)].T
    for f in range(rows):
        loads[f].wait()
        for k in range(slots):
            at = jnp.where(k < count_ref[f], cols_ref[f, k] - base, tiles)
            total[at] += jnp.dot(turned[f], a_ref[f, k], preferred_element_type=F32)
    for c in range(subs * rows):
        value = total[rows + c]
        high = value.astype(BF16)
        high_ref[c] = high
        low_ref[c] = (value - high.astype(F32)).astype(BF16)
    for k in range(subs):
        start = pl.multiple_of(lax.bitwise_xor(me, k) * COARSE_ROWS, COARSE_ROWS)
        for i, c in enumerate([*range(rows), *range(tiles - rows, tiles)]):
            part = total[c, pl.ds(start, COARSE_ROWS)]
            edges[k][:, i * tile : (i + 1) * tile] = part.astype(edges[k].dtype)


def terms_product(rows, sources, high_ref, low_ref, p_refs):
    me = lax.axis_index("sub")
    both = []
    for ref in (high_ref, low_ref):
        at = [lax.bitwise_xor(me, k) * rows + f for k in sources for f in range(rows)]
        both.append(jnp.concatenate([ref[i] for i in at], axis=1))
    stacked = jnp.concatenate([ref[i] for ref in p_refs for i in range(ref.shape[0])], axis=0)
    out = jnp.dot(jnp.concatenate(both, axis=0), stacked, preferred_element_type=F32)
    height = high_ref.shape[1]
    return out[:height] + out[height:]


def early_kernel(rows, sources, high_ref, low_ref, *rest):
    rest[-1][...] = terms_product(rows, sources, high_ref, low_ref, rest[:-1])


def late_kernel(subs, rows, sources, high_ref, low_ref, early_ref, *rest):
    p_refs, rest = rest[: 2 * subs], rest[2 * subs :]
    edges, outs, (near_ref, far_ref, mid, ends) = rest[:subs], rest[subs:-4], rest[-4:]
    width, piece = mid.shape[1], p_refs[0].shape[0]
    me, odd = lax.axis_index("sub"), lax.rem(lax.axis_index("dom"), 2)
    last = [p_refs[2 * k + i] for k in sources for i in range(2)]
    mid[...] = early_ref[...] + terms_product(rows, sources, high_ref, low_ref, last)
    for k in range(subs):
        start = pl.multiple_of(lax.bitwise_xor(me, k) * COARSE_ROWS, COARSE_ROWS)
        outs[k][:, :width] = mid[pl.ds(start, COARSE_ROWS)].astype(outs[k].dtype)
        outs[k][:, width:] = edges[k][...]
    for k in range(subs):
        for at, who in ((0, 0), (rows, subs - 1)):

            @pl.when(me == who ^ k)
            def _():
                for i in range(2):
                    ends[at + i * piece : at + (i + 1) * piece] = p_refs[2 * k + i][...]

    near_ref[...] = ends[pl.ds((1 - odd) * rows, rows)]
    far_ref[...] = ends[pl.ds(odd * rows, rows)]


def group_kernel(subs, half, cols_ref, count_ref, pair_ref, a_ref, edge_ref, *rest):
    p_refs, rest = rest[: 2 * subs], rest[2 * subs :]
    outs, (pool, q, mid_ref) = rest[:subs], rest[subs:]
    rows, slots, tile = a_ref.shape[0], a_ref.shape[1], a_ref.shape[2]
    zero = subs * rows
    width = 2 * half * tile
    me = lax.axis_index("sub")
    first = lax.axis_index("dom") * (subs * rows)
    piece = rows // 2
    for k in range(subs):
        for i in range(2):
            pool[pl.ds(lax.bitwise_xor(me, k) * rows + i * piece, piece)] = p_refs[2 * k + i][...]
    pool[zero] = jnp.zeros(pool.shape[1:], pool.dtype)
    for f in range(rows):
        a_row = side_by_side(a_ref, f)
        index = [[None] * slots for _ in range(half)]
        for k in range(slots):
            rel = cols_ref[f, k] - first
            inside = (rel >= 0) & (rel < zero) & (k < count_ref[f])
            safe = jnp.where(inside, rel, 0)
            for m in range(half):
                here = inside if half == 1 else inside & (pair_ref[rows + safe] == m)
                index[m][k] = jnp.where(here, safe, zero)
        for m in range(half):
            block = placed_product(a_row, pool, index[m])
            lo, hi = m * tile, (m + half) * tile
            q[f * tile : (f + 1) * tile, lo : lo + tile] = block[:, :tile]
            q[f * tile : (f + 1) * tile, hi : hi + tile] = block[:, tile:]
    for m, out in enumerate(restrict(own_tiles(rows, zero, half, me, pair_ref, pool), q[...], half)):
        mid_ref[m * tile : (m + 1) * tile] = out[:tile]
        mid_ref[(m + half) * tile : (m + half + 1) * tile] = out[tile:]
    for k in range(subs):
        at = pl.ds(pl.multiple_of(lax.bitwise_xor(me, k) * COARSE_ROWS, COARSE_ROWS), COARSE_ROWS)
        kind = outs[k].dtype
        outs[k][:, :width] = mid_ref[at].astype(kind)
        for c in range(2 * rows):
            outs[k][:, width + c * tile : width + (c + 1) * tile] = edge_ref[c, at].astype(kind)


def sum_kernel(subs, width, *refs):
    part_refs, (mid_ref, edge_ref) = refs[:subs], refs[subs:]
    total = part_refs[0][...]
    for k in range(1, subs):
        total = total + part_refs[k][...].astype(F32)
    mid_ref[...] = total[:, :width].astype(BF16)
    sums = total[:, width:]
    high = sums.astype(BF16)
    edge_ref[:COARSE_ROWS] = high
    edge_ref[COARSE_ROWS:] = (sums - high.astype(F32)).astype(BF16)


def finish_kernel(subs, half, *refs):
    pair_ref = refs[0] if half > 1 else None
    far_ref, near_ref, mid_ref, both_ref, out_ref, edge = refs[-6:]
    rows, tile = near_ref.shape[:2]
    width = 2 * half * tile
    odd = lax.rem(lax.axis_index("dom"), 2)
    edge[pl.ds((1 - odd) * rows, rows)] = near_ref[...]
    edge[pl.ds(odd * rows, rows)] = far_ref[...]
    out_ref[:, width : 2 * width] = mid_ref[...]
    both = both_ref[...]
    for side in range(2):
        blocks = [jnp.zeros((COARSE_ROWS, tile), F32) for _ in range(2 * half)]
        tiles = range(side * rows, (side + 1) * rows)
        if half == 1:
            stacked = jnp.concatenate([edge[c] for c in tiles], axis=0)
            lhs = both[:, side * rows * tile : (side + 1) * rows * tile]
            term = jnp.dot(lhs, stacked, preferred_element_type=F32)
            term = term[:COARSE_ROWS] + term[COARSE_ROWS:]
            blocks = [term[:, :tile], term[:, tile:]]
        else:
            for c in tiles:
                lhs = both[:, c * tile : (c + 1) * tile]
                term = jnp.dot(lhs, edge[c], preferred_element_type=F32)
                term = term[:COARSE_ROWS] + term[COARSE_ROWS:]
                m_here = pair_ref[c if side == 0 else subs * rows + c]
                for m in range(half):
                    here = m_here == m
                    blocks[m] = blocks[m] + jnp.where(here, term[:, :tile], 0.0)
                    blocks[m + half] = blocks[m + half] + jnp.where(here, term[:, tile:], 0.0)
        for b in range(2 * half):
            at = 2 * side * width + b * tile
            out_ref[:, at : at + tile] = blocks[b].astype(BF16)


def narrow_parts(a_tiles, a_held, a_cols, a_count, own, tiles, span):
    rows, slots, tile = a_tiles.shape[:3]
    subs = lax.axis_size("sub")
    width = 2 * tile
    smem = pl.BlockSpec(memory_space=pltpu.SMEM)
    vmem = pl.BlockSpec(memory_space=pltpu.VMEM)
    kinds = [F32] + [BF16] * (subs - 1)
    spare = 3 << 20
    products = 2 * width * rows * tile * width
    *edges, high, low = pl.pallas_call(
        functools.partial(terms_kernel, subs),
        out_shape=[jax.ShapeDtypeStruct((COARSE_ROWS, span - width), kind) for kind in kinds]
        + [jax.ShapeDtypeStruct((subs * rows, width, tile), BF16)] * 2,
        in_specs=[smem, smem, pl.BlockSpec(memory_space=pltpu.HBM), vmem, vmem, vmem],
        out_specs=[vmem] * (subs + 2),
        scratch_shapes=[
            pltpu.VMEM(a_tiles.shape, BF16),
            pltpu.VMEM(((subs + 2) * rows + 1, width, tile), F32),
            pltpu.VMEM((rows, width, tile), BF16),
            pltpu.SemaphoreType.DMA((rows,)),
        ],
        compiler_params=pltpu.CompilerParams(
            vmem_limit_bytes=2 * a_tiles.size + 4 * ((subs + 2) * rows + 1) * width * tile + spare
        ),
        cost_estimate=pl.CostEstimate(
            flops=1 << 31, bytes_accessed=2 * a_tiles.size, transcendentals=0
        ),
        name="terms",
    )(a_cols, a_count, pltpu.with_memory_space_constraint(a_tiles, pltpu.HBM), a_held, *own)
    first, last = list(range(subs - 1)), [subs - 1]
    early = pl.pallas_call(
        functools.partial(early_kernel, rows, first),
        out_shape=jax.ShapeDtypeStruct((width, width), F32),
        in_specs=[vmem] * (2 + 2 * len(first)),
        out_specs=vmem,
        compiler_params=pltpu.CompilerParams(vmem_limit_bytes=spare),
        cost_estimate=pl.CostEstimate(
            flops=2 * len(first) * products, bytes_accessed=1 << 20, transcendentals=0
        ),
        name="early_part",
    )(high, low, *[piece for k in first for piece in tiles[k]])
    return pl.pallas_call(
        functools.partial(late_kernel, subs, rows, last),
        out_shape=[jax.ShapeDtypeStruct((COARSE_ROWS, span), kind) for kind in kinds]
        + [jax.ShapeDtypeStruct((rows, tile, width), BF16)] * 2,
        in_specs=[vmem] * (3 + 3 * subs),
        out_specs=[vmem] * (subs + 2),
        scratch_shapes=[
            pltpu.VMEM((width, width), F32),
            pltpu.VMEM((2 * rows, tile, width), BF16),
        ],
        compiler_params=pltpu.CompilerParams(vmem_limit_bytes=spare),
        cost_estimate=pl.CostEstimate(
            flops=2 * products, bytes_accessed=1 << 20, transcendentals=0
        ),
        name="late_part",
    )(high, low, early, *[piece for pieces in tiles for piece in pieces], *edges)


def local(a_tiles, a_cols, a_count, p_tiles, p_cols):
    rows, slots, tile = a_tiles.shape[:3]
    subs, doms = lax.axis_size("sub"), lax.axis_size("dom")
    coarse_group = subs * COARSE_ROWS // tile
    half = coarse_group // 2
    width = coarse_group * tile
    group_tiles = rows * subs

    smem = pl.BlockSpec(memory_space=pltpu.SMEM)
    vmem = pl.BlockSpec(memory_space=pltpu.VMEM)
    p_bytes = rows * tile * 2 * tile * 2
    a_bytes = a_tiles.size * 2
    spare = 3 << 20

    def exchange(value, k):
        return lax.ppermute(value, "sub", [(s, s ^ k) for s in range(subs)])

    loaded = [p_cols.T, p_tiles] + ([a_tiles] if half == 1 else [])
    ordered = pl.pallas_call(
        functools.partial(order_kernel, half == 1),
        out_shape=[jax.ShapeDtypeStruct((rows // 2, tile, 2 * tile), BF16)] * 2
        + [jax.ShapeDtypeStruct(array.shape, BF16) for array in loaded[2:]],
        in_specs=[pl.BlockSpec(memory_space=pltpu.HBM)] * len(loaded),
        out_specs=[vmem] * len(loaded),
        scratch_shapes=[
            pltpu.SMEM((2, rows), jnp.int32),
            pltpu.VMEM(p_tiles.shape, BF16),
            pltpu.SemaphoreType.DMA((rows + 2,)),
        ],
        compiler_params=pltpu.CompilerParams(vmem_limit_bytes=spare),
        cost_estimate=pl.CostEstimate(
            flops=1 << 30, bytes_accessed=2 * p_bytes, transcendentals=0
        ),
        name="order_columns",
    )(*[pltpu.with_memory_space_constraint(array, pltpu.HBM) for array in loaded])
    own, a_held = ordered[:2], ordered[-1]

    tiles = [list(own)] + [[None, None] for _ in range(subs - 1)]
    for k in range(1, subs):
        low, high = k & -k, 1 << (k.bit_length() - 1)
        tiles[k][0] = exchange(tiles[k ^ low][0], low)
        tiles[k][1] = exchange(tiles[k ^ high][1], high)
    span = width + 2 * rows * tile
    pairs = []
    if half > 1:
        m_own = jnp.min(p_cols, axis=1) - lax.axis_index("dom") * coarse_group
        m_group = lax.all_gather(m_own, "sub", axis=0, tiled=True)
        m_left = lax.ppermute(
            m_group[group_tiles - rows :], "dom", [(d, d + 1) for d in range(doms - 1)]
        )
        m_right = lax.ppermute(m_group[:rows], "dom", [(d + 1, d) for d in range(doms - 1)])
        pair = jnp.concatenate([m_left, m_group, m_right])
        pairs = [pair]

    flat = [piece for pieces in tiles for piece in pieces]
    if half == 1:
        *parts, to_near, to_far = narrow_parts(a_tiles, a_held, a_cols, a_count, own, tiles, span)
    else:
        flops = 2 * rows * slots * tile * tile * 2 * tile * half
        edges, a_held = pl.pallas_call(
            functools.partial(edge_kernel, subs, half),
            out_shape=[
                jax.ShapeDtypeStruct((2 * rows, width, tile), F32),
                jax.ShapeDtypeStruct(a_tiles.shape, BF16),
            ],
            in_specs=[smem, smem, smem, pl.BlockSpec(memory_space=pltpu.HBM), vmem, vmem],
            out_specs=[vmem] * 2,
            scratch_shapes=[
                pltpu.VMEM((rows, 2 * tile, tile), BF16),
                pltpu.SemaphoreType.DMA((rows,)),
            ],
            compiler_params=pltpu.CompilerParams(vmem_limit_bytes=8 * rows * tile * width + spare),
            cost_estimate=pl.CostEstimate(
                flops=flops, bytes_accessed=a_bytes + p_bytes, transcendentals=0
            ),
            name="edge_part",
        )(a_cols, a_count, pair, pltpu.with_memory_space_constraint(a_tiles, pltpu.HBM), *own)

        *parts, pool = pl.pallas_call(
            functools.partial(group_kernel, subs, half),
            out_shape=[
                jax.ShapeDtypeStruct((COARSE_ROWS, span), F32 if k == 0 else BF16)
                for k in range(subs)
            ]
            + [jax.ShapeDtypeStruct((group_tiles + 1, tile, 2 * tile), BF16)],
            in_specs=[smem, smem, smem] + [vmem] * (2 * subs + 2),
            out_specs=[vmem] * (subs + 1),
            scratch_shapes=[
                pltpu.VMEM((rows * tile, width), BF16),
                pltpu.VMEM((width, width), F32),
            ],
            compiler_params=pltpu.CompilerParams(
                vmem_limit_bytes=2 * rows * tile * width + 4 * width * width + spare
            ),
            cost_estimate=pl.CostEstimate(
                flops=flops, bytes_accessed=a_bytes + subs * p_bytes, transcendentals=0
            ),
            name="group_part",
        )(a_cols, a_count, pair, a_held, edges, *flat)
        to_near, to_far = pl.pallas_call(
            functools.partial(hand_out_kernel, subs),
            out_shape=[jax.ShapeDtypeStruct(p_tiles.shape, BF16)] * 2,
            in_specs=[vmem],
            out_specs=[vmem] * 2,
            compiler_params=pltpu.CompilerParams(vmem_limit_bytes=spare),
            name="hand_out",
        )(pool)
    received = [exchange(parts[k], k) for k in range(subs - 1, 0, -1)]
    far = lax.ppermute(
        to_far, "dom", [(d, d - 1 + 2 * (d % 2)) for d in range(1, doms - 1)]
    )
    near = lax.ppermute(to_near, "dom", [(d, d ^ 1) for d in range(doms)])
    mid, both = pl.pallas_call(
        functools.partial(sum_kernel, subs, width),
        out_shape=[
            jax.ShapeDtypeStruct((COARSE_ROWS, width), BF16),
            jax.ShapeDtypeStruct((2 * COARSE_ROWS, span - width), BF16),
        ],
        in_specs=[vmem] * subs,
        out_specs=[vmem] * 2,
        compiler_params=pltpu.CompilerParams(vmem_limit_bytes=spare),
        cost_estimate=pl.CostEstimate(
            flops=1 << 31, bytes_accessed=8 * COARSE_ROWS * span, transcendentals=0
        ),
        name="sum_parts",
    )(parts[0], *received)
    return pl.pallas_call(
        functools.partial(finish_kernel, subs, half),
        out_shape=jax.ShapeDtypeStruct((COARSE_ROWS, 3 * width), BF16),
        in_specs=[smem] * len(pairs) + [vmem] * 4,
        out_specs=vmem,
        scratch_shapes=[pltpu.VMEM((2 * rows, tile, 2 * tile), BF16)],
        compiler_params=pltpu.CompilerParams(vmem_limit_bytes=2 * p_bytes + spare),
        cost_estimate=pl.CostEstimate(
            flops=1 << 28, bytes_accessed=4 * p_bytes, transcendentals=0
        ),
        name="finish",
    )(*pairs, far, near, mid, both)


def solution(mesh):
    placed = (
        P(("dom", "sub"), None, None, None),
        P(("dom", "sub"), None),
        P(("dom", "sub")),
        P(("dom", "sub"), None, None),
        P(("dom", "sub"), None),
    )
    return jax.shard_map(
        local, mesh=mesh, in_specs=placed, out_specs=P(("dom", "sub"), None), check_vma=False
    )
```

```python
import functools

import jax
import jax.numpy as jnp
from jax import lax
from jax.experimental import pallas as pl
from jax.experimental.pallas import tpu as pltpu
from jax.sharding import PartitionSpec as P

COARSE_ROWS = 64
BF16 = jnp.bfloat16
F32 = jnp.float32


def side_by_side(a_ref, f):
    return jnp.concatenate([a_ref[f, k] for k in range(a_ref.shape[1])], axis=1)


def placed_product(a_row, pool, index):
    stacked = jnp.concatenate([pool[i] for i in index], axis=0)
    return jnp.dot(a_row, stacked, preferred_element_type=F32).astype(BF16)


def own_tiles(rows, zero, half, me, pair_ref, pool):
    tiles = []
    for m in range(half):
        at = [me * rows + f for f in range(rows)]
        if half > 1:
            at = [jnp.where(pair_ref[rows + i] == m, i, zero) for i in at]
        tiles.append([pool[i] for i in at])
    return tiles


def restrict(tiles, q, half):
    outs = []
    for m in range(half):
        lhs = jnp.concatenate(tiles[m], axis=0)
        outs.append(
            lax.dot_general(lhs, q, (((0,), (0,)), ((), ())), preferred_element_type=F32)
        )
    return outs


def order_kernel(cols_hbm, p_hbm, *rest):
    outs, (cols_ref, p_ref, sems) = rest[:2], rest[2:]
    rows, tile = p_ref.shape[:2]
    piece = rows // 2
    lists = pltpu.make_async_copy(cols_hbm, cols_ref, sems.at[rows])
    lists.start()
    loads = [pltpu.make_async_copy(p_hbm.at[f], p_ref.at[f], sems.at[f]) for f in range(rows)]
    for load in loads:
        load.start()
    lists.wait()
    for f in range(rows):
        loads[f].wait()
        first = pl.multiple_of(jnp.where(cols_ref[0, f] > cols_ref[1, f], tile, 0), tile)
        for t, start in ((0, first), (1, pl.multiple_of(tile - first, tile))):
            outs[f // piece][f % piece, :, t * tile : (t + 1) * tile] = p_ref[f, :, pl.ds(start, tile)]


def hand_out_kernel(subs, pool, near_ref, far_ref):
    rows = near_ref.shape[0]
    odd = lax.rem(lax.axis_index("dom"), 2)
    last = (subs - 1) * rows
    near_ref[...] = pool[pl.ds((1 - odd) * last, rows)]
    far_ref[...] = pool[pl.ds(odd * last, rows)]


def edge_kernel(subs, half, cols_ref, count_ref, pair_ref, a_hbm, own_0, own_1, *rest):
    out_ref, a_ref, turned, sems = rest
    rows, slots, tile = a_ref.shape[:3]
    first = lax.axis_index("dom") * (subs * rows)
    me = lax.axis_index("sub")
    loads = [pltpu.make_async_copy(a_hbm.at[f], a_ref.at[f], sems.at[f]) for f in range(rows)]
    for load in loads:
        load.start()
    out_ref[...] = jnp.zeros(out_ref.shape, F32)
    for f in range(rows):
        turned[f] = (own_0, own_1)[f // (rows // 2)][f % (rows // 2)].T
    for f in range(rows):
        loads[f].wait()
        for k in range(slots):
            rel = cols_ref[f, k] - first
            live = (k < count_ref[f]) & ((rel < 0) | (rel >= subs * rows))

            @pl.when(live)
            def _():
                at = jnp.where(rel < 0, rel + rows, rel - subs * rows + rows)
                term = jnp.dot(turned[f], a_ref[f, k], preferred_element_type=F32)
                if half == 1:
                    out_ref[at] += term
                else:
                    m = pair_ref[rows + me * rows + f]
                    for start, part in ((m, term[:tile]), (m + half, term[tile:])):
                        out_ref[at, pl.ds(pl.multiple_of(start * tile, tile), tile)] += part


def terms_kernel(subs, cols_ref, count_ref, a_hbm, own_0, own_1, *rest):
    edges, (high_ref, low_ref, a_ref, total, turned, sems) = rest[:subs], rest[subs:]
    rows, slots, tile = a_ref.shape[:3]
    tiles = total.shape[0] - 1
    me = lax.axis_index("sub")
    base = lax.axis_index("dom") * (subs * rows) - rows
    loads = [pltpu.make_async_copy(a_hbm.at[f], a_ref.at[f], sems.at[f]) for f in range(rows)]
    for load in loads:
        load.start()
    total[...] = jnp.zeros(total.shape, F32)
    for f in range(rows):
        turned[f] = (own_0, own_1)[f // (rows // 2)][f % (rows // 2)].T
    for f in range(rows):
        loads[f].wait()
        for k in range(slots):
            at = jnp.where(k < count_ref[f], cols_ref[f, k] - base, tiles)
            total[at] += jnp.dot(turned[f], a_ref[f, k], preferred_element_type=F32)
    for c in range(subs * rows):
        value = total[rows + c]
        high = value.astype(BF16)
        high_ref[c] = high
        low_ref[c] = (value - high.astype(F32)).astype(BF16)
    for k in range(subs):
        start = pl.multiple_of(lax.bitwise_xor(me, k) * COARSE_ROWS, COARSE_ROWS)
        for i, c in enumerate([*range(rows), *range(tiles - rows, tiles)]):
            part = total[c, pl.ds(start, COARSE_ROWS)]
            edges[k][:, i * tile : (i + 1) * tile] = part.astype(edges[k].dtype)
    k = subs - 1
    start = pl.multiple_of(lax.bitwise_xor(me, k) * COARSE_ROWS, COARSE_ROWS)
    for f in range(rows):
        part = total[rows + lax.bitwise_xor(me, k) * rows + f, pl.ds(start, COARSE_ROWS)]
        at = (2 * rows + f) * tile
        edges[k][:, at : at + tile] = part.astype(edges[k].dtype)


def terms_product(rows, sources, high_ref, low_ref, p_refs):
    me = lax.axis_index("sub")
    both = []
    for ref in (high_ref, low_ref):
        at = [lax.bitwise_xor(me, k) * rows + f for k in sources for f in range(rows)]
        both.append(jnp.concatenate([ref[i] for i in at], axis=1))
    stacked = jnp.concatenate([ref[i] for ref in p_refs for i in range(ref.shape[0])], axis=0)
    out = jnp.dot(jnp.concatenate(both, axis=0), stacked, preferred_element_type=F32)
    height = high_ref.shape[1]
    return out[:height] + out[height:]


def early_kernel(subs, rows, sources, high_ref, low_ref, edge_ref, *rest):
    p_refs, (out_ref, part_ref) = rest[:-2], rest[-2:]
    out_ref[...] = terms_product(rows, sources, high_ref, low_ref, p_refs)
    width = out_ref.shape[1]
    start = lax.bitwise_xor(lax.axis_index("sub"), subs - 1) * COARSE_ROWS
    at = pl.ds(pl.multiple_of(start, COARSE_ROWS), COARSE_ROWS)
    part_ref[:, :width] = out_ref[at].astype(BF16)
    part_ref[:, width:] = edge_ref[...]


def late_kernel(subs, rows, sources, high_ref, low_ref, early_ref, *rest):
    p_refs, rest = rest[: 2 * subs], rest[2 * subs :]
    edges, outs, (near_ref, far_ref, mid, ends) = rest[: subs - 1], rest[subs - 1 : -4], rest[-4:]
    width, piece = mid.shape[1], p_refs[0].shape[0]
    me, odd = lax.axis_index("sub"), lax.rem(lax.axis_index("dom"), 2)
    last = [p_refs[2 * k + i] for k in sources for i in range(2)]
    mid[...] = early_ref[...] + terms_product(rows, sources, high_ref, low_ref, last)
    for k in range(subs - 1):
        start = pl.multiple_of(lax.bitwise_xor(me, k) * COARSE_ROWS, COARSE_ROWS)
        outs[k][:, :width] = mid[pl.ds(start, COARSE_ROWS)].astype(outs[k].dtype)
        outs[k][:, width:] = edges[k][...]
    for k in range(subs):
        for at, who in ((0, 0), (rows, subs - 1)):

            @pl.when(me == who ^ k)
            def _():
                for i in range(2):
                    ends[at + i * piece : at + (i + 1) * piece] = p_refs[2 * k + i][...]

    near_ref[...] = ends[pl.ds((1 - odd) * rows, rows)]
    far_ref[...] = ends[pl.ds(odd * rows, rows)]


def group_kernel(subs, half, cols_ref, count_ref, pair_ref, a_ref, edge_ref, *rest):
    p_refs, rest = rest[: 2 * subs], rest[2 * subs :]
    outs, (pool, q, mid_ref) = rest[:subs], rest[subs:]
    rows, slots, tile = a_ref.shape[0], a_ref.shape[1], a_ref.shape[2]
    zero = subs * rows
    width = 2 * half * tile
    me = lax.axis_index("sub")
    first = lax.axis_index("dom") * (subs * rows)
    piece = rows // 2
    for k in range(subs):
        for i in range(2):
            pool[pl.ds(lax.bitwise_xor(me, k) * rows + i * piece, piece)] = p_refs[2 * k + i][...]
    pool[zero] = jnp.zeros(pool.shape[1:], pool.dtype)
    for f in range(rows):
        a_row = side_by_side(a_ref, f)
        index = [[None] * slots for _ in range(half)]
        for k in range(slots):
            rel = cols_ref[f, k] - first
            inside = (rel >= 0) & (rel < zero) & (k < count_ref[f])
            safe = jnp.where(inside, rel, 0)
            for m in range(half):
                here = inside if half == 1 else inside & (pair_ref[rows + safe] == m)
                index[m][k] = jnp.where(here, safe, zero)
        for m in range(half):
            block = placed_product(a_row, pool, index[m])
            lo, hi = m * tile, (m + half) * tile
            q[f * tile : (f + 1) * tile, lo : lo + tile] = block[:, :tile]
            q[f * tile : (f + 1) * tile, hi : hi + tile] = block[:, tile:]
    for m, out in enumerate(restrict(own_tiles(rows, zero, half, me, pair_ref, pool), q[...], half)):
        mid_ref[m * tile : (m + 1) * tile] = out[:tile]
        mid_ref[(m + half) * tile : (m + half + 1) * tile] = out[tile:]
    for k in range(subs):
        at = pl.ds(pl.multiple_of(lax.bitwise_xor(me, k) * COARSE_ROWS, COARSE_ROWS), COARSE_ROWS)
        kind = outs[k].dtype
        outs[k][:, :width] = mid_ref[at].astype(kind)
        for c in range(2 * rows):
            outs[k][:, width + c * tile : width + (c + 1) * tile] = edge_ref[c, at].astype(kind)


def sum_kernel(subs, width, *refs):
    part_refs, own_refs, (mid_ref, edge_ref, total_ref) = refs[:subs], refs[subs:-3], refs[-3:]
    span = total_ref.shape[1]
    total_ref[...] = part_refs[0][...]
    for part in part_refs[1:]:
        total_ref[...] += part[:, :span].astype(F32)
        if part.shape[1] > span:
            stacked = jnp.concatenate([ref[i] for ref in own_refs for i in range(ref.shape[0])], axis=0)
            total_ref[:, :width] += jnp.dot(part[:, span:], stacked, preferred_element_type=F32)
    total = total_ref[...]
    mid_ref[...] = total[:, :width].astype(BF16)
    sums = total[:, width:]
    high = sums.astype(BF16)
    edge_ref[:COARSE_ROWS] = high
    edge_ref[COARSE_ROWS:] = (sums - high.astype(F32)).astype(BF16)


def finish_kernel(subs, half, *refs):
    pair_ref = refs[0] if half > 1 else None
    far_ref, near_ref, mid_ref, both_ref, out_ref, edge = refs[-6:]
    rows, tile = near_ref.shape[:2]
    width = 2 * half * tile
    odd = lax.rem(lax.axis_index("dom"), 2)
    edge[pl.ds((1 - odd) * rows, rows)] = near_ref[...]
    edge[pl.ds(odd * rows, rows)] = far_ref[...]
    out_ref[:, width : 2 * width] = mid_ref[...]
    both = both_ref[...]
    for side in range(2):
        blocks = [jnp.zeros((COARSE_ROWS, tile), F32) for _ in range(2 * half)]
        tiles = range(side * rows, (side + 1) * rows)
        if half == 1:
            stacked = jnp.concatenate([edge[c] for c in tiles], axis=0)
            lhs = both[:, side * rows * tile : (side + 1) * rows * tile]
            term = jnp.dot(lhs, stacked, preferred_element_type=F32)
            term = term[:COARSE_ROWS] + term[COARSE_ROWS:]
            blocks = [term[:, :tile], term[:, tile:]]
        else:
            for c in tiles:
                lhs = both[:, c * tile : (c + 1) * tile]
                term = jnp.dot(lhs, edge[c], preferred_element_type=F32)
                term = term[:COARSE_ROWS] + term[COARSE_ROWS:]
                m_here = pair_ref[c if side == 0 else subs * rows + c]
                for m in range(half):
                    here = m_here == m
                    blocks[m] = blocks[m] + jnp.where(here, term[:, :tile], 0.0)
                    blocks[m + half] = blocks[m + half] + jnp.where(here, term[:, tile:], 0.0)
        for b in range(2 * half):
            at = 2 * side * width + b * tile
            out_ref[:, at : at + tile] = blocks[b].astype(BF16)


def narrow_parts(a_tiles, a_cols, a_count, own, tiles, span):
    rows, slots, tile = a_tiles.shape[:3]
    subs = lax.axis_size("sub")
    width = 2 * tile
    smem = pl.BlockSpec(memory_space=pltpu.SMEM)
    vmem = pl.BlockSpec(memory_space=pltpu.VMEM)
    kinds = [F32] + [BF16] * (subs - 1)
    spare = 3 << 20
    products = 2 * width * rows * tile * width
    *edges, high, low = pl.pallas_call(
        functools.partial(terms_kernel, subs),
        out_shape=[
            jax.ShapeDtypeStruct((COARSE_ROWS, span - width + (k == subs - 1) * rows * tile), kind)
            for k, kind in enumerate(kinds)
        ]
        + [jax.ShapeDtypeStruct((subs * rows, width, tile), BF16)] * 2,
        in_specs=[smem, smem, pl.BlockSpec(memory_space=pltpu.HBM), vmem, vmem],
        out_specs=[vmem] * (subs + 2),
        scratch_shapes=[
            pltpu.VMEM(a_tiles.shape, BF16),
            pltpu.VMEM(((subs + 2) * rows + 1, width, tile), F32),
            pltpu.VMEM((rows, width, tile), BF16),
            pltpu.SemaphoreType.DMA((rows,)),
        ],
        compiler_params=pltpu.CompilerParams(
            vmem_limit_bytes=2 * a_tiles.size + 4 * ((subs + 2) * rows + 1) * width * tile + spare
        ),
        cost_estimate=pl.CostEstimate(
            flops=1 << 31, bytes_accessed=2 * a_tiles.size, transcendentals=0
        ),
        name="terms",
    )(a_cols, a_count, pltpu.with_memory_space_constraint(a_tiles, pltpu.HBM), *own)
    first, last = list(range(subs - 1)), [subs - 1]
    early, farthest = pl.pallas_call(
        functools.partial(early_kernel, subs, rows, first),
        out_shape=[
            jax.ShapeDtypeStruct((width, width), F32),
            jax.ShapeDtypeStruct((COARSE_ROWS, span + rows * tile), BF16),
        ],
        in_specs=[vmem] * (3 + 2 * len(first)),
        out_specs=[vmem] * 2,
        compiler_params=pltpu.CompilerParams(vmem_limit_bytes=spare),
        cost_estimate=pl.CostEstimate(
            flops=2 * len(first) * products, bytes_accessed=1 << 20, transcendentals=0
        ),
        name="early_part",
    )(high, low, edges[-1], *[piece for k in first for piece in tiles[k]])
    *parts, near, far = pl.pallas_call(
        functools.partial(late_kernel, subs, rows, last),
        out_shape=[jax.ShapeDtypeStruct((COARSE_ROWS, span), kind) for kind in kinds[:-1]]
        + [jax.ShapeDtypeStruct((rows, tile, width), BF16)] * 2,
        in_specs=[vmem] * (2 + 3 * subs),
        out_specs=[vmem] * (subs + 1),
        scratch_shapes=[
            pltpu.VMEM((width, width), F32),
            pltpu.VMEM((2 * rows, tile, width), BF16),
        ],
        compiler_params=pltpu.CompilerParams(vmem_limit_bytes=spare),
        cost_estimate=pl.CostEstimate(
            flops=2 * products, bytes_accessed=1 << 20, transcendentals=0
        ),
        name="late_part",
    )(high, low, early, *[piece for pieces in tiles for piece in pieces], *edges[:-1])
    return [*parts, farthest, near, far]


def local(a_tiles, a_cols, a_count, p_tiles, p_cols):
    rows, slots, tile = a_tiles.shape[:3]
    subs, doms = lax.axis_size("sub"), lax.axis_size("dom")
    coarse_group = subs * COARSE_ROWS // tile
    half = coarse_group // 2
    width = coarse_group * tile
    group_tiles = rows * subs

    smem = pl.BlockSpec(memory_space=pltpu.SMEM)
    vmem = pl.BlockSpec(memory_space=pltpu.VMEM)
    p_bytes = rows * tile * 2 * tile * 2
    a_bytes = a_tiles.size * 2
    spare = 3 << 20

    def exchange(value, k):
        return lax.ppermute(value, "sub", [(s, s ^ k) for s in range(subs)])

    own = pl.pallas_call(
        order_kernel,
        out_shape=[jax.ShapeDtypeStruct((rows // 2, tile, 2 * tile), BF16)] * 2,
        in_specs=[pl.BlockSpec(memory_space=pltpu.HBM)] * 2,
        out_specs=[vmem] * 2,
        scratch_shapes=[
            pltpu.SMEM((2, rows), jnp.int32),
            pltpu.VMEM(p_tiles.shape, BF16),
            pltpu.SemaphoreType.DMA((rows + 1,)),
        ],
        compiler_params=pltpu.CompilerParams(vmem_limit_bytes=spare),
        cost_estimate=pl.CostEstimate(
            flops=1 << 30, bytes_accessed=2 * p_bytes, transcendentals=0
        ),
        name="order_columns",
    )(
        pltpu.with_memory_space_constraint(p_cols.T, pltpu.HBM),
        pltpu.with_memory_space_constraint(p_tiles, pltpu.HBM),
    )

    tiles = [list(own)] + [[None, None] for _ in range(subs - 1)]
    for k in range(1, subs):
        low, high = k & -k, 1 << (k.bit_length() - 1)
        tiles[k][0] = exchange(tiles[k ^ low][0], low)
        tiles[k][1] = exchange(tiles[k ^ high][1], high)
    span = width + 2 * rows * tile
    pairs = []
    if half > 1:
        m_own = jnp.min(p_cols, axis=1) - lax.axis_index("dom") * coarse_group
        m_group = lax.all_gather(m_own, "sub", axis=0, tiled=True)
        m_left = lax.ppermute(
            m_group[group_tiles - rows :], "dom", [(d, d + 1) for d in range(doms - 1)]
        )
        m_right = lax.ppermute(m_group[:rows], "dom", [(d + 1, d) for d in range(doms - 1)])
        pair = jnp.concatenate([m_left, m_group, m_right])
        pairs = [pair]

    flat = [piece for pieces in tiles for piece in pieces]
    if half == 1:
        *parts, to_near, to_far = narrow_parts(a_tiles, a_cols, a_count, own, tiles, span)
    else:
        flops = 2 * rows * slots * tile * tile * 2 * tile * half
        edges, a_held = pl.pallas_call(
            functools.partial(edge_kernel, subs, half),
            out_shape=[
                jax.ShapeDtypeStruct((2 * rows, width, tile), F32),
                jax.ShapeDtypeStruct(a_tiles.shape, BF16),
            ],
            in_specs=[smem, smem, smem, pl.BlockSpec(memory_space=pltpu.HBM), vmem, vmem],
            out_specs=[vmem] * 2,
            scratch_shapes=[
                pltpu.VMEM((rows, 2 * tile, tile), BF16),
                pltpu.SemaphoreType.DMA((rows,)),
            ],
            compiler_params=pltpu.CompilerParams(vmem_limit_bytes=8 * rows * tile * width + spare),
            cost_estimate=pl.CostEstimate(
                flops=flops, bytes_accessed=a_bytes + p_bytes, transcendentals=0
            ),
            name="edge_part",
        )(a_cols, a_count, pair, pltpu.with_memory_space_constraint(a_tiles, pltpu.HBM), *own)

        *parts, pool = pl.pallas_call(
            functools.partial(group_kernel, subs, half),
            out_shape=[
                jax.ShapeDtypeStruct((COARSE_ROWS, span), F32 if k == 0 else BF16)
                for k in range(subs)
            ]
            + [jax.ShapeDtypeStruct((group_tiles + 1, tile, 2 * tile), BF16)],
            in_specs=[smem, smem, smem] + [vmem] * (2 * subs + 2),
            out_specs=[vmem] * (subs + 1),
            scratch_shapes=[
                pltpu.VMEM((rows * tile, width), BF16),
                pltpu.VMEM((width, width), F32),
            ],
            compiler_params=pltpu.CompilerParams(
                vmem_limit_bytes=2 * rows * tile * width + 4 * width * width + spare
            ),
            cost_estimate=pl.CostEstimate(
                flops=flops, bytes_accessed=a_bytes + subs * p_bytes, transcendentals=0
            ),
            name="group_part",
        )(a_cols, a_count, pair, a_held, edges, *flat)
        to_near, to_far = pl.pallas_call(
            functools.partial(hand_out_kernel, subs),
            out_shape=[jax.ShapeDtypeStruct(p_tiles.shape, BF16)] * 2,
            in_specs=[vmem],
            out_specs=[vmem] * 2,
            compiler_params=pltpu.CompilerParams(vmem_limit_bytes=spare),
            name="hand_out",
        )(pool)
    received = [exchange(parts[k], k) for k in range(subs - 1, 0, -1)]
    far = lax.ppermute(
        to_far, "dom", [(d, d - 1 + 2 * (d % 2)) for d in range(1, doms - 1)]
    )
    near = lax.ppermute(to_near, "dom", [(d, d ^ 1) for d in range(doms)])
    mid, both = pl.pallas_call(
        functools.partial(sum_kernel, subs, width),
        out_shape=[
            jax.ShapeDtypeStruct((COARSE_ROWS, width), BF16),
            jax.ShapeDtypeStruct((2 * COARSE_ROWS, span - width), BF16),
        ],
        in_specs=[vmem] * (subs + len(own)),
        out_specs=[vmem] * 2,
        scratch_shapes=[pltpu.VMEM((COARSE_ROWS, span), F32)],
        compiler_params=pltpu.CompilerParams(vmem_limit_bytes=spare),
        cost_estimate=pl.CostEstimate(
            flops=1 << 31, bytes_accessed=8 * COARSE_ROWS * span, transcendentals=0
        ),
        name="sum_parts",
    )(parts[0], *received, *own)
    return pl.pallas_call(
        functools.partial(finish_kernel, subs, half),
        out_shape=jax.ShapeDtypeStruct((COARSE_ROWS, 3 * width), BF16),
        in_specs=[smem] * len(pairs) + [vmem] * 4,
        out_specs=vmem,
        scratch_shapes=[pltpu.VMEM((2 * rows, tile, 2 * tile), BF16)],
        compiler_params=pltpu.CompilerParams(vmem_limit_bytes=2 * p_bytes + spare),
        cost_estimate=pl.CostEstimate(
            flops=1 << 28, bytes_accessed=4 * p_bytes, transcendentals=0
        ),
        name="finish",
    )(*pairs, far, near, mid, both)


def solution(mesh):
    placed = (
        P(("dom", "sub"), None, None, None),
        P(("dom", "sub"), None),
        P(("dom", "sub")),
        P(("dom", "sub"), None, None),
        P(("dom", "sub"), None),
    )
    return jax.shard_map(
        local, mesh=mesh, in_specs=placed, out_specs=P(("dom", "sub"), None), check_vma=False
    )
```

```python
import functools

import jax
import jax.numpy as jnp
from jax import lax
from jax.experimental import pallas as pl
from jax.experimental.pallas import tpu as pltpu
from jax.sharding import PartitionSpec as P

COARSE_ROWS = 64
BF16 = jnp.bfloat16
F32 = jnp.float32


def side_by_side(a_ref, f):
    return jnp.concatenate([a_ref[f, k] for k in range(a_ref.shape[1])], axis=1)


def placed_product(a_row, pool, index):
    stacked = jnp.concatenate([pool[i] for i in index], axis=0)
    return jnp.dot(a_row, stacked, preferred_element_type=F32).astype(BF16)


def own_tiles(rows, zero, half, me, pair_ref, pool):
    tiles = []
    for m in range(half):
        at = [me * rows + f for f in range(rows)]
        if half > 1:
            at = [jnp.where(pair_ref[rows + i] == m, i, zero) for i in at]
        tiles.append([pool[i] for i in at])
    return tiles


def restrict(tiles, q, half):
    outs = []
    for m in range(half):
        lhs = jnp.concatenate(tiles[m], axis=0)
        outs.append(
            lax.dot_general(lhs, q, (((0,), (0,)), ((), ())), preferred_element_type=F32)
        )
    return outs


def order_kernel(cols_hbm, p_hbm, *rest):
    outs, (cols_ref, p_ref, sems) = rest[:2], rest[2:]
    rows, tile = p_ref.shape[:2]
    piece = rows // 2
    lists = pltpu.make_async_copy(cols_hbm, cols_ref, sems.at[rows])
    lists.start()
    loads = [pltpu.make_async_copy(p_hbm.at[f], p_ref.at[f], sems.at[f]) for f in range(rows)]
    for load in loads:
        load.start()
    lists.wait()
    for f in range(rows):
        loads[f].wait()
        first = pl.multiple_of(jnp.where(cols_ref[0, f] > cols_ref[1, f], tile, 0), tile)
        for t, start in ((0, first), (1, pl.multiple_of(tile - first, tile))):
            outs[f // piece][f % piece, :, t * tile : (t + 1) * tile] = p_ref[f, :, pl.ds(start, tile)]


def hand_out_kernel(subs, pool, near_ref, far_ref):
    rows = near_ref.shape[0]
    odd = lax.rem(lax.axis_index("dom"), 2)
    last = (subs - 1) * rows
    near_ref[...] = pool[pl.ds((1 - odd) * last, rows)]
    far_ref[...] = pool[pl.ds(odd * last, rows)]


def edge_kernel(subs, half, cols_ref, count_ref, pair_ref, a_hbm, own_0, own_1, *rest):
    out_ref, a_ref, turned, sems = rest
    rows, slots, tile = a_ref.shape[:3]
    first = lax.axis_index("dom") * (subs * rows)
    me = lax.axis_index("sub")
    loads = [pltpu.make_async_copy(a_hbm.at[f], a_ref.at[f], sems.at[f]) for f in range(rows)]
    for load in loads:
        load.start()
    out_ref[...] = jnp.zeros(out_ref.shape, F32)
    for f in range(rows):
        turned[f] = (own_0, own_1)[f // (rows // 2)][f % (rows // 2)].T
    for f in range(rows):
        loads[f].wait()
        for k in range(slots):
            rel = cols_ref[f, k] - first
            live = (k < count_ref[f]) & ((rel < 0) | (rel >= subs * rows))

            @pl.when(live)
            def _():
                at = jnp.where(rel < 0, rel + rows, rel - subs * rows + rows)
                term = jnp.dot(turned[f], a_ref[f, k], preferred_element_type=F32)
                if half == 1:
                    out_ref[at] += term
                else:
                    m = pair_ref[rows + me * rows + f]
                    for start, part in ((m, term[:tile]), (m + half, term[tile:])):
                        out_ref[at, pl.ds(pl.multiple_of(start * tile, tile), tile)] += part


def terms_kernel(subs, cols_ref, count_ref, a_hbm, own_0, own_1, *rest):
    edges, (high_ref, low_ref, a_ref, total, turned, sems) = rest[:subs], rest[subs:]
    rows, slots, tile = a_ref.shape[:3]
    tiles = total.shape[0] - 1
    me = lax.axis_index("sub")
    base = lax.axis_index("dom") * (subs * rows) - rows
    loads = [pltpu.make_async_copy(a_hbm.at[f], a_ref.at[f], sems.at[f]) for f in range(rows)]
    for load in loads:
        load.start()
    total[...] = jnp.zeros(total.shape, F32)
    for f in range(rows):
        turned[f] = (own_0, own_1)[f // (rows // 2)][f % (rows // 2)].T
    for f in range(rows):
        loads[f].wait()
        for k in range(0, slots, 2):
            pair = range(k, min(k + 2, slots))
            side = jnp.concatenate([a_ref[f, i] for i in pair], axis=1)
            terms = jnp.dot(turned[f], side, preferred_element_type=F32)
            for i in pair:
                at = jnp.where(i < count_ref[f], cols_ref[f, i] - base, tiles)
                total[at] += terms[:, (i - k) * tile : (i - k + 1) * tile]
    for c in range(subs * rows):
        value = total[rows + c]
        high = value.astype(BF16)
        high_ref[c] = high
        low_ref[c] = (value - high.astype(F32)).astype(BF16)
    for k in range(subs):
        start = pl.multiple_of(lax.bitwise_xor(me, k) * COARSE_ROWS, COARSE_ROWS)
        for i, c in enumerate([*range(rows), *range(tiles - rows, tiles)]):
            part = total[c, pl.ds(start, COARSE_ROWS)]
            edges[k][:, i * tile : (i + 1) * tile] = part.astype(edges[k].dtype)
    k = subs - 1
    start = pl.multiple_of(lax.bitwise_xor(me, k) * COARSE_ROWS, COARSE_ROWS)
    for f in range(rows):
        part = total[rows + lax.bitwise_xor(me, k) * rows + f, pl.ds(start, COARSE_ROWS)]
        at = (2 * rows + f) * tile
        edges[k][:, at : at + tile] = part.astype(edges[k].dtype)


def terms_product(rows, sources, high_ref, low_ref, p_refs):
    me = lax.axis_index("sub")
    both = []
    for ref in (high_ref, low_ref):
        at = [lax.bitwise_xor(me, k) * rows + f for k in sources for f in range(rows)]
        both.append(jnp.concatenate([ref[i] for i in at], axis=1))
    stacked = jnp.concatenate([ref[i] for ref in p_refs for i in range(ref.shape[0])], axis=0)
    out = jnp.dot(jnp.concatenate(both, axis=0), stacked, preferred_element_type=F32)
    height = high_ref.shape[1]
    return out[:height] + out[height:]


def early_kernel(subs, rows, sources, high_ref, low_ref, edge_ref, *rest):
    p_refs, (out_ref, part_ref) = rest[:-2], rest[-2:]
    out_ref[...] = terms_product(rows, sources, high_ref, low_ref, p_refs)
    width = out_ref.shape[1]
    start = lax.bitwise_xor(lax.axis_index("sub"), subs - 1) * COARSE_ROWS
    at = pl.ds(pl.multiple_of(start, COARSE_ROWS), COARSE_ROWS)
    part_ref[:, :width] = out_ref[at].astype(BF16)
    part_ref[:, width:] = edge_ref[...]


def late_kernel(subs, rows, sources, high_ref, low_ref, early_ref, *rest):
    p_refs, rest = rest[: 2 * subs], rest[2 * subs :]
    edges, outs, (near_ref, far_ref, mid, ends) = rest[: subs - 1], rest[subs - 1 : -4], rest[-4:]
    width, piece = mid.shape[1], p_refs[0].shape[0]
    me, odd = lax.axis_index("sub"), lax.rem(lax.axis_index("dom"), 2)
    last = [p_refs[2 * k + i] for k in sources for i in range(2)]
    mid[...] = early_ref[...] + terms_product(rows, sources, high_ref, low_ref, last)
    for k in range(subs - 1):
        start = pl.multiple_of(lax.bitwise_xor(me, k) * COARSE_ROWS, COARSE_ROWS)
        outs[k][:, :width] = mid[pl.ds(start, COARSE_ROWS)].astype(outs[k].dtype)
        outs[k][:, width:] = edges[k][...]
    for k in range(subs):
        for at, who in ((0, 0), (rows, subs - 1)):

            @pl.when(me == who ^ k)
            def _():
                for i in range(2):
                    ends[at + i * piece : at + (i + 1) * piece] = p_refs[2 * k + i][...]

    near_ref[...] = ends[pl.ds((1 - odd) * rows, rows)]
    far_ref[...] = ends[pl.ds(odd * rows, rows)]


def group_kernel(subs, half, cols_ref, count_ref, pair_ref, a_ref, edge_ref, *rest):
    p_refs, rest = rest[: 2 * subs], rest[2 * subs :]
    outs, (pool, q, mid_ref) = rest[:subs], rest[subs:]
    rows, slots, tile = a_ref.shape[0], a_ref.shape[1], a_ref.shape[2]
    zero = subs * rows
    width = 2 * half * tile
    me = lax.axis_index("sub")
    first = lax.axis_index("dom") * (subs * rows)
    piece = rows // 2
    for k in range(subs):
        for i in range(2):
            pool[pl.ds(lax.bitwise_xor(me, k) * rows + i * piece, piece)] = p_refs[2 * k + i][...]
    pool[zero] = jnp.zeros(pool.shape[1:], pool.dtype)
    for f in range(rows):
        a_row = side_by_side(a_ref, f)
        index = [[None] * slots for _ in range(half)]
        for k in range(slots):
            rel = cols_ref[f, k] - first
            inside = (rel >= 0) & (rel < zero) & (k < count_ref[f])
            safe = jnp.where(inside, rel, 0)
            for m in range(half):
                here = inside if half == 1 else inside & (pair_ref[rows + safe] == m)
                index[m][k] = jnp.where(here, safe, zero)
        for m in range(half):
            block = placed_product(a_row, pool, index[m])
            lo, hi = m * tile, (m + half) * tile
            q[f * tile : (f + 1) * tile, lo : lo + tile] = block[:, :tile]
            q[f * tile : (f + 1) * tile, hi : hi + tile] = block[:, tile:]
    for m, out in enumerate(restrict(own_tiles(rows, zero, half, me, pair_ref, pool), q[...], half)):
        mid_ref[m * tile : (m + 1) * tile] = out[:tile]
        mid_ref[(m + half) * tile : (m + half + 1) * tile] = out[tile:]
    for k in range(subs):
        at = pl.ds(pl.multiple_of(lax.bitwise_xor(me, k) * COARSE_ROWS, COARSE_ROWS), COARSE_ROWS)
        kind = outs[k].dtype
        outs[k][:, :width] = mid_ref[at].astype(kind)
        for c in range(2 * rows):
            outs[k][:, width + c * tile : width + (c + 1) * tile] = edge_ref[c, at].astype(kind)


def sum_kernel(subs, width, *refs):
    part_refs, own_refs, (mid_ref, edge_ref, total_ref) = refs[:subs], refs[subs:-3], refs[-3:]
    span = total_ref.shape[1]
    total_ref[...] = part_refs[0][...]
    for part in part_refs[1:]:
        total_ref[...] += part[:, :span].astype(F32)
        if part.shape[1] > span:
            stacked = jnp.concatenate([ref[i] for ref in own_refs for i in range(ref.shape[0])], axis=0)
            total_ref[:, :width] += jnp.dot(part[:, span:], stacked, preferred_element_type=F32)
    total = total_ref[...]
    mid_ref[...] = total[:, :width].astype(BF16)
    sums = total[:, width:]
    high = sums.astype(BF16)
    edge_ref[:COARSE_ROWS] = high
    edge_ref[COARSE_ROWS:] = (sums - high.astype(F32)).astype(BF16)


def finish_kernel(subs, half, *refs):
    pair_ref = refs[0] if half > 1 else None
    far_ref, near_ref, mid_ref, both_ref, out_ref, edge = refs[-6:]
    rows, tile = near_ref.shape[:2]
    width = 2 * half * tile
    odd = lax.rem(lax.axis_index("dom"), 2)
    edge[pl.ds((1 - odd) * rows, rows)] = near_ref[...]
    edge[pl.ds(odd * rows, rows)] = far_ref[...]
    out_ref[:, width : 2 * width] = mid_ref[...]
    both = both_ref[...]
    for side in range(2):
        blocks = [jnp.zeros((COARSE_ROWS, tile), F32) for _ in range(2 * half)]
        tiles = range(side * rows, (side + 1) * rows)
        if half == 1:
            stacked = jnp.concatenate([edge[c] for c in tiles], axis=0)
            lhs = both[:, side * rows * tile : (side + 1) * rows * tile]
            term = jnp.dot(lhs, stacked, preferred_element_type=F32)
            term = term[:COARSE_ROWS] + term[COARSE_ROWS:]
            blocks = [term[:, :tile], term[:, tile:]]
        else:
            for c in tiles:
                lhs = both[:, c * tile : (c + 1) * tile]
                term = jnp.dot(lhs, edge[c], preferred_element_type=F32)
                term = term[:COARSE_ROWS] + term[COARSE_ROWS:]
                m_here = pair_ref[c if side == 0 else subs * rows + c]
                for m in range(half):
                    here = m_here == m
                    blocks[m] = blocks[m] + jnp.where(here, term[:, :tile], 0.0)
                    blocks[m + half] = blocks[m + half] + jnp.where(here, term[:, tile:], 0.0)
        for b in range(2 * half):
            at = 2 * side * width + b * tile
            out_ref[:, at : at + tile] = blocks[b].astype(BF16)


def narrow_parts(a_tiles, a_cols, a_count, own, tiles, span):
    rows, slots, tile = a_tiles.shape[:3]
    subs = lax.axis_size("sub")
    width = 2 * tile
    smem = pl.BlockSpec(memory_space=pltpu.SMEM)
    vmem = pl.BlockSpec(memory_space=pltpu.VMEM)
    kinds = [F32] + [BF16] * (subs - 1)
    spare = 3 << 20
    products = 2 * width * rows * tile * width
    *edges, high, low = pl.pallas_call(
        functools.partial(terms_kernel, subs),
        out_shape=[
            jax.ShapeDtypeStruct((COARSE_ROWS, span - width + (k == subs - 1) * rows * tile), kind)
            for k, kind in enumerate(kinds)
        ]
        + [jax.ShapeDtypeStruct((subs * rows, width, tile), BF16)] * 2,
        in_specs=[smem, smem, pl.BlockSpec(memory_space=pltpu.HBM), vmem, vmem],
        out_specs=[vmem] * (subs + 2),
        scratch_shapes=[
            pltpu.VMEM(a_tiles.shape, BF16),
            pltpu.VMEM(((subs + 2) * rows + 1, width, tile), F32),
            pltpu.VMEM((rows, width, tile), BF16),
            pltpu.SemaphoreType.DMA((rows,)),
        ],
        compiler_params=pltpu.CompilerParams(
            vmem_limit_bytes=2 * a_tiles.size + 4 * ((subs + 2) * rows + 1) * width * tile + spare
        ),
        cost_estimate=pl.CostEstimate(
            flops=1 << 31, bytes_accessed=2 * a_tiles.size, transcendentals=0
        ),
        name="terms",
    )(a_cols, a_count, pltpu.with_memory_space_constraint(a_tiles, pltpu.HBM), *own)
    first, last = list(range(subs - 1)), [subs - 1]
    early, farthest = pl.pallas_call(
        functools.partial(early_kernel, subs, rows, first),
        out_shape=[
            jax.ShapeDtypeStruct((width, width), F32),
            jax.ShapeDtypeStruct((COARSE_ROWS, span + rows * tile), BF16),
        ],
        in_specs=[vmem] * (3 + 2 * len(first)),
        out_specs=[vmem] * 2,
        compiler_params=pltpu.CompilerParams(vmem_limit_bytes=spare),
        cost_estimate=pl.CostEstimate(
            flops=2 * len(first) * products, bytes_accessed=1 << 20, transcendentals=0
        ),
        name="early_part",
    )(high, low, edges[-1], *[piece for k in first for piece in tiles[k]])
    *parts, near, far = pl.pallas_call(
        functools.partial(late_kernel, subs, rows, last),
        out_shape=[jax.ShapeDtypeStruct((COARSE_ROWS, span), kind) for kind in kinds[:-1]]
        + [jax.ShapeDtypeStruct((rows, tile, width), BF16)] * 2,
        in_specs=[vmem] * (2 + 3 * subs),
        out_specs=[vmem] * (subs + 1),
        scratch_shapes=[
            pltpu.VMEM((width, width), F32),
            pltpu.VMEM((2 * rows, tile, width), BF16),
        ],
        compiler_params=pltpu.CompilerParams(vmem_limit_bytes=spare),
        cost_estimate=pl.CostEstimate(
            flops=2 * products, bytes_accessed=1 << 20, transcendentals=0
        ),
        name="late_part",
    )(high, low, early, *[piece for pieces in tiles for piece in pieces], *edges[:-1])
    return [*parts, farthest, near, far]


def local(a_tiles, a_cols, a_count, p_tiles, p_cols):
    rows, slots, tile = a_tiles.shape[:3]
    subs, doms = lax.axis_size("sub"), lax.axis_size("dom")
    coarse_group = subs * COARSE_ROWS // tile
    half = coarse_group // 2
    width = coarse_group * tile
    group_tiles = rows * subs

    smem = pl.BlockSpec(memory_space=pltpu.SMEM)
    vmem = pl.BlockSpec(memory_space=pltpu.VMEM)
    p_bytes = rows * tile * 2 * tile * 2
    a_bytes = a_tiles.size * 2
    spare = 3 << 20

    def exchange(value, k):
        return lax.ppermute(value, "sub", [(s, s ^ k) for s in range(subs)])

    own = pl.pallas_call(
        order_kernel,
        out_shape=[jax.ShapeDtypeStruct((rows // 2, tile, 2 * tile), BF16)] * 2,
        in_specs=[pl.BlockSpec(memory_space=pltpu.HBM)] * 2,
        out_specs=[vmem] * 2,
        scratch_shapes=[
            pltpu.SMEM((2, rows), jnp.int32),
            pltpu.VMEM(p_tiles.shape, BF16),
            pltpu.SemaphoreType.DMA((rows + 1,)),
        ],
        compiler_params=pltpu.CompilerParams(vmem_limit_bytes=spare),
        cost_estimate=pl.CostEstimate(
            flops=1 << 30, bytes_accessed=2 * p_bytes, transcendentals=0
        ),
        name="order_columns",
    )(
        pltpu.with_memory_space_constraint(p_cols.T, pltpu.HBM),
        pltpu.with_memory_space_constraint(p_tiles, pltpu.HBM),
    )

    tiles = [list(own)] + [[None, None] for _ in range(subs - 1)]
    for k in range(1, subs):
        low, high = k & -k, 1 << (k.bit_length() - 1)
        tiles[k][0] = exchange(tiles[k ^ low][0], low)
        tiles[k][1] = exchange(tiles[k ^ high][1], high)
    span = width + 2 * rows * tile
    pairs = []
    if half > 1:
        m_own = jnp.min(p_cols, axis=1) - lax.axis_index("dom") * coarse_group
        m_group = lax.all_gather(m_own, "sub", axis=0, tiled=True)
        m_left = lax.ppermute(
            m_group[group_tiles - rows :], "dom", [(d, d + 1) for d in range(doms - 1)]
        )
        m_right = lax.ppermute(m_group[:rows], "dom", [(d + 1, d) for d in range(doms - 1)])
        pair = jnp.concatenate([m_left, m_group, m_right])
        pairs = [pair]

    flat = [piece for pieces in tiles for piece in pieces]
    if half == 1:
        *parts, to_near, to_far = narrow_parts(a_tiles, a_cols, a_count, own, tiles, span)
    else:
        flops = 2 * rows * slots * tile * tile * 2 * tile * half
        edges, a_held = pl.pallas_call(
            functools.partial(edge_kernel, subs, half),
            out_shape=[
                jax.ShapeDtypeStruct((2 * rows, width, tile), F32),
                jax.ShapeDtypeStruct(a_tiles.shape, BF16),
            ],
            in_specs=[smem, smem, smem, pl.BlockSpec(memory_space=pltpu.HBM), vmem, vmem],
            out_specs=[vmem] * 2,
            scratch_shapes=[
                pltpu.VMEM((rows, 2 * tile, tile), BF16),
                pltpu.SemaphoreType.DMA((rows,)),
            ],
            compiler_params=pltpu.CompilerParams(vmem_limit_bytes=8 * rows * tile * width + spare),
            cost_estimate=pl.CostEstimate(
                flops=flops, bytes_accessed=a_bytes + p_bytes, transcendentals=0
            ),
            name="edge_part",
        )(a_cols, a_count, pair, pltpu.with_memory_space_constraint(a_tiles, pltpu.HBM), *own)

        *parts, pool = pl.pallas_call(
            functools.partial(group_kernel, subs, half),
            out_shape=[
                jax.ShapeDtypeStruct((COARSE_ROWS, span), F32 if k == 0 else BF16)
                for k in range(subs)
            ]
            + [jax.ShapeDtypeStruct((group_tiles + 1, tile, 2 * tile), BF16)],
            in_specs=[smem, smem, smem] + [vmem] * (2 * subs + 2),
            out_specs=[vmem] * (subs + 1),
            scratch_shapes=[
                pltpu.VMEM((rows * tile, width), BF16),
                pltpu.VMEM((width, width), F32),
            ],
            compiler_params=pltpu.CompilerParams(
                vmem_limit_bytes=2 * rows * tile * width + 4 * width * width + spare
            ),
            cost_estimate=pl.CostEstimate(
                flops=flops, bytes_accessed=a_bytes + subs * p_bytes, transcendentals=0
            ),
            name="group_part",
        )(a_cols, a_count, pair, a_held, edges, *flat)
        to_near, to_far = pl.pallas_call(
            functools.partial(hand_out_kernel, subs),
            out_shape=[jax.ShapeDtypeStruct(p_tiles.shape, BF16)] * 2,
            in_specs=[vmem],
            out_specs=[vmem] * 2,
            compiler_params=pltpu.CompilerParams(vmem_limit_bytes=spare),
            name="hand_out",
        )(pool)
    received = [exchange(parts[k], k) for k in range(subs - 1, 0, -1)]
    far = lax.ppermute(
        to_far, "dom", [(d, d - 1 + 2 * (d % 2)) for d in range(1, doms - 1)]
    )
    near = lax.ppermute(to_near, "dom", [(d, d ^ 1) for d in range(doms)])
    mid, both = pl.pallas_call(
        functools.partial(sum_kernel, subs, width),
        out_shape=[
            jax.ShapeDtypeStruct((COARSE_ROWS, width), BF16),
            jax.ShapeDtypeStruct((2 * COARSE_ROWS, span - width), BF16),
        ],
        in_specs=[vmem] * (subs + len(own)),
        out_specs=[vmem] * 2,
        scratch_shapes=[pltpu.VMEM((COARSE_ROWS, span), F32)],
        compiler_params=pltpu.CompilerParams(vmem_limit_bytes=spare),
        cost_estimate=pl.CostEstimate(
            flops=1 << 31, bytes_accessed=8 * COARSE_ROWS * span, transcendentals=0
        ),
        name="sum_parts",
    )(parts[0], *received, *own)
    return pl.pallas_call(
        functools.partial(finish_kernel, subs, half),
        out_shape=jax.ShapeDtypeStruct((COARSE_ROWS, 3 * width), BF16),
        in_specs=[smem] * len(pairs) + [vmem] * 4,
        out_specs=vmem,
        scratch_shapes=[pltpu.VMEM((2 * rows, tile, 2 * tile), BF16)],
        compiler_params=pltpu.CompilerParams(vmem_limit_bytes=2 * p_bytes + spare),
        cost_estimate=pl.CostEstimate(
            flops=1 << 28, bytes_accessed=4 * p_bytes, transcendentals=0
        ),
        name="finish",
    )(*pairs, far, near, mid, both)


def solution(mesh):
    placed = (
        P(("dom", "sub"), None, None, None),
        P(("dom", "sub"), None),
        P(("dom", "sub")),
        P(("dom", "sub"), None, None),
        P(("dom", "sub"), None),
    )
    return jax.shard_map(
        local, mesh=mesh, in_specs=placed, out_specs=P(("dom", "sub"), None), check_vma=False
    )
```

```python
import functools

import jax
import jax.numpy as jnp
from jax import lax
from jax.experimental import pallas as pl
from jax.experimental.pallas import tpu as pltpu
from jax.sharding import PartitionSpec as P

COARSE_ROWS = 64
BF16 = jnp.bfloat16
F32 = jnp.float32


def side_by_side(a_ref, f):
    return jnp.concatenate([a_ref[f, k] for k in range(a_ref.shape[1])], axis=1)


def placed_product(a_row, pool, index):
    stacked = jnp.concatenate([pool[i] for i in index], axis=0)
    return jnp.dot(a_row, stacked, preferred_element_type=F32).astype(BF16)


def own_tiles(rows, zero, half, me, pair_ref, pool):
    tiles = []
    for m in range(half):
        at = [me * rows + f for f in range(rows)]
        if half > 1:
            at = [jnp.where(pair_ref[rows + i] == m, i, zero) for i in at]
        tiles.append([pool[i] for i in at])
    return tiles


def restrict(tiles, q, half):
    outs = []
    for m in range(half):
        lhs = jnp.concatenate(tiles[m], axis=0)
        outs.append(
            lax.dot_general(lhs, q, (((0,), (0,)), ((), ())), preferred_element_type=F32)
        )
    return outs


def order_kernel(cols_hbm, p_hbm, *rest):
    outs, (cols_ref, p_ref, sems) = rest[:2], rest[2:]
    rows, tile = p_ref.shape[:2]
    piece = rows // 2
    lists = pltpu.make_async_copy(cols_hbm, cols_ref, sems.at[rows])
    lists.start()
    loads = [pltpu.make_async_copy(p_hbm.at[f], p_ref.at[f], sems.at[f]) for f in range(rows)]
    for load in loads:
        load.start()
    lists.wait()
    for f in range(rows):
        loads[f].wait()
        first = pl.multiple_of(jnp.where(cols_ref[0, f] > cols_ref[1, f], tile, 0), tile)
        for t, start in ((0, first), (1, pl.multiple_of(tile - first, tile))):
            outs[f // piece][f % piece, :, t * tile : (t + 1) * tile] = p_ref[f, :, pl.ds(start, tile)]


def hand_out_kernel(subs, pool, near_ref, far_ref):
    rows = near_ref.shape[0]
    odd = lax.rem(lax.axis_index("dom"), 2)
    last = (subs - 1) * rows
    near_ref[...] = pool[pl.ds((1 - odd) * last, rows)]
    far_ref[...] = pool[pl.ds(odd * last, rows)]


def edge_kernel(subs, half, cols_ref, count_ref, pair_ref, a_hbm, own_0, own_1, *rest):
    out_ref, a_ref, turned, sems = rest
    rows, slots, tile = a_ref.shape[:3]
    first = lax.axis_index("dom") * (subs * rows)
    me = lax.axis_index("sub")
    loads = [pltpu.make_async_copy(a_hbm.at[f], a_ref.at[f], sems.at[f]) for f in range(rows)]
    for load in loads:
        load.start()
    out_ref[...] = jnp.zeros(out_ref.shape, F32)
    for f in range(rows):
        turned[f] = (own_0, own_1)[f // (rows // 2)][f % (rows // 2)].T
    for f in range(rows):
        loads[f].wait()
        for k in range(slots):
            rel = cols_ref[f, k] - first
            live = (k < count_ref[f]) & ((rel < 0) | (rel >= subs * rows))

            @pl.when(live)
            def _():
                at = jnp.where(rel < 0, rel + rows, rel - subs * rows + rows)
                term = jnp.dot(turned[f], a_ref[f, k], preferred_element_type=F32)
                if half == 1:
                    out_ref[at] += term
                else:
                    m = pair_ref[rows + me * rows + f]
                    for start, part in ((m, term[:tile]), (m + half, term[tile:])):
                        out_ref[at, pl.ds(pl.multiple_of(start * tile, tile), tile)] += part


def terms_kernel(subs, cols_ref, count_ref, a_hbm, own_0, own_1, *rest):
    edges, (high_ref, low_ref, a_ref, upper, lower, turned, sems) = rest[:subs], rest[subs:]
    rows, slots, tile = a_ref.shape[:3]
    tiles = upper.shape[0] - 1
    middle = upper.shape[1]
    me = lax.axis_index("sub")
    base = lax.axis_index("dom") * (subs * rows) - rows
    loads = [pltpu.make_async_copy(a_hbm.at[f], a_ref.at[f], sems.at[f]) for f in range(rows)]
    for load in loads:
        load.start()
    upper[...] = jnp.zeros(upper.shape, F32)
    lower[...] = jnp.zeros(lower.shape, F32)
    for f in range(rows):
        turned[f] = (own_0, own_1)[f // (rows // 2)][f % (rows // 2)].T
    for f in range(rows):
        loads[f].wait()
        for k in range(slots):
            at = jnp.where(k < count_ref[f], cols_ref[f, k] - base, tiles)
            term = jnp.dot(turned[f], a_ref[f, k], preferred_element_type=F32)
            upper[at] += term[:middle]
            lower[at] += term[middle:]
    for c in range(subs * rows):
        for at, ref in ((0, upper), (middle, lower)):
            value = ref[rows + c]
            high = value.astype(BF16)
            high_ref[c, at : at + middle] = high
            low_ref[c, at : at + middle] = (value - high.astype(F32)).astype(BF16)

    def owned(c, k):
        at = lax.bitwise_xor(me, k) * COARSE_ROWS
        here = pl.ds(pl.multiple_of(lax.rem(at, middle), COARSE_ROWS), COARSE_ROWS)
        return jnp.where(at < middle, upper[c, here], lower[c, here])

    for k in range(subs):
        for i, c in enumerate([*range(rows), *range(tiles - rows, tiles)]):
            part = owned(c, k)
            edges[k][:, i * tile : (i + 1) * tile] = part.astype(edges[k].dtype)
    k = subs - 1
    for f in range(rows):
        part = owned(rows + lax.bitwise_xor(me, k) * rows + f, k)
        at = (2 * rows + f) * tile
        edges[k][:, at : at + tile] = part.astype(edges[k].dtype)


def terms_product(rows, sources, high_ref, low_ref, p_refs):
    me = lax.axis_index("sub")
    both = []
    for ref in (high_ref, low_ref):
        at = [lax.bitwise_xor(me, k) * rows + f for k in sources for f in range(rows)]
        both.append(jnp.concatenate([ref[i] for i in at], axis=1))
    stacked = jnp.concatenate([ref[i] for ref in p_refs for i in range(ref.shape[0])], axis=0)
    out = jnp.dot(jnp.concatenate(both, axis=0), stacked, preferred_element_type=F32)
    height = high_ref.shape[1]
    return out[:height] + out[height:]


def early_kernel(subs, rows, sources, high_ref, low_ref, edge_ref, *rest):
    p_refs, (out_ref, part_ref) = rest[:-2], rest[-2:]
    out_ref[...] = terms_product(rows, sources, high_ref, low_ref, p_refs)
    width = out_ref.shape[1]
    start = lax.bitwise_xor(lax.axis_index("sub"), subs - 1) * COARSE_ROWS
    at = pl.ds(pl.multiple_of(start, COARSE_ROWS), COARSE_ROWS)
    part_ref[:, :width] = out_ref[at].astype(BF16)
    part_ref[:, width:] = edge_ref[...]


def late_kernel(subs, rows, sources, high_ref, low_ref, early_ref, *rest):
    p_refs, rest = rest[: 2 * subs], rest[2 * subs :]
    edges, outs, (near_ref, far_ref, mid, ends) = rest[: subs - 1], rest[subs - 1 : -4], rest[-4:]
    width, piece = mid.shape[1], p_refs[0].shape[0]
    me, odd = lax.axis_index("sub"), lax.rem(lax.axis_index("dom"), 2)
    last = [p_refs[2 * k + i] for k in sources for i in range(2)]
    mid[...] = early_ref[...] + terms_product(rows, sources, high_ref, low_ref, last)
    for k in range(subs - 1):
        start = pl.multiple_of(lax.bitwise_xor(me, k) * COARSE_ROWS, COARSE_ROWS)
        outs[k][:, :width] = mid[pl.ds(start, COARSE_ROWS)].astype(outs[k].dtype)
        outs[k][:, width:] = edges[k][...]
    for k in range(subs):
        for at, who in ((0, 0), (rows, subs - 1)):

            @pl.when(me == who ^ k)
            def _():
                for i in range(2):
                    ends[at + i * piece : at + (i + 1) * piece] = p_refs[2 * k + i][...]

    near_ref[...] = ends[pl.ds((1 - odd) * rows, rows)]
    far_ref[...] = ends[pl.ds(odd * rows, rows)]


def group_kernel(subs, half, cols_ref, count_ref, pair_ref, a_ref, edge_ref, *rest):
    p_refs, rest = rest[: 2 * subs], rest[2 * subs :]
    outs, (pool, q, mid_ref) = rest[:subs], rest[subs:]
    rows, slots, tile = a_ref.shape[0], a_ref.shape[1], a_ref.shape[2]
    zero = subs * rows
    width = 2 * half * tile
    me = lax.axis_index("sub")
    first = lax.axis_index("dom") * (subs * rows)
    piece = rows // 2
    for k in range(subs):
        for i in range(2):
            pool[pl.ds(lax.bitwise_xor(me, k) * rows + i * piece, piece)] = p_refs[2 * k + i][...]
    pool[zero] = jnp.zeros(pool.shape[1:], pool.dtype)
    for f in range(rows):
        a_row = side_by_side(a_ref, f)
        index = [[None] * slots for _ in range(half)]
        for k in range(slots):
            rel = cols_ref[f, k] - first
            inside = (rel >= 0) & (rel < zero) & (k < count_ref[f])
            safe = jnp.where(inside, rel, 0)
            for m in range(half):
                here = inside if half == 1 else inside & (pair_ref[rows + safe] == m)
                index[m][k] = jnp.where(here, safe, zero)
        for m in range(half):
            block = placed_product(a_row, pool, index[m])
            lo, hi = m * tile, (m + half) * tile
            q[f * tile : (f + 1) * tile, lo : lo + tile] = block[:, :tile]
            q[f * tile : (f + 1) * tile, hi : hi + tile] = block[:, tile:]
    for m, out in enumerate(restrict(own_tiles(rows, zero, half, me, pair_ref, pool), q[...], half)):
        mid_ref[m * tile : (m + 1) * tile] = out[:tile]
        mid_ref[(m + half) * tile : (m + half + 1) * tile] = out[tile:]
    for k in range(subs):
        at = pl.ds(pl.multiple_of(lax.bitwise_xor(me, k) * COARSE_ROWS, COARSE_ROWS), COARSE_ROWS)
        kind = outs[k].dtype
        outs[k][:, :width] = mid_ref[at].astype(kind)
        for c in range(2 * rows):
            outs[k][:, width + c * tile : width + (c + 1) * tile] = edge_ref[c, at].astype(kind)


def sum_kernel(subs, width, *refs):
    part_refs, own_refs, (mid_ref, edge_ref, total_ref) = refs[:subs], refs[subs:-3], refs[-3:]
    span = total_ref.shape[1]
    total_ref[...] = part_refs[0][...]
    for part in part_refs[1:]:
        total_ref[...] += part[:, :span].astype(F32)
        if part.shape[1] > span:
            stacked = jnp.concatenate([ref[i] for ref in own_refs for i in range(ref.shape[0])], axis=0)
            total_ref[:, :width] += jnp.dot(part[:, span:], stacked, preferred_element_type=F32)
    total = total_ref[...]
    mid_ref[...] = total[:, :width].astype(BF16)
    sums = total[:, width:]
    high = sums.astype(BF16)
    edge_ref[:COARSE_ROWS] = high
    edge_ref[COARSE_ROWS:] = (sums - high.astype(F32)).astype(BF16)


def finish_kernel(subs, half, *refs):
    pair_ref = refs[0] if half > 1 else None
    far_ref, near_ref, mid_ref, both_ref, out_ref, edge = refs[-6:]
    rows, tile = near_ref.shape[:2]
    width = 2 * half * tile
    odd = lax.rem(lax.axis_index("dom"), 2)
    edge[pl.ds((1 - odd) * rows, rows)] = near_ref[...]
    edge[pl.ds(odd * rows, rows)] = far_ref[...]
    out_ref[:, width : 2 * width] = mid_ref[...]
    both = both_ref[...]
    for side in range(2):
        blocks = [jnp.zeros((COARSE_ROWS, tile), F32) for _ in range(2 * half)]
        tiles = range(side * rows, (side + 1) * rows)
        if half == 1:
            stacked = jnp.concatenate([edge[c] for c in tiles], axis=0)
            lhs = both[:, side * rows * tile : (side + 1) * rows * tile]
            term = jnp.dot(lhs, stacked, preferred_element_type=F32)
            term = term[:COARSE_ROWS] + term[COARSE_ROWS:]
            blocks = [term[:, :tile], term[:, tile:]]
        else:
            for c in tiles:
                lhs = both[:, c * tile : (c + 1) * tile]
                term = jnp.dot(lhs, edge[c], preferred_element_type=F32)
                term = term[:COARSE_ROWS] + term[COARSE_ROWS:]
                m_here = pair_ref[c if side == 0 else subs * rows + c]
                for m in range(half):
                    here = m_here == m
                    blocks[m] = blocks[m] + jnp.where(here, term[:, :tile], 0.0)
                    blocks[m + half] = blocks[m + half] + jnp.where(here, term[:, tile:], 0.0)
        for b in range(2 * half):
            at = 2 * side * width + b * tile
            out_ref[:, at : at + tile] = blocks[b].astype(BF16)


def narrow_parts(a_tiles, a_cols, a_count, own, tiles, span):
    rows, slots, tile = a_tiles.shape[:3]
    subs = lax.axis_size("sub")
    width = 2 * tile
    smem = pl.BlockSpec(memory_space=pltpu.SMEM)
    vmem = pl.BlockSpec(memory_space=pltpu.VMEM)
    kinds = [F32] + [BF16] * (subs - 1)
    spare = 3 << 20
    products = 2 * width * rows * tile * width
    *edges, high, low = pl.pallas_call(
        functools.partial(terms_kernel, subs),
        out_shape=[
            jax.ShapeDtypeStruct((COARSE_ROWS, span - width + (k == subs - 1) * rows * tile), kind)
            for k, kind in enumerate(kinds)
        ]
        + [jax.ShapeDtypeStruct((subs * rows, width, tile), BF16)] * 2,
        in_specs=[smem, smem, pl.BlockSpec(memory_space=pltpu.HBM), vmem, vmem],
        out_specs=[vmem] * (subs + 2),
        scratch_shapes=[
            pltpu.VMEM(a_tiles.shape, BF16),
            pltpu.VMEM(((subs + 2) * rows + 1, width // 2, tile), F32),
            pltpu.VMEM(((subs + 2) * rows + 1, width // 2, tile), F32),
            pltpu.VMEM((rows, width, tile), BF16),
            pltpu.SemaphoreType.DMA((rows,)),
        ],
        compiler_params=pltpu.CompilerParams(
            vmem_limit_bytes=2 * a_tiles.size + 4 * ((subs + 2) * rows + 1) * width * tile + spare
        ),
        cost_estimate=pl.CostEstimate(
            flops=1 << 31, bytes_accessed=2 * a_tiles.size, transcendentals=0
        ),
        name="terms",
    )(a_cols, a_count, pltpu.with_memory_space_constraint(a_tiles, pltpu.HBM), *own)
    first, last = list(range(subs - 1)), [subs - 1]
    early, farthest = pl.pallas_call(
        functools.partial(early_kernel, subs, rows, first),
        out_shape=[
            jax.ShapeDtypeStruct((width, width), F32),
            jax.ShapeDtypeStruct((COARSE_ROWS, span + rows * tile), BF16),
        ],
        in_specs=[vmem] * (3 + 2 * len(first)),
        out_specs=[vmem] * 2,
        compiler_params=pltpu.CompilerParams(vmem_limit_bytes=spare),
        cost_estimate=pl.CostEstimate(
            flops=2 * len(first) * products, bytes_accessed=1 << 20, transcendentals=0
        ),
        name="early_part",
    )(high, low, edges[-1], *[piece for k in first for piece in tiles[k]])
    *parts, near, far = pl.pallas_call(
        functools.partial(late_kernel, subs, rows, last),
        out_shape=[jax.ShapeDtypeStruct((COARSE_ROWS, span), kind) for kind in kinds[:-1]]
        + [jax.ShapeDtypeStruct((rows, tile, width), BF16)] * 2,
        in_specs=[vmem] * (2 + 3 * subs),
        out_specs=[vmem] * (subs + 1),
        scratch_shapes=[
            pltpu.VMEM((width, width), F32),
            pltpu.VMEM((2 * rows, tile, width), BF16),
        ],
        compiler_params=pltpu.CompilerParams(vmem_limit_bytes=spare),
        cost_estimate=pl.CostEstimate(
            flops=2 * products, bytes_accessed=1 << 20, transcendentals=0
        ),
        name="late_part",
    )(high, low, early, *[piece for pieces in tiles for piece in pieces], *edges[:-1])
    return [*parts, farthest, near, far]


def local(a_tiles, a_cols, a_count, p_tiles, p_cols):
    rows, slots, tile = a_tiles.shape[:3]
    subs, doms = lax.axis_size("sub"), lax.axis_size("dom")
    coarse_group = subs * COARSE_ROWS // tile
    half = coarse_group // 2
    width = coarse_group * tile
    group_tiles = rows * subs

    smem = pl.BlockSpec(memory_space=pltpu.SMEM)
    vmem = pl.BlockSpec(memory_space=pltpu.VMEM)
    p_bytes = rows * tile * 2 * tile * 2
    a_bytes = a_tiles.size * 2
    spare = 3 << 20

    def exchange(value, k):
        return lax.ppermute(value, "sub", [(s, s ^ k) for s in range(subs)])

    own = pl.pallas_call(
        order_kernel,
        out_shape=[jax.ShapeDtypeStruct((rows // 2, tile, 2 * tile), BF16)] * 2,
        in_specs=[pl.BlockSpec(memory_space=pltpu.HBM)] * 2,
        out_specs=[vmem] * 2,
        scratch_shapes=[
            pltpu.SMEM((2, rows), jnp.int32),
            pltpu.VMEM(p_tiles.shape, BF16),
            pltpu.SemaphoreType.DMA((rows + 1,)),
        ],
        compiler_params=pltpu.CompilerParams(vmem_limit_bytes=spare),
        cost_estimate=pl.CostEstimate(
            flops=1 << 30, bytes_accessed=2 * p_bytes, transcendentals=0
        ),
        name="order_columns",
    )(
        pltpu.with_memory_space_constraint(p_cols.T, pltpu.HBM),
        pltpu.with_memory_space_constraint(p_tiles, pltpu.HBM),
    )

    tiles = [list(own)] + [[None, None] for _ in range(subs - 1)]
    for k in range(1, subs):
        low, high = k & -k, 1 << (k.bit_length() - 1)
        tiles[k][0] = exchange(tiles[k ^ low][0], low)
        tiles[k][1] = exchange(tiles[k ^ high][1], high)
    span = width + 2 * rows * tile
    pairs = []
    if half > 1:
        m_own = jnp.min(p_cols, axis=1) - lax.axis_index("dom") * coarse_group
        m_group = lax.all_gather(m_own, "sub", axis=0, tiled=True)
        m_left = lax.ppermute(
            m_group[group_tiles - rows :], "dom", [(d, d + 1) for d in range(doms - 1)]
        )
        m_right = lax.ppermute(m_group[:rows], "dom", [(d + 1, d) for d in range(doms - 1)])
        pair = jnp.concatenate([m_left, m_group, m_right])
        pairs = [pair]

    flat = [piece for pieces in tiles for piece in pieces]
    if half == 1:
        *parts, to_near, to_far = narrow_parts(a_tiles, a_cols, a_count, own, tiles, span)
    else:
        flops = 2 * rows * slots * tile * tile * 2 * tile * half
        edges, a_held = pl.pallas_call(
            functools.partial(edge_kernel, subs, half),
            out_shape=[
                jax.ShapeDtypeStruct((2 * rows, width, tile), F32),
                jax.ShapeDtypeStruct(a_tiles.shape, BF16),
            ],
            in_specs=[smem, smem, smem, pl.BlockSpec(memory_space=pltpu.HBM), vmem, vmem],
            out_specs=[vmem] * 2,
            scratch_shapes=[
                pltpu.VMEM((rows, 2 * tile, tile), BF16),
                pltpu.SemaphoreType.DMA((rows,)),
            ],
            compiler_params=pltpu.CompilerParams(vmem_limit_bytes=8 * rows * tile * width + spare),
            cost_estimate=pl.CostEstimate(
                flops=flops, bytes_accessed=a_bytes + p_bytes, transcendentals=0
            ),
            name="edge_part",
        )(a_cols, a_count, pair, pltpu.with_memory_space_constraint(a_tiles, pltpu.HBM), *own)

        *parts, pool = pl.pallas_call(
            functools.partial(group_kernel, subs, half),
            out_shape=[
                jax.ShapeDtypeStruct((COARSE_ROWS, span), F32 if k == 0 else BF16)
                for k in range(subs)
            ]
            + [jax.ShapeDtypeStruct((group_tiles + 1, tile, 2 * tile), BF16)],
            in_specs=[smem, smem, smem] + [vmem] * (2 * subs + 2),
            out_specs=[vmem] * (subs + 1),
            scratch_shapes=[
                pltpu.VMEM((rows * tile, width), BF16),
                pltpu.VMEM((width, width), F32),
            ],
            compiler_params=pltpu.CompilerParams(
                vmem_limit_bytes=2 * rows * tile * width + 4 * width * width + spare
            ),
            cost_estimate=pl.CostEstimate(
                flops=flops, bytes_accessed=a_bytes + subs * p_bytes, transcendentals=0
            ),
            name="group_part",
        )(a_cols, a_count, pair, a_held, edges, *flat)
        to_near, to_far = pl.pallas_call(
            functools.partial(hand_out_kernel, subs),
            out_shape=[jax.ShapeDtypeStruct(p_tiles.shape, BF16)] * 2,
            in_specs=[vmem],
            out_specs=[vmem] * 2,
            compiler_params=pltpu.CompilerParams(vmem_limit_bytes=spare),
            name="hand_out",
        )(pool)
    received = [exchange(parts[k], k) for k in range(subs - 1, 0, -1)]
    far = lax.ppermute(
        to_far, "dom", [(d, d - 1 + 2 * (d % 2)) for d in range(1, doms - 1)]
    )
    near = lax.ppermute(to_near, "dom", [(d, d ^ 1) for d in range(doms)])
    mid, both = pl.pallas_call(
        functools.partial(sum_kernel, subs, width),
        out_shape=[
            jax.ShapeDtypeStruct((COARSE_ROWS, width), BF16),
            jax.ShapeDtypeStruct((2 * COARSE_ROWS, span - width), BF16),
        ],
        in_specs=[vmem] * (subs + len(own)),
        out_specs=[vmem] * 2,
        scratch_shapes=[pltpu.VMEM((COARSE_ROWS, span), F32)],
        compiler_params=pltpu.CompilerParams(vmem_limit_bytes=spare),
        cost_estimate=pl.CostEstimate(
            flops=1 << 31, bytes_accessed=8 * COARSE_ROWS * span, transcendentals=0
        ),
        name="sum_parts",
    )(parts[0], *received, *own)
    return pl.pallas_call(
        functools.partial(finish_kernel, subs, half),
        out_shape=jax.ShapeDtypeStruct((COARSE_ROWS, 3 * width), BF16),
        in_specs=[smem] * len(pairs) + [vmem] * 4,
        out_specs=vmem,
        scratch_shapes=[pltpu.VMEM((2 * rows, tile, 2 * tile), BF16)],
        compiler_params=pltpu.CompilerParams(vmem_limit_bytes=2 * p_bytes + spare),
        cost_estimate=pl.CostEstimate(
            flops=1 << 28, bytes_accessed=4 * p_bytes, transcendentals=0
        ),
        name="finish",
    )(*pairs, far, near, mid, both)


def solution(mesh):
    placed = (
        P(("dom", "sub"), None, None, None),
        P(("dom", "sub"), None),
        P(("dom", "sub")),
        P(("dom", "sub"), None, None),
        P(("dom", "sub"), None),
    )
    return jax.shard_map(
        local, mesh=mesh, in_specs=placed, out_specs=P(("dom", "sub"), None), check_vma=False
    )
```

```python
import functools

import jax
import jax.numpy as jnp
from jax import lax
from jax.experimental import pallas as pl
from jax.experimental.pallas import tpu as pltpu
from jax.sharding import PartitionSpec as P

COARSE_ROWS = 64
BF16 = jnp.bfloat16
F32 = jnp.float32


def side_by_side(a_ref, f):
    return jnp.concatenate([a_ref[f, k] for k in range(a_ref.shape[1])], axis=1)


def placed_product(a_row, pool, index):
    stacked = jnp.concatenate([pool[i] for i in index], axis=0)
    return jnp.dot(a_row, stacked, preferred_element_type=F32).astype(BF16)


def own_tiles(rows, zero, half, me, pair_ref, pool):
    tiles = []
    for m in range(half):
        at = [me * rows + f for f in range(rows)]
        if half > 1:
            at = [jnp.where(pair_ref[rows + i] == m, i, zero) for i in at]
        tiles.append([pool[i] for i in at])
    return tiles


def restrict(tiles, q, half):
    outs = []
    for m in range(half):
        lhs = jnp.concatenate(tiles[m], axis=0)
        outs.append(
            lax.dot_general(lhs, q, (((0,), (0,)), ((), ())), preferred_element_type=F32)
        )
    return outs


def order_kernel(cols_hbm, p_hbm, *rest):
    outs, (cols_ref, p_ref, sems) = rest[:2], rest[2:]
    rows, tile = p_ref.shape[:2]
    piece = rows // 2
    lists = pltpu.make_async_copy(cols_hbm, cols_ref, sems.at[rows])
    lists.start()
    loads = [pltpu.make_async_copy(p_hbm.at[f], p_ref.at[f], sems.at[f]) for f in range(rows)]
    for load in loads:
        load.start()
    lists.wait()
    for f in range(rows):
        loads[f].wait()
        first = pl.multiple_of(jnp.where(cols_ref[0, f] > cols_ref[1, f], tile, 0), tile)
        for t, start in ((0, first), (1, pl.multiple_of(tile - first, tile))):
            outs[f // piece][f % piece, :, t * tile : (t + 1) * tile] = p_ref[f, :, pl.ds(start, tile)]


def hand_out_kernel(subs, pool, near_ref, far_ref):
    rows = near_ref.shape[0]
    odd = lax.rem(lax.axis_index("dom"), 2)
    last = (subs - 1) * rows
    near_ref[...] = pool[pl.ds((1 - odd) * last, rows)]
    far_ref[...] = pool[pl.ds(odd * last, rows)]


def edge_kernel(subs, half, cols_ref, count_ref, pair_ref, a_hbm, own_0, own_1, *rest):
    out_ref, a_ref, turned, sems = rest
    rows, slots, tile = a_ref.shape[:3]
    first = lax.axis_index("dom") * (subs * rows)
    me = lax.axis_index("sub")
    loads = [pltpu.make_async_copy(a_hbm.at[f], a_ref.at[f], sems.at[f]) for f in range(rows)]
    for load in loads:
        load.start()
    out_ref[...] = jnp.zeros(out_ref.shape, F32)
    for f in range(rows):
        turned[f] = (own_0, own_1)[f // (rows // 2)][f % (rows // 2)].T
    for f in range(rows):
        loads[f].wait()
        for k in range(slots):
            rel = cols_ref[f, k] - first
            live = (k < count_ref[f]) & ((rel < 0) | (rel >= subs * rows))

            @pl.when(live)
            def _():
                at = jnp.where(rel < 0, rel + rows, rel - subs * rows + rows)
                term = jnp.dot(turned[f], a_ref[f, k], preferred_element_type=F32)
                if half == 1:
                    out_ref[at] += term
                else:
                    m = pair_ref[rows + me * rows + f]
                    for start, part in ((m, term[:tile]), (m + half, term[tile:])):
                        out_ref[at, pl.ds(pl.multiple_of(start * tile, tile), tile)] += part


def terms_kernel(subs, cols_ref, count_ref, a_ref, own_0, own_1, *rest):
    edges, (high_ref, low_ref, total, turned) = rest[:subs], rest[subs:]
    rows, slots, tile = a_ref.shape[:3]
    tiles = total.shape[0] - 1
    me = lax.axis_index("sub")
    base = lax.axis_index("dom") * (subs * rows) - rows
    total[...] = jnp.zeros(total.shape, F32)
    for f in range(rows):
        turned[f] = (own_0, own_1)[f // (rows // 2)][f % (rows // 2)].T
    for f in range(rows):
        for k in range(slots):
            at = jnp.where(k < count_ref[f], cols_ref[f, k] - base, tiles)
            total[at] += jnp.dot(turned[f], a_ref[f, k], preferred_element_type=F32)
    for c in range(subs * rows):
        value = total[rows + c]
        high = value.astype(BF16)
        high_ref[c] = high
        low_ref[c] = (value - high.astype(F32)).astype(BF16)
    for k in range(subs):
        start = pl.multiple_of(lax.bitwise_xor(me, k) * COARSE_ROWS, COARSE_ROWS)
        for i, c in enumerate([*range(rows), *range(tiles - rows, tiles)]):
            part = total[c, pl.ds(start, COARSE_ROWS)]
            edges[k][:, i * tile : (i + 1) * tile] = part.astype(edges[k].dtype)
    k = subs - 1
    start = pl.multiple_of(lax.bitwise_xor(me, k) * COARSE_ROWS, COARSE_ROWS)
    for f in range(rows):
        part = total[rows + lax.bitwise_xor(me, k) * rows + f, pl.ds(start, COARSE_ROWS)]
        at = (2 * rows + f) * tile
        edges[k][:, at : at + tile] = part.astype(edges[k].dtype)


def terms_product(rows, sources, high_ref, low_ref, p_refs):
    me = lax.axis_index("sub")
    both = []
    for ref in (high_ref, low_ref):
        at = [lax.bitwise_xor(me, k) * rows + f for k in sources for f in range(rows)]
        both.append(jnp.concatenate([ref[i] for i in at], axis=1))
    stacked = jnp.concatenate([ref[i] for ref in p_refs for i in range(ref.shape[0])], axis=0)
    out = jnp.dot(jnp.concatenate(both, axis=0), stacked, preferred_element_type=F32)
    height = high_ref.shape[1]
    return out[:height] + out[height:]


def early_kernel(subs, rows, sources, high_ref, low_ref, edge_ref, *rest):
    p_refs, (out_ref, part_ref) = rest[:-2], rest[-2:]
    out_ref[...] = terms_product(rows, sources, high_ref, low_ref, p_refs)
    width = out_ref.shape[1]
    start = lax.bitwise_xor(lax.axis_index("sub"), subs - 1) * COARSE_ROWS
    at = pl.ds(pl.multiple_of(start, COARSE_ROWS), COARSE_ROWS)
    part_ref[:, :width] = out_ref[at].astype(BF16)
    part_ref[:, width:] = edge_ref[...]


def late_kernel(subs, rows, sources, high_ref, low_ref, early_ref, *rest):
    p_refs, rest = rest[: 2 * subs], rest[2 * subs :]
    edges, outs, (near_ref, far_ref, mid, ends) = rest[: subs - 1], rest[subs - 1 : -4], rest[-4:]
    width, piece = mid.shape[1], p_refs[0].shape[0]
    me, odd = lax.axis_index("sub"), lax.rem(lax.axis_index("dom"), 2)
    last = [p_refs[2 * k + i] for k in sources for i in range(2)]
    mid[...] = early_ref[...] + terms_product(rows, sources, high_ref, low_ref, last)
    for k in range(subs - 1):
        start = pl.multiple_of(lax.bitwise_xor(me, k) * COARSE_ROWS, COARSE_ROWS)
        outs[k][:, :width] = mid[pl.ds(start, COARSE_ROWS)].astype(outs[k].dtype)
        outs[k][:, width:] = edges[k][...]
    for k in range(subs):
        for at, who in ((0, 0), (rows, subs - 1)):

            @pl.when(me == who ^ k)
            def _():
                for i in range(2):
                    ends[at + i * piece : at + (i + 1) * piece] = p_refs[2 * k + i][...]

    near_ref[...] = ends[pl.ds((1 - odd) * rows, rows)]
    far_ref[...] = ends[pl.ds(odd * rows, rows)]


def group_kernel(subs, half, cols_ref, count_ref, pair_ref, a_ref, edge_ref, *rest):
    p_refs, rest = rest[: 2 * subs], rest[2 * subs :]
    outs, (pool, q, mid_ref) = rest[:subs], rest[subs:]
    rows, slots, tile = a_ref.shape[0], a_ref.shape[1], a_ref.shape[2]
    zero = subs * rows
    width = 2 * half * tile
    me = lax.axis_index("sub")
    first = lax.axis_index("dom") * (subs * rows)
    piece = rows // 2
    for k in range(subs):
        for i in range(2):
            pool[pl.ds(lax.bitwise_xor(me, k) * rows + i * piece, piece)] = p_refs[2 * k + i][...]
    pool[zero] = jnp.zeros(pool.shape[1:], pool.dtype)
    for f in range(rows):
        a_row = side_by_side(a_ref, f)
        index = [[None] * slots for _ in range(half)]
        for k in range(slots):
            rel = cols_ref[f, k] - first
            inside = (rel >= 0) & (rel < zero) & (k < count_ref[f])
            safe = jnp.where(inside, rel, 0)
            for m in range(half):
                here = inside if half == 1 else inside & (pair_ref[rows + safe] == m)
                index[m][k] = jnp.where(here, safe, zero)
        for m in range(half):
            block = placed_product(a_row, pool, index[m])
            lo, hi = m * tile, (m + half) * tile
            q[f * tile : (f + 1) * tile, lo : lo + tile] = block[:, :tile]
            q[f * tile : (f + 1) * tile, hi : hi + tile] = block[:, tile:]
    for m, out in enumerate(restrict(own_tiles(rows, zero, half, me, pair_ref, pool), q[...], half)):
        mid_ref[m * tile : (m + 1) * tile] = out[:tile]
        mid_ref[(m + half) * tile : (m + half + 1) * tile] = out[tile:]
    for k in range(subs):
        at = pl.ds(pl.multiple_of(lax.bitwise_xor(me, k) * COARSE_ROWS, COARSE_ROWS), COARSE_ROWS)
        kind = outs[k].dtype
        outs[k][:, :width] = mid_ref[at].astype(kind)
        for c in range(2 * rows):
            outs[k][:, width + c * tile : width + (c + 1) * tile] = edge_ref[c, at].astype(kind)


def sum_kernel(subs, width, *refs):
    part_refs, own_refs, (mid_ref, edge_ref, total_ref) = refs[:subs], refs[subs:-3], refs[-3:]
    span = total_ref.shape[1]
    total_ref[...] = part_refs[0][...]
    for part in part_refs[1:]:
        total_ref[...] += part[:, :span].astype(F32)
        if part.shape[1] > span:
            stacked = jnp.concatenate([ref[i] for ref in own_refs for i in range(ref.shape[0])], axis=0)
            total_ref[:, :width] += jnp.dot(part[:, span:], stacked, preferred_element_type=F32)
    total = total_ref[...]
    mid_ref[...] = total[:, :width].astype(BF16)
    sums = total[:, width:]
    high = sums.astype(BF16)
    edge_ref[:COARSE_ROWS] = high
    edge_ref[COARSE_ROWS:] = (sums - high.astype(F32)).astype(BF16)


def finish_kernel(subs, half, *refs):
    pair_ref = refs[0] if half > 1 else None
    far_ref, near_ref, mid_ref, both_ref, out_ref, edge = refs[-6:]
    rows, tile = near_ref.shape[:2]
    width = 2 * half * tile
    odd = lax.rem(lax.axis_index("dom"), 2)
    edge[pl.ds((1 - odd) * rows, rows)] = near_ref[...]
    edge[pl.ds(odd * rows, rows)] = far_ref[...]
    out_ref[:, width : 2 * width] = mid_ref[...]
    both = both_ref[...]
    for side in range(2):
        blocks = [jnp.zeros((COARSE_ROWS, tile), F32) for _ in range(2 * half)]
        tiles = range(side * rows, (side + 1) * rows)
        if half == 1:
            stacked = jnp.concatenate([edge[c] for c in tiles], axis=0)
            lhs = both[:, side * rows * tile : (side + 1) * rows * tile]
            term = jnp.dot(lhs, stacked, preferred_element_type=F32)
            term = term[:COARSE_ROWS] + term[COARSE_ROWS:]
            blocks = [term[:, :tile], term[:, tile:]]
        else:
            for c in tiles:
                lhs = both[:, c * tile : (c + 1) * tile]
                term = jnp.dot(lhs, edge[c], preferred_element_type=F32)
                term = term[:COARSE_ROWS] + term[COARSE_ROWS:]
                m_here = pair_ref[c if side == 0 else subs * rows + c]
                for m in range(half):
                    here = m_here == m
                    blocks[m] = blocks[m] + jnp.where(here, term[:, :tile], 0.0)
                    blocks[m + half] = blocks[m + half] + jnp.where(here, term[:, tile:], 0.0)
        for b in range(2 * half):
            at = 2 * side * width + b * tile
            out_ref[:, at : at + tile] = blocks[b].astype(BF16)


def narrow_parts(a_tiles, a_cols, a_count, own, tiles, span):
    rows, slots, tile = a_tiles.shape[:3]
    subs = lax.axis_size("sub")
    width = 2 * tile
    smem = pl.BlockSpec(memory_space=pltpu.SMEM)
    vmem = pl.BlockSpec(memory_space=pltpu.VMEM)
    kinds = [F32] + [BF16] * (subs - 1)
    spare = 3 << 20
    products = 2 * width * rows * tile * width
    *edges, high, low = pl.pallas_call(
        functools.partial(terms_kernel, subs),
        out_shape=[
            jax.ShapeDtypeStruct((COARSE_ROWS, span - width + (k == subs - 1) * rows * tile), kind)
            for k, kind in enumerate(kinds)
        ]
        + [jax.ShapeDtypeStruct((subs * rows, width, tile), BF16)] * 2,
        in_specs=[smem, smem, vmem, vmem, vmem],
        out_specs=[vmem] * (subs + 2),
        scratch_shapes=[
            pltpu.VMEM(((subs + 2) * rows + 1, width, tile), F32),
            pltpu.VMEM((rows, width, tile), BF16),
        ],
        compiler_params=pltpu.CompilerParams(
            vmem_limit_bytes=4 * ((subs + 2) * rows + 1) * width * tile + spare
        ),
        cost_estimate=pl.CostEstimate(
            flops=1 << 31, bytes_accessed=2 * a_tiles.size, transcendentals=0
        ),
        name="terms",
    )(a_cols, a_count, a_tiles, *own)
    first, last = list(range(subs - 1)), [subs - 1]
    early, farthest = pl.pallas_call(
        functools.partial(early_kernel, subs, rows, first),
        out_shape=[
            jax.ShapeDtypeStruct((width, width), F32),
            jax.ShapeDtypeStruct((COARSE_ROWS, span + rows * tile), BF16),
        ],
        in_specs=[vmem] * (3 + 2 * len(first)),
        out_specs=[vmem] * 2,
        compiler_params=pltpu.CompilerParams(vmem_limit_bytes=spare),
        cost_estimate=pl.CostEstimate(
            flops=2 * len(first) * products, bytes_accessed=1 << 20, transcendentals=0
        ),
        name="early_part",
    )(high, low, edges[-1], *[piece for k in first for piece in tiles[k]])
    *parts, near, far = pl.pallas_call(
        functools.partial(late_kernel, subs, rows, last),
        out_shape=[jax.ShapeDtypeStruct((COARSE_ROWS, span), kind) for kind in kinds[:-1]]
        + [jax.ShapeDtypeStruct((rows, tile, width), BF16)] * 2,
        in_specs=[vmem] * (2 + 3 * subs),
        out_specs=[vmem] * (subs + 1),
        scratch_shapes=[
            pltpu.VMEM((width, width), F32),
            pltpu.VMEM((2 * rows, tile, width), BF16),
        ],
        compiler_params=pltpu.CompilerParams(vmem_limit_bytes=spare),
        cost_estimate=pl.CostEstimate(
            flops=2 * products, bytes_accessed=1 << 20, transcendentals=0
        ),
        name="late_part",
    )(high, low, early, *[piece for pieces in tiles for piece in pieces], *edges[:-1])
    return [*parts, farthest, near, far]


def local(a_tiles, a_cols, a_count, p_tiles, p_cols):
    rows, slots, tile = a_tiles.shape[:3]
    subs, doms = lax.axis_size("sub"), lax.axis_size("dom")
    coarse_group = subs * COARSE_ROWS // tile
    half = coarse_group // 2
    width = coarse_group * tile
    group_tiles = rows * subs

    smem = pl.BlockSpec(memory_space=pltpu.SMEM)
    vmem = pl.BlockSpec(memory_space=pltpu.VMEM)
    p_bytes = rows * tile * 2 * tile * 2
    a_bytes = a_tiles.size * 2
    spare = 3 << 20

    def exchange(value, k):
        return lax.ppermute(value, "sub", [(s, s ^ k) for s in range(subs)])

    own = pl.pallas_call(
        order_kernel,
        out_shape=[jax.ShapeDtypeStruct((rows // 2, tile, 2 * tile), BF16)] * 2,
        in_specs=[pl.BlockSpec(memory_space=pltpu.HBM)] * 2,
        out_specs=[vmem] * 2,
        scratch_shapes=[
            pltpu.SMEM((2, rows), jnp.int32),
            pltpu.VMEM(p_tiles.shape, BF16),
            pltpu.SemaphoreType.DMA((rows + 1,)),
        ],
        compiler_params=pltpu.CompilerParams(vmem_limit_bytes=spare),
        cost_estimate=pl.CostEstimate(
            flops=1 << 30, bytes_accessed=2 * p_bytes, transcendentals=0
        ),
        name="order_columns",
    )(
        pltpu.with_memory_space_constraint(p_cols.T, pltpu.HBM),
        pltpu.with_memory_space_constraint(p_tiles, pltpu.HBM),
    )

    tiles = [list(own)] + [[None, None] for _ in range(subs - 1)]
    for k in range(1, subs):
        low, high = k & -k, 1 << (k.bit_length() - 1)
        tiles[k][0] = exchange(tiles[k ^ low][0], low)
        tiles[k][1] = exchange(tiles[k ^ high][1], high)
    span = width + 2 * rows * tile
    pairs = []
    if half > 1:
        m_own = jnp.min(p_cols, axis=1) - lax.axis_index("dom") * coarse_group
        m_group = lax.all_gather(m_own, "sub", axis=0, tiled=True)
        m_left = lax.ppermute(
            m_group[group_tiles - rows :], "dom", [(d, d + 1) for d in range(doms - 1)]
        )
        m_right = lax.ppermute(m_group[:rows], "dom", [(d + 1, d) for d in range(doms - 1)])
        pair = jnp.concatenate([m_left, m_group, m_right])
        pairs = [pair]

    flat = [piece for pieces in tiles for piece in pieces]
    if half == 1:
        *parts, to_near, to_far = narrow_parts(a_tiles, a_cols, a_count, own, tiles, span)
    else:
        flops = 2 * rows * slots * tile * tile * 2 * tile * half
        edges, a_held = pl.pallas_call(
            functools.partial(edge_kernel, subs, half),
            out_shape=[
                jax.ShapeDtypeStruct((2 * rows, width, tile), F32),
                jax.ShapeDtypeStruct(a_tiles.shape, BF16),
            ],
            in_specs=[smem, smem, smem, pl.BlockSpec(memory_space=pltpu.HBM), vmem, vmem],
            out_specs=[vmem] * 2,
            scratch_shapes=[
                pltpu.VMEM((rows, 2 * tile, tile), BF16),
                pltpu.SemaphoreType.DMA((rows,)),
            ],
            compiler_params=pltpu.CompilerParams(vmem_limit_bytes=8 * rows * tile * width + spare),
            cost_estimate=pl.CostEstimate(
                flops=flops, bytes_accessed=a_bytes + p_bytes, transcendentals=0
            ),
            name="edge_part",
        )(a_cols, a_count, pair, pltpu.with_memory_space_constraint(a_tiles, pltpu.HBM), *own)

        *parts, pool = pl.pallas_call(
            functools.partial(group_kernel, subs, half),
            out_shape=[
                jax.ShapeDtypeStruct((COARSE_ROWS, span), F32 if k == 0 else BF16)
                for k in range(subs)
            ]
            + [jax.ShapeDtypeStruct((group_tiles + 1, tile, 2 * tile), BF16)],
            in_specs=[smem, smem, smem] + [vmem] * (2 * subs + 2),
            out_specs=[vmem] * (subs + 1),
            scratch_shapes=[
                pltpu.VMEM((rows * tile, width), BF16),
                pltpu.VMEM((width, width), F32),
            ],
            compiler_params=pltpu.CompilerParams(
                vmem_limit_bytes=2 * rows * tile * width + 4 * width * width + spare
            ),
            cost_estimate=pl.CostEstimate(
                flops=flops, bytes_accessed=a_bytes + subs * p_bytes, transcendentals=0
            ),
            name="group_part",
        )(a_cols, a_count, pair, a_held, edges, *flat)
        to_near, to_far = pl.pallas_call(
            functools.partial(hand_out_kernel, subs),
            out_shape=[jax.ShapeDtypeStruct(p_tiles.shape, BF16)] * 2,
            in_specs=[vmem],
            out_specs=[vmem] * 2,
            compiler_params=pltpu.CompilerParams(vmem_limit_bytes=spare),
            name="hand_out",
        )(pool)
    received = [exchange(parts[k], k) for k in range(subs - 1, 0, -1)]
    far = lax.ppermute(
        to_far, "dom", [(d, d - 1 + 2 * (d % 2)) for d in range(1, doms - 1)]
    )
    near = lax.ppermute(to_near, "dom", [(d, d ^ 1) for d in range(doms)])
    mid, both = pl.pallas_call(
        functools.partial(sum_kernel, subs, width),
        out_shape=[
            jax.ShapeDtypeStruct((COARSE_ROWS, width), BF16),
            jax.ShapeDtypeStruct((2 * COARSE_ROWS, span - width), BF16),
        ],
        in_specs=[vmem] * (subs + len(own)),
        out_specs=[vmem] * 2,
        scratch_shapes=[pltpu.VMEM((COARSE_ROWS, span), F32)],
        compiler_params=pltpu.CompilerParams(vmem_limit_bytes=spare),
        cost_estimate=pl.CostEstimate(
            flops=1 << 31, bytes_accessed=8 * COARSE_ROWS * span, transcendentals=0
        ),
        name="sum_parts",
    )(parts[0], *received, *own)
    return pl.pallas_call(
        functools.partial(finish_kernel, subs, half),
        out_shape=jax.ShapeDtypeStruct((COARSE_ROWS, 3 * width), BF16),
        in_specs=[smem] * len(pairs) + [vmem] * 4,
        out_specs=vmem,
        scratch_shapes=[pltpu.VMEM((2 * rows, tile, 2 * tile), BF16)],
        compiler_params=pltpu.CompilerParams(vmem_limit_bytes=2 * p_bytes + spare),
        cost_estimate=pl.CostEstimate(
            flops=1 << 28, bytes_accessed=4 * p_bytes, transcendentals=0
        ),
        name="finish",
    )(*pairs, far, near, mid, both)


def solution(mesh):
    placed = (
        P(("dom", "sub"), None, None, None),
        P(("dom", "sub"), None),
        P(("dom", "sub")),
        P(("dom", "sub"), None, None),
        P(("dom", "sub"), None),
    )
    return jax.shard_map(
        local, mesh=mesh, in_specs=placed, out_specs=P(("dom", "sub"), None), check_vma=False
    )
```
